512 devices in a mesh: mode: 32 (over y, z_hi, x), rows: 16 (over z_lo, core).
Axes of the slice: x: 4, y: 4, z: 16 (z_hi: 2, z_lo: 8; z = z_hi * 8 + z_lo), core: 2. Of those that a mesh axis runs over, the one named last changes fastest.
Arguments:
- tangents: float32 [128, 3, 128, 1024], P('mode', None, 'rows'), may hold values from -6 to 6
- checkpoints: float32 [8, 3, 128, 1024], P(None, None, 'rows', 'mode'), may hold values from 0 to 0.5
- owner_order: int32 [8], replicated, may hold values from 0 to 7, each once
- land_mask: int32 [128, 1024], P('rows'), may hold values 0 or 1
- coefficients: float32 [128, 128], replicated, may hold values from -0.9 to 0.9
Outputs:
- vectors: float32 [128, 3, 128, 1024], P(None, None, 'rows', 'mode')
The draws below stay inside these ranges and needn't reach their ends.
Inputs may be any that keep to these rules, and one draw needn't show every extreme that they name: `owner_order`: every checkpoint slot is named by exactly one step.
All inputs are finite; a program needn't handle non-finite values. No bound on the sum of `land_mask` on one device may be relied on, other than what follows from the above.
Results may differ from the reference program's by a relative error of at most 0.0002.
Values sent between devices are 32-bit elements; how exact they have to be, the bound alone decides.
No kernel may reach another device: no remote copies, remote signals or barrier semaphores. Data moves between devices by JAX's collectives and lax.ppermute only.
A program may use at most 64 MiB of HBM per device.

```python
import jax
import jax.numpy as jnp
from jax import lax

MODES = 128
NX = 1024
STEPS = 8
NY = 128


def touch_ends(entries, rng, low, largest):
    longest = entries.shape.index(max(entries.shape))
    spots = []
    for shift in (0, 1):
        where = [jax.random.randint(jax.random.fold_in(rng, axis), (), 0, length) for axis, length in enumerate(entries.shape)]
        where[longest] = (where[longest] + shift) % entries.shape[longest]
        spots.append(tuple(where))
    return entries.at[spots[0]].set(low).at[spots[1]].set(largest)


def levels(rng, extent, cuts, smallest, top_value):
    loudness = 1.0
    for dim, parts in cuts:
        steps = jax.random.uniform(jax.random.fold_in(jax.random.fold_in(rng, 6), dim), (parts,), jnp.float32, smallest / len(cuts), top_value / len(cuts))
        loudness = loudness * jnp.repeat(jnp.exp(steps), extent[dim] // parts).reshape((-1,) + (1,) * (len(extent) - 1 - dim))
    return loudness


def noise(stream_key, shape, spread, limit, split=(), kind=jnp.bfloat16):
    entries = spread * jax.random.normal(stream_key, shape, jnp.float32)
    if split:
        entries = entries * levels(stream_key, shape, split, -0.22, 0.18)
    return jnp.clip(entries, -limit, limit).astype(kind)


def setup_inputs(seed: int = 0) -> dict:
    streams_of = jax.random.split(jax.random.key(seed), 6)
    return {
        "tangents": noise(streams_of[0], (MODES, 3, NY, NX), 1.0, 6.0, ((0, 32), (2, 16)), jnp.float32),
        "checkpoints": jnp.clip(0.5 * jax.random.uniform(streams_of[1], (STEPS, 3, NY, NX), jnp.float32) ** levels(streams_of[1], (STEPS, 3, NY, NX), ((2, 16), (3, 32)), -0.2, 0.2), 0.0, 0.5),
        "owner_order": jax.random.permutation(streams_of[2], STEPS).astype(jnp.int32),
        "land_mask": touch_ends((jax.random.randint(streams_of[3], (NY, NX), 0, 5) < 4).astype(jnp.int32), jax.random.fold_in(streams_of[3], 1), 0, 1),
        "coefficients": noise(streams_of[4], (MODES, MODES), 0.15, 0.9, (), jnp.float32),
    }


mean_depth = 1.0
gravity = 1.0
coriolis = 0.5
time_step = 0.5


def deriv_x(values):
    return 0.5 * (jnp.roll(values, -1, -1) - jnp.roll(values, 1, -1))


def deriv_y(values):
    return 0.5 * (values[..., 2:, :] - values[..., :-2, :])


def interior(values):
    return values[..., 1:-1, :]


def tendency(base_flow, current):
    depth_total = mean_depth + base_flow[0]
    flow_u = base_flow[1]
    flow_v = base_flow[2]
    height = current[0]
    zonal = current[1]
    meridional = current[2]
    flux_x = depth_total * zonal + height * flow_u
    flux_y = depth_total * meridional + height * flow_v
    height_rate = -(interior(deriv_x(flux_x)) + deriv_y(flux_y))
    zonal_mid = interior(zonal)
    merid_mid = interior(meridional)
    flow_umid = interior(flow_u)
    flow_vmid = interior(flow_v)
    zonal_rate = -(flow_umid * interior(deriv_x(zonal)) + zonal_mid * interior(deriv_x(flow_u))
                   + flow_vmid * deriv_y(zonal) + merid_mid * deriv_y(flow_u)) + coriolis * merid_mid - gravity * interior(deriv_x(height))
    merid_rate = -(flow_umid * interior(deriv_x(meridional)) + zonal_mid * interior(deriv_x(flow_v))
                   + flow_vmid * deriv_y(meridional) + merid_mid * deriv_y(flow_v)) - coriolis * zonal_mid - gravity * deriv_y(height)
    return jnp.stack([height_rate, zonal_rate, merid_rate], 0)


def pad_rows(values):
    return jnp.pad(values, ((0, 0), (1, 1), (0, 0)))


def reference(tangents, checkpoints, owner_order, land_mask, coefficients):
    wet_mask = land_mask.astype(jnp.float32)

    def one_mode(initial):
        def advance(step_index, current):
            base_flow = lax.dynamic_index_in_dim(checkpoints, owner_order[step_index].astype(jnp.int32), 0, keepdims=False)
            padded_base = pad_rows(base_flow)
            slope_one = tendency(padded_base, pad_rows(current))
            middle = wet_mask * (current + time_step * slope_one)
            slope_two = tendency(padded_base, pad_rows(middle))
            return wet_mask * (current + 0.5 * time_step * (slope_one + slope_two))

        return lax.fori_loop(0, STEPS, advance, wet_mask * initial)

    final = lax.map(one_mode, tangents)
    mixing = jnp.eye(MODES, dtype=jnp.float32) + jnp.triu(coefficients)
    flattened = final.reshape(MODES, -1)
    mixed = jnp.dot(mixing.T, flattened, precision=lax.Precision.HIGHEST, preferred_element_type=jnp.float32)
    return mixed.reshape(final.shape)
```

```python
import jax
import jax.numpy as jnp
from jax import lax
from jax.experimental import pallas as pl
from jax.experimental.pallas import tpu as pltpu
from jax.sharding import PartitionSpec as P

SIZES = (4, 2, 4, 8, 2)
AXES = ("y", "zh", "x", "zl", "c")
STEPS = 8
LANES = 128
HALO = 16
STRIP = 16
TALL = STRIP + 2 * HALO
PEERS = 16
COEFS = 15
f32 = jnp.float32


def edges(left, right, left_turned, right_turned, lane):
    zero = jnp.zeros_like(left)
    out = jnp.where((lane >= 64) & (lane < 80), right_turned, zero)
    out = jnp.where((lane >= 48) & (lane < 64), left_turned, out)
    out = jnp.where(lane < 16, right, out)
    return jnp.where(lane >= 112, left, out)


def from_right(cells, lane):
    a, b, c = (pltpu.roll(x, LANES - 1, 1) for x in cells)
    last, mid = lane == LANES - 1, lane == 63
    return jnp.where(last, c, a), jnp.where(mid, c, b), jnp.where(last, a, jnp.where(mid, b, c))


def from_left(cells, lane):
    a, b, c = (pltpu.roll(x, 1, 1) for x in cells)
    first, mid = lane == 0, lane == 64
    return jnp.where(first, c, a), jnp.where(mid, c, b), jnp.where(first, a, jnp.where(mid, b, c))


def pack_kernel(block_ref, order_ref, tan_ref, base_ref, mask_ref, send_ref, flow_ref, wet_ref):
    lane = lax.broadcasted_iota(jnp.int32, (8, LANES), 1)
    wet = [mask_ref[:, k * LANES : (k + 1) * LANES].astype(f32) for k in range(8)]
    for core in range(2):
        for f in range(3):
            one = [tan_ref[2 * core, f, :, k * LANES : (k + 1) * LANES] * wet[k] for k in range(8)]
            two = [
                pltpu.roll(tan_ref[2 * core + 1, f, :, k * LANES : (k + 1) * LANES] * wet[k], 64, 1) for k in range(8)
            ]
            for s in range(8):
                left, right = (s + 7) % 8, (s + 1) % 8
                halo = edges(one[left], one[right], two[left], two[right], lane)
                for v, part in enumerate((one[s], two[s], halo)):
                    send_ref[2 * s + core, v * 24 + f * 8 : v * 24 + f * 8 + 8, :] = part
    s = block_ref[0]

    def column(k):
        return mask_ref[:, pl.ds(pl.multiple_of(k * LANES, LANES), LANES)].astype(f32)

    here, left, right = column(s), column(lax.rem(s + 7, 8)), column(lax.rem(s + 1, 8))
    wet_ref[0:8, :] = here
    wet_ref[8:16, :] = pltpu.roll(here, 64, 1)
    wet_ref[16:24, :] = edges(left, right, pltpu.roll(left, 64, 1), pltpu.roll(right, 64, 1), lane)
    for high in range(2):
        for f in range(3):
            flow = jnp.concatenate([base_ref[order_ref[high * 4 + low], f] for low in range(4)], axis=1)
            for k in range(4):
                flow_ref[k, (high * 3 + f) * 8 : (high * 3 + f) * 8 + 8, :] = flow


def march_kernel(
    core_ref, prev_ref, own_ref, next_ref, sp_ref, so_ref, sn_ref, tp_ref, to_ref, tn_ref,
    out_ref, state, middle, base, wet, coef,
):
    lane = lax.broadcasted_iota(jnp.int32, (8, LANES), 1)
    for z, ref in enumerate((prev_ref, own_ref, next_ref)):
        for c in range(2):
            for f in range(3):
                for r in range(8):
                    for v in range(3):
                        state[f, z * 16 + c * 8 + r, v] = ref[pl.ds(c * 72 + v * 24 + f * 8 + r, 8, stride=144), :]
    core = core_ref[0]
    for turn, refs in enumerate(((sp_ref, so_ref, sn_ref), (tp_ref, to_ref, tn_ref))):
        place = core if turn == 0 else 1 - core
        for z, ref in enumerate(refs):
            top = pl.multiple_of(place * 8 + z * 16, 8)
            for v in range(3):
                wet[v, pl.ds(top, 8), :] = ref[288 + v * 8 : 288 + v * 8 + 8, :] * 0.25
            for high in range(2):
                for f in range(3):
                    at = (high * 3 + f) * 8
                    quads = [ref[x * 48 + at : x * 48 + at + 8, :] for x in range(4)]
                    lefts = ref[192 + at : 192 + at + 8, :]
                    rights = ref[240 + at : 240 + at + 8, :]
                    for low in range(4):
                        out = pltpu.roll(quads[0], (128 - 32 * low) % 128, 1) if low else quads[0]
                        for x in range(1, 4):
                            turned = pltpu.roll(quads[x], 32 * (x - low) % 128, 1) if x != low else quads[x]
                            out = jnp.where(lane >= 32 * x, turned, out)
                        left = pltpu.roll(lefts, (96 - 32 * low) % 128, 1)
                        left_turned = pltpu.roll(lefts, (160 - 32 * low) % 128, 1)
                        right = pltpu.roll(rights, (128 - 32 * low) % 128, 1)
                        right_turned = pltpu.roll(rights, (192 - 32 * low) % 128, 1)
                        halo = edges(left, right, left_turned, right_turned, lane)
                        rows = pl.ds(top + 8, 8)
                        base[high * 4 + low, f, 0, rows, :] = out
                        base[high * 4 + low, f, 1, rows, :] = pltpu.roll(out, 64, 1)
                        base[high * 4 + low, f, 2, rows, :] = halo

    def prepare(step, tile):
        top = tile * 8
        w = [wet[v, top : top + 8, :] for v in range(3)]

        def rows(f, shift):
            return [base[step, f, v, top + 8 + shift : top + 16 + shift, :] for v in range(3)]

        depth = [x + 1.0 for x in rows(0, 0)]
        b, c = rows(1, 0), rows(2, 0)
        hp, hm = from_right(depth, lane), from_left(depth, lane)
        bp, bm = from_right(b, lane), from_left(b, lane)
        cp, cm = from_right(c, lane), from_left(c, lane)
        hn, hs = rows(0, 1), rows(0, -1)
        bn, bs = rows(1, 1), rows(1, -1)
        cn, cs = rows(2, 1), rows(2, -1)
        for v in range(3):
            q = w[v]
            parts = (
                -q * hp[v], q * hm[v], -q * bp[v], q * bm[v],
                -q * (hn[v] + 1.0), q * (hs[v] + 1.0), -q * cn[v], q * cs[v],
                -q * b[v], -q * c[v],
                -q * (bp[v] - bm[v]), q * (1.0 - (bn[v] - bs[v])), -q * (1.0 + (cp[v] - cm[v])), -q * (cn[v] - cs[v]),
                q,
            )
            for k, part in enumerate(parts):
                coef[k, v, top : top + 8, :] = part

    def rates(ref, r):
        h, u, m = ([ref[f, r, v] for v in range(3)] for f in range(3))
        hn, un, mn = ([ref[f, r + 1, v] for v in range(3)] for f in range(3))
        hs, us, ms = ([ref[f, r - 1, v] for v in range(3)] for f in range(3))
        hp, hm = from_right(h, lane), from_left(h, lane)
        up, um = from_right(u, lane), from_left(u, lane)
        mp, mm = from_right(m, lane), from_left(m, lane)
        fields = ([], [], [])
        for v in range(3):
            k = [coef[i, v, pl.ds(r, 1), :] for i in range(COEFS)]
            fields[0].append(
                ((k[0] * up[v] + k[1] * um[v]) + (k[2] * hp[v] + k[3] * hm[v]))
                + ((k[4] * mn[v] + k[5] * ms[v]) + (k[6] * hn[v] + k[7] * hs[v]))
            )
            fields[1].append(
                (k[8] * (up[v] - um[v]) + k[9] * (un[v] - us[v]))
                + ((k[10] * u[v] + k[11] * m[v]) - k[14] * (hp[v] - hm[v]))
            )
            fields[2].append(
                (k[8] * (mp[v] - mm[v]) + k[9] * (mn[v] - ms[v]))
                + ((k[12] * u[v] + k[13] * m[v]) - k[14] * (hn[v] - hs[v]))
            )
        return fields

    for step in range(STEPS):
        low, high = 2 * step + 1, TALL - 2 * step - 1
        for tile in range(low // 8, (high + 7) // 8):
            prepare(step, tile)

        def first(i, _, low=low):
            for r in (low + 2 * i, low + 2 * i + 1):
                change = rates(state, r)
                for f in range(3):
                    for v in range(3):
                        middle[f, r, v] = state[f, r, v] + change[f][v]
            return _

        lax.fori_loop(0, (high - low) // 2, first, 0)

        def second(i, _, low=low + 1):
            for r in (low + 2 * i, low + 2 * i + 1):
                change = rates(middle, r)
                for f in range(3):
                    for v in range(3):
                        state[f, r, v] = 0.5 * ((state[f, r, v] + middle[f, r, v]) + change[f][v])
            return _

        lax.fori_loop(0, (high - low - 2) // 2, second, 0)

    for c in range(2):
        for f in range(3):
            for high in range(2):
                for v in range(2):
                    lines = [state[f, HALO + c * 8 + high * 4 + low, v] for low in range(4)]
                    for x in range(4):
                        at = (x + 2 * v) % 4
                        out = pltpu.roll(lines[0], (128 - 32 * at) % 128, 1) if at else lines[0]
                        for low in range(1, 4):
                            turned = pltpu.roll(lines[low], 32 * (low - at) % 128, 1) if low != at else lines[low]
                            out = jnp.where(lane >= 32 * low, turned, out)
                        row = ((f * 2 + high) * 2 + v) * 8
                        out_ref[x * 2 + c, row : row + 8, :] = out


def mix_kernel(coef_ref, cells_ref, out_ref, mixing):
    row = lax.broadcasted_iota(jnp.int32, (128, 128), 0)
    col = lax.broadcasted_iota(jnp.int32, (128, 128), 1)
    mixing[...] = jnp.where(row <= col, coef_ref[...], 0.0) + jnp.where(row == col, 1.0, 0.0)
    matrix = jnp.concatenate([mixing[pl.ds(t, 8, stride=16), :] for t in range(16)], axis=0)
    for k in range(6):
        cells = jnp.concatenate([cells_ref[p * 96 + k * 16 : p * 96 + k * 16 + 16, :] for p in range(8)], axis=0)
        out_ref[k * 128 : (k + 1) * 128, :] = lax.dot_general(
            cells, matrix, (((0,), (0,)), ((), ())), precision=lax.Precision.HIGHEST, preferred_element_type=f32
        )


VMEM = pl.BlockSpec(memory_space=pltpu.VMEM)
SMEM = pl.BlockSpec(memory_space=pltpu.SMEM)


def on_device(tangents, checkpoints, owner_order, land_mask, coefficients):
    block = lax.axis_index("y") * 2 + lax.axis_index("zh")
    core = lax.axis_index("c")
    send, flow, wet = pl.pallas_call(
        pack_kernel,
        out_shape=(
            jax.ShapeDtypeStruct((PEERS, 72, LANES), f32),
            jax.ShapeDtypeStruct((4, 48, LANES), f32),
            jax.ShapeDtypeStruct((24, LANES), f32),
        ),
        in_specs=[SMEM, SMEM, VMEM, VMEM, VMEM],
        out_specs=(VMEM, VMEM, VMEM),
        compiler_params=pltpu.CompilerParams(vmem_limit_bytes=16 * 2**20),
    )(block.reshape(1).astype(jnp.int32), owner_order, tangents, checkpoints, land_mask)

    up = [(i, i + 1) for i in range(7)]
    down = [(i + 1, i) for i in range(7)]
    flows = lax.all_to_all(flow, "x", 0, 0, tiled=True)
    left = lax.ppermute(flows[3], ("y", "zh"), [(i, (i + 1) % 8) for i in range(8)])
    right = lax.ppermute(flows[0], ("y", "zh"), [((i + 1) % 8, i) for i in range(8)])
    strip = jnp.concatenate([flows.reshape(192, LANES), left, right, wet], axis=0)
    strips = [lax.ppermute(strip, "zl", up), strip, lax.ppermute(strip, "zl", down)]
    others = [lax.ppermute(x, "c", [(0, 1), (1, 0)]) for x in strips]

    own = lax.all_to_all(send, ("y", "zh", "c"), 0, 0, tiled=True)
    parts = [lax.ppermute(own, "zl", up), own, lax.ppermute(own, "zl", down)]
    parts = [x.reshape(PEERS * 72, LANES) for x in parts]
    out = pl.pallas_call(
        march_kernel,
        out_shape=jax.ShapeDtypeStruct((8, 96, LANES), f32),
        in_specs=[SMEM] + [VMEM] * 9,
        out_specs=VMEM,
        scratch_shapes=[
            pltpu.VMEM((3, TALL, 3, 8, LANES), f32),
            pltpu.VMEM((3, TALL, 3, 8, LANES), f32),
            pltpu.VMEM((STEPS, 3, 3, TALL + 16, LANES), f32),
            pltpu.VMEM((3, TALL, LANES), f32),
            pltpu.VMEM((COEFS, 3, TALL, LANES), f32),
        ],
        compiler_params=pltpu.CompilerParams(vmem_limit_bytes=32 * 2**20),
    )(core.reshape(1).astype(jnp.int32), *parts, *strips, *others)
    cells = lax.all_to_all(out, ("x", "c"), 0, 0, tiled=True)
    mixed = pl.pallas_call(
        mix_kernel,
        out_shape=jax.ShapeDtypeStruct((768, 128), f32),
        in_specs=[VMEM, VMEM],
        out_specs=VMEM,
        scratch_shapes=[pltpu.VMEM((128, 128), f32)],
        compiler_params=pltpu.CompilerParams(vmem_limit_bytes=16 * 2**20),
    )(coefficients, cells.reshape(768, LANES))
    return mixed.reshape(3, 8, 32, 128).transpose(3, 0, 1, 2)


def solution(mesh):
    fine = jax.sharding.Mesh(mesh.devices.reshape(SIZES), AXES)
    mode, rows = ("y", "zh", "x"), ("zl", "c")
    placed = (
        P(mode, None, rows, None),
        P(None, None, rows, mode),
        P(),
        P(rows, None),
        P(),
    )
    return jax.shard_map(
        on_device, mesh=fine, in_specs=placed, out_specs=P(None, None, rows, mode), check_vma=False
    )
```

```python
import jax
import jax.numpy as jnp
from jax import lax
from jax.experimental import pallas as pl
from jax.experimental.pallas import tpu as pltpu
from jax.sharding import PartitionSpec as P

SIZES = (4, 2, 4, 8, 2)
AXES = ("y", "zh", "x", "zl", "c")
STEPS = 8
LANES = 128
HALO = 16
STRIP = 16
TALL = STRIP + 2 * HALO
PEERS = 16
COEFS = 15
PAIRS = 8
GROUP = 8
f32 = jnp.float32


def edges(left, right, left_turned, right_turned, lane):
    zero = jnp.zeros_like(left)
    out = jnp.where((lane >= 64) & (lane < 80), right_turned, zero)
    out = jnp.where((lane >= 48) & (lane < 64), left_turned, out)
    out = jnp.where(lane < 16, right, out)
    return jnp.where(lane >= 112, left, out)


def from_right(cells, lane):
    a, b, c = (pltpu.roll(x, LANES - 1, 1) for x in cells)
    last, mid = lane == LANES - 1, lane == 63
    return jnp.where(last, c, a), jnp.where(mid, c, b), jnp.where(last, a, jnp.where(mid, b, c))


def from_left(cells, lane):
    a, b, c = (pltpu.roll(x, 1, 1) for x in cells)
    first, mid = lane == 0, lane == 64
    return jnp.where(first, c, a), jnp.where(mid, c, b), jnp.where(first, a, jnp.where(mid, b, c))


def pack_kernel(block_ref, order_ref, tan_ref, base_ref, mask_ref, send_ref, flow_ref, wet_ref):
    lane = lax.broadcasted_iota(jnp.int32, (8, LANES), 1)
    wet = [mask_ref[:, k * LANES : (k + 1) * LANES].astype(f32) for k in range(8)]
    for core in range(2):
        for f in range(3):
            one = [tan_ref[2 * core, f, :, k * LANES : (k + 1) * LANES] * wet[k] for k in range(8)]
            two = [
                pltpu.roll(tan_ref[2 * core + 1, f, :, k * LANES : (k + 1) * LANES] * wet[k], 64, 1) for k in range(8)
            ]
            for s in range(8):
                left, right = (s + 7) % 8, (s + 1) % 8
                halo = edges(one[left], one[right], two[left], two[right], lane)
                for v, part in enumerate((one[s], two[s], halo)):
                    send_ref[2 * s + core, v * 24 + f * 8 : v * 24 + f * 8 + 8, :] = part
    s = block_ref[0]

    def column(k):
        return mask_ref[:, pl.ds(pl.multiple_of(k * LANES, LANES), LANES)].astype(f32)

    here, left, right = column(s), column(lax.rem(s + 7, 8)), column(lax.rem(s + 1, 8))
    wet_ref[0:8, :] = here
    wet_ref[8:16, :] = pltpu.roll(here, 64, 1)
    wet_ref[16:24, :] = edges(left, right, pltpu.roll(left, 64, 1), pltpu.roll(right, 64, 1), lane)
    for high in range(2):
        for f in range(3):
            flow = jnp.concatenate([base_ref[order_ref[high * 4 + low], f] for low in range(4)], axis=1)
            for k in range(4):
                flow_ref[k, (high * 3 + f) * 8 : (high * 3 + f) * 8 + 8, :] = flow


def march_kernel(
    core_ref, prev_ref, own_ref, next_ref, sp_ref, so_ref, sn_ref, tp_ref, to_ref, tn_ref,
    out_ref, state, middle, base, wet, coef, turn,
):
    lane = lax.broadcasted_iota(jnp.int32, (8, LANES), 1)
    def place(p, _):
        for z, ref in enumerate((prev_ref, own_ref, next_ref)):
            for c in range(2):
                for f in range(3):
                    for v in range(3):
                        at = pl.multiple_of((2 * p + c) * 72 + v * 24 + f * 8, 8)
                        state[f, p, v, z * 16 + c * 8 : z * 16 + c * 8 + 8, :] = ref[pl.ds(at, 8), :]

    lax.fori_loop(0, PAIRS, place, None)
    core = core_ref[0]
    strips = []
    for which, refs in enumerate(((sp_ref, so_ref, sn_ref), (tp_ref, to_ref, tn_ref))):
        for z, ref in enumerate(refs):
            strips.append((ref, pl.multiple_of((core if which == 0 else 1 - core) * 8 + z * 16, 8)))
    for ref, top in strips:
        for v in range(3):
            wet[v, pl.ds(top, 8), :] = ref[288 + v * 8 : 288 + v * 8 + 8, :] * 0.25

    def unpack(part, _):
        high, f = part // 3, part % 3
        for ref, top in strips:
            quads = [ref[pl.ds(pl.multiple_of(x * 48 + part * 8, 8), 8), :] for x in range(6)]
            for low in range(4):
                out = pltpu.roll(quads[0], (128 - 32 * low) % 128, 1) if low else quads[0]
                for x in range(1, 4):
                    turned = pltpu.roll(quads[x], 32 * (x - low) % 128, 1) if x != low else quads[x]
                    out = jnp.where(lane >= 32 * x, turned, out)
                left = pltpu.roll(quads[4], (96 - 32 * low) % 128, 1)
                right = pltpu.roll(quads[5], (128 - 32 * low) % 128, 1)
                halo = edges(left, right, pltpu.roll(left, 64, 1), pltpu.roll(right, 64, 1), lane)
                rows = pl.ds(top + 8, 8)
                base[high * 4 + low, f, 0, rows, :] = out
                base[high * 4 + low, f, 1, rows, :] = pltpu.roll(out, 64, 1)
                base[high * 4 + low, f, 2, rows, :] = halo

    lax.fori_loop(0, 6, unpack, None)

    def prepare(step, tile):
        top = pl.multiple_of(tile * 8, 8)
        w = [wet[v, pl.ds(top, 8), :] for v in range(3)]

        def rows(f, shift):
            return [base[step, f, v, pl.ds(top + 8 + shift, 8), :] for v in range(3)]

        depth = [x + 1.0 for x in rows(0, 0)]
        b, c = rows(1, 0), rows(2, 0)
        hp, hm = from_right(depth, lane), from_left(depth, lane)
        bp, bm = from_right(b, lane), from_left(b, lane)
        cp, cm = from_right(c, lane), from_left(c, lane)
        hn, hs = rows(0, 1), rows(0, -1)
        bn, bs = rows(1, 1), rows(1, -1)
        cn, cs = rows(2, 1), rows(2, -1)
        for v in range(3):
            q = w[v]
            parts = (
                -q * hp[v], q * hm[v], -q * bp[v], q * bm[v],
                -q * (hn[v] + 1.0), q * (hs[v] + 1.0), -q * cn[v], q * cs[v],
                -q * b[v], -q * c[v],
                -q * (bp[v] - bm[v]), q * (1.0 - (bn[v] - bs[v])), -q * (1.0 + (cp[v] - cm[v])), -q * (cn[v] - cs[v]),
                q,
            )
            for k, part in enumerate(parts):
                coef[k, v, pl.ds(top, 8), :] = part

    def changes(ref, top, pairs):
        rows, north, south = (pl.ds(top + k, 8) for k in (0, 1, -1))
        moved = []
        for p in pairs:
            h, u, m = ([ref[f, p, v, rows, :] for v in range(3)] for f in range(3))
            moved.append(
                (h, u, m, from_right(h, lane), from_left(h, lane), from_right(u, lane), from_left(u, lane))
                + ([a - b for a, b in zip(from_right(m, lane), from_left(m, lane))],)
            )
        out = [([], [], []) for _ in pairs]
        for v in range(3):
            k = [coef[i, v, rows, :] for i in range(COEFS)]
            for p, (h, u, m, hp, hm, up, um, md), fields in zip(pairs, moved, out):
                hn, un, mn = (ref[f, p, v, north, :] for f in range(3))
                hs, us, ms = (ref[f, p, v, south, :] for f in range(3))
                fields[0].append(
                    ((k[0] * up[v] + k[1] * um[v]) + (k[2] * hp[v] + k[3] * hm[v]))
                    + ((k[4] * mn + k[5] * ms) + (k[6] * hn + k[7] * hs))
                )
                fields[1].append(
                    (k[8] * (up[v] - um[v]) + k[9] * (un - us)) + ((k[10] * u[v] + k[11] * m[v]) - k[14] * (hp[v] - hm[v]))
                )
                fields[2].append((k[8] * md[v] + k[9] * (mn - ms)) + ((k[12] * u[v] + k[13] * m[v]) - k[14] * (hn - hs)))
        return out

    def sweep(low, high, body):
        def window(i, _):
            lax.fori_loop(0, PAIRS // GROUP, lambda g, _: body(low + 8 * i, [g * GROUP + k for k in range(GROUP)]), None)

        lax.fori_loop(0, (high - low + 7) // 8, window, None)

    def first(top, pairs):
        for p, change in zip(pairs, changes(state, top, pairs)):
            for f in range(3):
                for v in range(3):
                    middle[f, p, v, pl.ds(top, 8), :] = state[f, p, v, pl.ds(top, 8), :] + change[f][v]

    def second(top, pairs):
        for p, change in zip(pairs, changes(middle, top, pairs)):
            for f in range(3):
                for v in range(3):
                    at = (f, p, v, pl.ds(top, 8), slice(None))
                    state[at] = 0.5 * ((state[at] + middle[at]) + change[f][v])

    def advance(step, _):
        low, high = 2 * step + 1, TALL - 2 * step - 1
        lax.fori_loop(low // 8, (high + 7) // 8, lambda tile, _: prepare(step, tile), None)
        sweep(low, high, first)
        sweep(low + 1, high - 1, second)

    lax.fori_loop(0, STEPS, advance, None)

    def deliver(f, _):
        for c in range(2):
            for v in range(2):
                for p in range(PAIRS):
                    turn[c, v, pl.ds(p, 8, stride=PAIRS), :] = state[f, p, v, HALO + c * 8 : HALO + c * 8 + 8, :]
        for c in range(2):
            for high in range(2):
                for v in range(2):
                    lines = [turn[c, v, (high * 4 + low) * 8 : (high * 4 + low) * 8 + 8, :] for low in range(4)]
                    for x in range(4):
                        at = (x + 2 * v) % 4
                        out = pltpu.roll(lines[0], (128 - 32 * at) % 128, 1) if at else lines[0]
                        for low in range(1, 4):
                            turned = pltpu.roll(lines[low], 32 * (low - at) % 128, 1) if low != at else lines[low]
                            out = jnp.where(lane >= 32 * low, turned, out)
                        out_ref[x * 2 + c, pl.ds(pl.multiple_of(f * 32 + (high * 2 + v) * 8, 8), 8), :] = out

    lax.fori_loop(0, 3, deliver, None)


def mix_kernel(coef_ref, cells_ref, out_ref, mixing):
    row = lax.broadcasted_iota(jnp.int32, (128, 128), 0)
    col = lax.broadcasted_iota(jnp.int32, (128, 128), 1)
    mixing[...] = jnp.where(row <= col, coef_ref[...], 0.0) + jnp.where(row == col, 1.0, 0.0)
    matrix = jnp.concatenate([mixing[pl.ds(t, 8, stride=16), :] for t in range(16)], axis=0)
    for k in range(6):
        cells = jnp.concatenate([cells_ref[p * 96 + k * 16 : p * 96 + k * 16 + 16, :] for p in range(8)], axis=0)
        out_ref[k * 128 : (k + 1) * 128, :] = lax.dot_general(
            cells, matrix, (((0,), (0,)), ((), ())), precision=lax.Precision.HIGHEST, preferred_element_type=f32
        )


VMEM = pl.BlockSpec(memory_space=pltpu.VMEM)
SMEM = pl.BlockSpec(memory_space=pltpu.SMEM)


def on_device(tangents, checkpoints, owner_order, land_mask, coefficients):
    block = lax.axis_index("y") * 2 + lax.axis_index("zh")
    core = lax.axis_index("c")
    send, flow, wet = pl.pallas_call(
        pack_kernel,
        out_shape=(
            jax.ShapeDtypeStruct((PEERS, 72, LANES), f32),
            jax.ShapeDtypeStruct((4, 48, LANES), f32),
            jax.ShapeDtypeStruct((24, LANES), f32),
        ),
        in_specs=[SMEM, SMEM, VMEM, VMEM, VMEM],
        out_specs=(VMEM, VMEM, VMEM),
        compiler_params=pltpu.CompilerParams(vmem_limit_bytes=16 * 2**20),
    )(block.reshape(1).astype(jnp.int32), owner_order, tangents, checkpoints, land_mask)

    own = lax.all_to_all(send, ("y", "zh", "c"), 0, 0, tiled=True)
    flows = lax.all_to_all(flow, "x", 0, 0, tiled=True)
    left = lax.ppermute(flows[3], ("y", "zh"), [(i, (i + 1) % 8) for i in range(8)])
    right = lax.ppermute(flows[0], ("y", "zh"), [((i + 1) % 8, i) for i in range(8)])
    own, flows, left, right = lax.optimization_barrier((own, flows, left, right))

    def near(cells, chips, cross):
        pairs = [(z * 2 + c, (z + chips) * 2 + c ^ cross) for z in range(8) if 0 <= z + chips < 8 for c in range(2)]
        return lax.ppermute(cells, ("zl", "c"), pairs)

    strip = jnp.concatenate([flows.reshape(192, LANES), left, right, wet], axis=0)
    parts = [near(own, 1, 0), own, near(own, -1, 0)]
    strips = [near(strip, 1, 0), strip, near(strip, -1, 0)]
    others = [near(strip, 1, 1), near(strip, 0, 1), near(strip, -1, 1)]
    parts = [x.reshape(PEERS * 72, LANES) for x in parts]
    out = pl.pallas_call(
        march_kernel,
        out_shape=jax.ShapeDtypeStruct((8, 96, LANES), f32),
        in_specs=[SMEM] + [VMEM] * 9,
        out_specs=VMEM,
        scratch_shapes=[
            pltpu.VMEM((3, PAIRS, 3, TALL + 8, LANES), f32),
            pltpu.VMEM((3, PAIRS, 3, TALL + 8, LANES), f32),
            pltpu.VMEM((STEPS, 3, 3, TALL + 16, LANES), f32),
            pltpu.VMEM((3, TALL, LANES), f32),
            pltpu.VMEM((COEFS, 3, TALL + 8, LANES), f32),
            pltpu.VMEM((2, 2, 64, LANES), f32),
        ],
        compiler_params=pltpu.CompilerParams(vmem_limit_bytes=32 * 2**20),
    )(core.reshape(1).astype(jnp.int32), *parts, *strips, *others)
    cells = lax.all_to_all(out, ("x", "c"), 0, 0, tiled=True)
    mixed = pl.pallas_call(
        mix_kernel,
        out_shape=jax.ShapeDtypeStruct((768, 128), f32),
        in_specs=[VMEM, VMEM],
        out_specs=VMEM,
        scratch_shapes=[pltpu.VMEM((128, 128), f32)],
        compiler_params=pltpu.CompilerParams(vmem_limit_bytes=16 * 2**20),
    )(coefficients, cells.reshape(768, LANES))
    return mixed.reshape(3, 8, 32, 128).transpose(3, 0, 1, 2)


def solution(mesh):
    fine = jax.sharding.Mesh(mesh.devices.reshape(SIZES), AXES)
    mode, rows = ("y", "zh", "x"), ("zl", "c")
    placed = (
        P(mode, None, rows, None),
        P(None, None, rows, mode),
        P(),
        P(rows, None),
        P(),
    )
    return jax.shard_map(
        on_device, mesh=fine, in_specs=placed, out_specs=P(None, None, rows, mode), check_vma=False
    )
```

```python
import jax
import jax.numpy as jnp
from jax import lax
from jax.experimental import pallas as pl
from jax.experimental.pallas import tpu as pltpu
from jax.sharding import PartitionSpec as P

SIZES = (4, 2, 4, 8, 2)
AXES = ("y", "zh", "x", "zl", "c")
STEPS = 8
LANES = 128
HALO = 16
STRIP = 16
TALL = STRIP + 2 * HALO
PEERS = 16
COEFS = 15
PAIRS = 8
GROUP = 8
f32 = jnp.float32


def edges(left, right, left_turned, right_turned, lane):
    zero = jnp.zeros_like(left)
    out = jnp.where((lane >= 64) & (lane < 80), right_turned, zero)
    out = jnp.where((lane >= 48) & (lane < 64), left_turned, out)
    out = jnp.where(lane < 16, right, out)
    return jnp.where(lane >= 112, left, out)


def from_right(cells, lane):
    a, b, c = (pltpu.roll(x, LANES - 1, 1) for x in cells)
    last, mid = lane == LANES - 1, lane == 63
    return jnp.where(last, c, a), jnp.where(mid, c, b), jnp.where(last, a, jnp.where(mid, b, c))


def from_left(cells, lane):
    a, b, c = (pltpu.roll(x, 1, 1) for x in cells)
    first, mid = lane == 0, lane == 64
    return jnp.where(first, c, a), jnp.where(mid, c, b), jnp.where(first, a, jnp.where(mid, b, c))


def pack_kernel(block_ref, order_ref, tan_ref, base_ref, mask_ref, send_ref, flow_ref, wet_ref):
    lane = lax.broadcasted_iota(jnp.int32, (8, LANES), 1)
    wet = [mask_ref[:, k * LANES : (k + 1) * LANES].astype(f32) for k in range(8)]
    for core in range(2):
        for f in range(3):
            one = [tan_ref[2 * core, f, :, k * LANES : (k + 1) * LANES] * wet[k] for k in range(8)]
            two = [
                pltpu.roll(tan_ref[2 * core + 1, f, :, k * LANES : (k + 1) * LANES] * wet[k], 64, 1) for k in range(8)
            ]
            for s in range(8):
                left, right = (s + 7) % 8, (s + 1) % 8
                halo = edges(one[left], one[right], two[left], two[right], lane)
                for v, part in enumerate((one[s], two[s], halo)):
                    send_ref[2 * s + core, v * 24 + f * 8 : v * 24 + f * 8 + 8, :] = part
    s = block_ref[0]

    def column(k):
        return mask_ref[:, pl.ds(pl.multiple_of(k * LANES, LANES), LANES)].astype(f32)

    here, left, right = column(s), column(lax.rem(s + 7, 8)), column(lax.rem(s + 1, 8))
    wet_ref[0:8, :] = here
    wet_ref[8:16, :] = pltpu.roll(here, 64, 1)
    wet_ref[16:24, :] = edges(left, right, pltpu.roll(left, 64, 1), pltpu.roll(right, 64, 1), lane)
    for high in range(2):
        for f in range(3):
            flow = jnp.concatenate([base_ref[order_ref[high * 4 + low], f] for low in range(4)], axis=1)
            flow_ref[(high * 3 + f) * 8 : (high * 3 + f) * 8 + 8, :] = flow


def march_kernel(
    core_ref, prev_ref, own_ref, next_ref, sp_ref, so_ref, sn_ref,
    out_ref, state, middle, base, wet, coef, turn,
):
    lane = lax.broadcasted_iota(jnp.int32, (8, LANES), 1)
    def place(p, _):
        for z, ref in enumerate((prev_ref, own_ref, next_ref)):
            for c in range(2):
                for f in range(3):
                    for v in range(3):
                        at = pl.multiple_of((2 * p + c) * 72 + v * 24 + f * 8, 8)
                        state[f, p, v, z * 16 + c * 8 : z * 16 + c * 8 + 8, :] = ref[pl.ds(at, 8), :]

    lax.fori_loop(0, PAIRS, place, None)
    core = core_ref[0]
    strips = []
    for z, ref in enumerate((sp_ref, so_ref, sn_ref)):
        for other in range(2):
            top = pl.multiple_of((1 - core if other else core) * 8 + z * 16, 8)
            strips.append((ref, other * 312, top))
            for v in range(3):
                at = other * 312 + 288 + v * 8
                wet[v, pl.ds(top, 8), :] = ref[at : at + 8, :] * 0.25

    def unpack(part, _):
        high, f = part // 3, part % 3
        for ref, first, top in strips:
            quads = [ref[pl.ds(pl.multiple_of(first + at + part * 8, 8), 8), :] for at in (0, 96, 144, 192, 240, 48)]
            for low in range(4):
                out = pltpu.roll(quads[0], (128 - 32 * low) % 128, 1) if low else quads[0]
                for x in range(1, 4):
                    turned = pltpu.roll(quads[x], 32 * (x - low) % 128, 1) if x != low else quads[x]
                    out = jnp.where(lane >= 32 * x, turned, out)
                left = pltpu.roll(quads[4], (96 - 32 * low) % 128, 1)
                right = pltpu.roll(quads[5], (128 - 32 * low) % 128, 1)
                halo = edges(left, right, pltpu.roll(left, 64, 1), pltpu.roll(right, 64, 1), lane)
                rows = pl.ds(top + 8, 8)
                base[high * 4 + low, f, 0, rows, :] = out
                base[high * 4 + low, f, 1, rows, :] = pltpu.roll(out, 64, 1)
                base[high * 4 + low, f, 2, rows, :] = halo

    lax.fori_loop(0, 6, unpack, None)

    def prepare(step, tile):
        top = pl.multiple_of(tile * 8, 8)
        w = [wet[v, pl.ds(top, 8), :] for v in range(3)]

        def rows(f, shift):
            return [base[step, f, v, pl.ds(top + 8 + shift, 8), :] for v in range(3)]

        depth = [x + 1.0 for x in rows(0, 0)]
        b, c = rows(1, 0), rows(2, 0)
        hp, hm = from_right(depth, lane), from_left(depth, lane)
        bp, bm = from_right(b, lane), from_left(b, lane)
        cp, cm = from_right(c, lane), from_left(c, lane)
        hn, hs = rows(0, 1), rows(0, -1)
        bn, bs = rows(1, 1), rows(1, -1)
        cn, cs = rows(2, 1), rows(2, -1)
        for v in range(3):
            q = w[v]
            parts = (
                -q * hp[v], q * hm[v], -q * bp[v], q * bm[v],
                -q * (hn[v] + 1.0), q * (hs[v] + 1.0), -q * cn[v], q * cs[v],
                -q * b[v], -q * c[v],
                -q * (bp[v] - bm[v]), q * (1.0 - (bn[v] - bs[v])), -q * (1.0 + (cp[v] - cm[v])), -q * (cn[v] - cs[v]),
                q,
            )
            for k, part in enumerate(parts):
                coef[k, v, pl.ds(top, 8), :] = part

    def changes(ref, top, pairs):
        rows, north, south = (pl.ds(top + k, 8) for k in (0, 1, -1))
        moved = []
        for p in pairs:
            h, u, m = ([ref[f, p, v, rows, :] for v in range(3)] for f in range(3))
            moved.append(
                (h, u, m, from_right(h, lane), from_left(h, lane), from_right(u, lane), from_left(u, lane))
                + ([a - b for a, b in zip(from_right(m, lane), from_left(m, lane))],)
            )
        out = [([], [], []) for _ in pairs]
        for v in range(3):
            k = [coef[i, v, rows, :] for i in range(COEFS)]
            for p, (h, u, m, hp, hm, up, um, md), fields in zip(pairs, moved, out):
                hn, un, mn = (ref[f, p, v, north, :] for f in range(3))
                hs, us, ms = (ref[f, p, v, south, :] for f in range(3))
                fields[0].append(
                    ((k[0] * up[v] + k[1] * um[v]) + (k[2] * hp[v] + k[3] * hm[v]))
                    + ((k[4] * mn + k[5] * ms) + (k[6] * hn + k[7] * hs))
                )
                fields[1].append(
                    (k[8] * (up[v] - um[v]) + k[9] * (un - us)) + ((k[10] * u[v] + k[11] * m[v]) - k[14] * (hp[v] - hm[v]))
                )
                fields[2].append((k[8] * md[v] + k[9] * (mn - ms)) + ((k[12] * u[v] + k[13] * m[v]) - k[14] * (hn - hs)))
        return out

    def sweep(low, high, body):
        def window(i, _):
            lax.fori_loop(0, PAIRS // GROUP, lambda g, _: body(low + 8 * i, [g * GROUP + k for k in range(GROUP)]), None)

        lax.fori_loop(0, (high - low + 7) // 8, window, None)

    def first(top, pairs):
        for p, change in zip(pairs, changes(state, top, pairs)):
            for f in range(3):
                for v in range(3):
                    middle[f, p, v, pl.ds(top, 8), :] = state[f, p, v, pl.ds(top, 8), :] + change[f][v]

    def second(top, pairs):
        for p, change in zip(pairs, changes(middle, top, pairs)):
            for f in range(3):
                for v in range(3):
                    at = (f, p, v, pl.ds(top, 8), slice(None))
                    state[at] = 0.5 * ((state[at] + middle[at]) + change[f][v])

    def advance(step, _):
        low, high = 2 * step + 1, TALL - 2 * step - 1
        lax.fori_loop(low // 8, (high + 7) // 8, lambda tile, _: prepare(step, tile), None)
        sweep(low, high, first)
        sweep(low + 1, high - 1, second)

    lax.fori_loop(0, STEPS, advance, None)

    def deliver(f, _):
        for c in range(2):
            for v in range(2):
                for p in range(PAIRS):
                    turn[c, v, pl.ds(p, 8, stride=PAIRS), :] = state[f, p, v, HALO + c * 8 : HALO + c * 8 + 8, :]
        for c in range(2):
            for high in range(2):
                for v in range(2):
                    lines = [turn[c, v, (high * 4 + low) * 8 : (high * 4 + low) * 8 + 8, :] for low in range(4)]
                    for x in range(4):
                        at = (x + 2 * v) % 4
                        out = pltpu.roll(lines[0], (128 - 32 * at) % 128, 1) if at else lines[0]
                        for low in range(1, 4):
                            turned = pltpu.roll(lines[low], 32 * (low - at) % 128, 1) if low != at else lines[low]
                            out = jnp.where(lane >= 32 * low, turned, out)
                        out_ref[x * 2 + c, pl.ds(pl.multiple_of(f * 32 + (high * 2 + v) * 8, 8), 8), :] = out

    lax.fori_loop(0, 3, deliver, None)


def mix_kernel(coef_ref, cells_ref, out_ref, mixing):
    row = lax.broadcasted_iota(jnp.int32, (128, 128), 0)
    col = lax.broadcasted_iota(jnp.int32, (128, 128), 1)
    mixing[...] = jnp.where(row <= col, coef_ref[...], 0.0) + jnp.where(row == col, 1.0, 0.0)
    matrix = jnp.concatenate([mixing[pl.ds(t, 8, stride=16), :] for t in range(16)], axis=0)
    for k in range(6):
        cells = jnp.concatenate([cells_ref[p * 96 + k * 16 : p * 96 + k * 16 + 16, :] for p in range(8)], axis=0)
        out_ref[k * 128 : (k + 1) * 128, :] = lax.dot_general(
            cells, matrix, (((0,), (0,)), ((), ())), precision=lax.Precision.HIGHEST, preferred_element_type=f32
        )


VMEM = pl.BlockSpec(memory_space=pltpu.VMEM)
SMEM = pl.BlockSpec(memory_space=pltpu.SMEM)


def on_device(tangents, checkpoints, owner_order, land_mask, coefficients):
    block = lax.axis_index("y") * 2 + lax.axis_index("zh")
    core = lax.axis_index("c")
    send, flow, wet = pl.pallas_call(
        pack_kernel,
        out_shape=(
            jax.ShapeDtypeStruct((PEERS, 72, LANES), f32),
            jax.ShapeDtypeStruct((48, LANES), f32),
            jax.ShapeDtypeStruct((24, LANES), f32),
        ),
        in_specs=[SMEM, SMEM, VMEM, VMEM, VMEM],
        out_specs=(VMEM, VMEM, VMEM),
        compiler_params=pltpu.CompilerParams(vmem_limit_bytes=16 * 2**20),
    )(block.reshape(1).astype(jnp.int32), owner_order, tangents, checkpoints, land_mask)

    ring = [(s * 4 + x, (s + step) % 8 * 4 + x) for s in range(8) for x, step in ((3, 1), (0, -1))]
    halo = lax.ppermute(flow, ("y", "zh", "x"), ring)
    own = lax.all_to_all(send, ("y", "zh", "c"), 0, 0, tiled=True)
    flows = jnp.concatenate([flow, halo], axis=0)
    flows = lax.all_to_all(jnp.broadcast_to(flows, (4, 96, LANES)), "x", 0, 0, tiled=True)
    strip = jnp.concatenate([flows[0], flows[1, :48], flows[2, :48], flows[3], wet], axis=0)
    strip = jnp.concatenate([strip, lax.ppermute(strip, "c", [(0, 1), (1, 0)])], axis=0)
    up = [(i, i + 1) for i in range(7)]
    down = [(i + 1, i) for i in range(7)]
    strips = [lax.ppermute(strip, "zl", up), strip, lax.ppermute(strip, "zl", down)]
    own, strips = lax.optimization_barrier((own, strips))
    parts = [lax.ppermute(own, "zl", up), own, lax.ppermute(own, "zl", down)]
    parts = [x.reshape(PEERS * 72, LANES) for x in parts]
    out = pl.pallas_call(
        march_kernel,
        out_shape=jax.ShapeDtypeStruct((8, 96, LANES), f32),
        in_specs=[SMEM] + [VMEM] * 6,
        out_specs=VMEM,
        scratch_shapes=[
            pltpu.VMEM((3, PAIRS, 3, TALL + 8, LANES), f32),
            pltpu.VMEM((3, PAIRS, 3, TALL + 8, LANES), f32),
            pltpu.VMEM((STEPS, 3, 3, TALL + 16, LANES), f32),
            pltpu.VMEM((3, TALL, LANES), f32),
            pltpu.VMEM((COEFS, 3, TALL + 8, LANES), f32),
            pltpu.VMEM((2, 2, 64, LANES), f32),
        ],
        compiler_params=pltpu.CompilerParams(vmem_limit_bytes=32 * 2**20),
    )(core.reshape(1).astype(jnp.int32), *parts, *strips)
    cells = lax.all_to_all(out, ("x", "c"), 0, 0, tiled=True)
    mixed = pl.pallas_call(
        mix_kernel,
        out_shape=jax.ShapeDtypeStruct((768, 128), f32),
        in_specs=[VMEM, VMEM],
        out_specs=VMEM,
        scratch_shapes=[pltpu.VMEM((128, 128), f32)],
        compiler_params=pltpu.CompilerParams(vmem_limit_bytes=16 * 2**20),
    )(coefficients, cells.reshape(768, LANES))
    return mixed.reshape(3, 8, 32, 128).transpose(3, 0, 1, 2)


def solution(mesh):
    fine = jax.sharding.Mesh(mesh.devices.reshape(SIZES), AXES)
    mode, rows = ("y", "zh", "x"), ("zl", "c")
    placed = (
        P(mode, None, rows, None),
        P(None, None, rows, mode),
        P(),
        P(rows, None),
        P(),
    )
    return jax.shard_map(
        on_device, mesh=fine, in_specs=placed, out_specs=P(None, None, rows, mode), check_vma=False
    )
```

```python
import jax
import jax.numpy as jnp
from jax import lax
from jax.experimental import pallas as pl
from jax.experimental.pallas import tpu as pltpu
from jax.sharding import PartitionSpec as P

SIZES = (4, 2, 4, 8, 2)
AXES = ("y", "zh", "x", "zl", "c")
STEPS = 8
LANES = 128
HALO = 16
STRIP = 16
TALL = STRIP + 2 * HALO
PEERS = 16
COEFS = 15
PAIRS = 8
GROUP = 8
f32 = jnp.float32


def edges(left, right, left_turned, right_turned, lane):
    zero = jnp.zeros_like(left)
    out = jnp.where((lane >= 64) & (lane < 80), right_turned, zero)
    out = jnp.where((lane >= 48) & (lane < 64), left_turned, out)
    out = jnp.where(lane < 16, right, out)
    return jnp.where(lane >= 112, left, out)


def from_right(cells, lane):
    a, b, c = (pltpu.roll(x, LANES - 1, 1) for x in cells)
    last, mid = lane == LANES - 1, lane == 63
    return jnp.where(last, c, a), jnp.where(mid, c, b), jnp.where(last, a, jnp.where(mid, b, c))


def from_left(cells, lane):
    a, b, c = (pltpu.roll(x, 1, 1) for x in cells)
    first, mid = lane == 0, lane == 64
    return jnp.where(first, c, a), jnp.where(mid, c, b), jnp.where(first, a, jnp.where(mid, b, c))


def flow_kernel(order_ref, base_ref, flow_ref):
    for high in range(2):
        for f in range(3):
            flow = jnp.concatenate([base_ref[order_ref[high * 4 + low], f] for low in range(4)], axis=1)
            for k in range(4):
                flow_ref[k, (high * 3 + f) * 8 : (high * 3 + f) * 8 + 8, :] = flow


def pack_kernel(block_ref, tan_ref, mask_ref, flows_ref, send_ref, strip_ref):
    lane = lax.broadcasted_iota(jnp.int32, (8, LANES), 1)
    s = block_ref[0]
    wet = [mask_ref[:, k * LANES : (k + 1) * LANES].astype(f32) for k in range(8)]

    def fields(f, _):
        at = f * 8
        early = lane % 32 < 16
        last = [flows_ref[3, pl.ds(pl.multiple_of(high * 24 + at, 8), 8), :] for high in range(2)]
        head = [flows_ref[0, pl.ds(pl.multiple_of(high * 24 + at, 8), 8), :] for high in range(2)]
        to_right = jnp.where(early, pltpu.roll(last[0], LANES - 16, 1), last[1])
        to_left = jnp.where(early, head[0], pltpu.roll(head[1], 16, 1))
        for core in range(2):
            one = [tan_ref[2 * core, f, :, k * LANES : (k + 1) * LANES] * wet[k] for k in range(8)]
            two = [
                pltpu.roll(tan_ref[2 * core + 1, f, :, k * LANES : (k + 1) * LANES] * wet[k], 64, 1) for k in range(8)
            ]
            for k in range(8):
                left, right = (k + 7) % 8, (k + 1) % 8
                halo = edges(one[left], one[right], two[left], two[right], lane)
                border = jnp.where(lax.rem(s + 7, 8) == k, to_left, to_right)
                for v, part in enumerate((one[k], two[k], halo, border)):
                    send_ref[2 * k + core, pl.ds(pl.multiple_of(v * 24 + at, 8), 8), :] = part

    lax.fori_loop(0, 3, fields, None)

    def column(k):
        return mask_ref[:, pl.ds(pl.multiple_of(k * LANES, LANES), LANES)].astype(f32)

    here, left, right = column(s), column(lax.rem(s + 7, 8)), column(lax.rem(s + 1, 8))
    strip_ref[192:200, :] = here
    strip_ref[200:208, :] = pltpu.roll(here, 64, 1)
    strip_ref[208:216, :] = edges(left, right, pltpu.roll(left, 64, 1), pltpu.roll(right, 64, 1), lane)
    for x in range(4):
        strip_ref[x * 48 : x * 48 + 48, :] = flows_ref[x]


CELLS = PEERS * 72
BORDER = CELLS + 2 * 216
NEAR = BORDER + 4 * 24


def near_kernel(block_ref, own_ref, strip_ref, other_ref, near_ref):
    s = block_ref[0]
    for p in range(PEERS):
        near_ref[p * 72 : p * 72 + 72, :] = own_ref[p * 96 : p * 96 + 72, :]
    near_ref[CELLS : CELLS + 216, :] = strip_ref[...]
    near_ref[CELLS + 216 : CELLS + 432, :] = other_ref[...]
    for c in range(2):
        for side, block in enumerate((lax.rem(s + 7, 8), lax.rem(s + 1, 8))):
            at = BORDER + (c * 2 + side) * 24
            start = pl.multiple_of((block * 2 + c) * 96 + 72, 8)
            near_ref[at : at + 24, :] = own_ref[pl.ds(start, 24), :]


def march_kernel(
    core_ref, prev_ref, own_ref, next_ref,
    out_ref, state, middle, base, wet, coef, turn,
):
    lane = lax.broadcasted_iota(jnp.int32, (8, LANES), 1)
    def place(p, _):
        for z, ref in enumerate((prev_ref, own_ref, next_ref)):
            for c in range(2):
                for f in range(3):
                    for v in range(3):
                        at = pl.multiple_of((2 * p + c) * 72 + v * 24 + f * 8, 8)
                        state[f, p, v, z * 16 + c * 8 : z * 16 + c * 8 + 8, :] = ref[pl.ds(at, 8), :]

    lax.fori_loop(0, PAIRS, place, None)
    core = core_ref[0]
    strips = []
    for z, ref in enumerate((prev_ref, own_ref, next_ref)):
        for other in range(2):
            which = 1 - core if other else core
            first, top = CELLS + other * 216, pl.multiple_of(which * 8 + z * 16, 8)
            strips.append((ref, first, BORDER + which * 48, top))
            for v in range(3):
                at = first + 192 + v * 8
                wet[v, pl.ds(top, 8), :] = ref[at : at + 8, :] * 0.25

    def unpack(f, _):
        for ref, first, border, top in strips:
            left, right = (ref[pl.ds(pl.multiple_of(border + side * 24 + f * 8, 8), 8), :] for side in range(2))
            for high in range(2):
                quads = [ref[pl.ds(pl.multiple_of(first + x * 48 + high * 24 + f * 8, 8), 8), :] for x in range(4)]
                for low in range(4):
                    out = pltpu.roll(quads[0], (128 - 32 * low) % 128, 1) if low else quads[0]
                    for x in range(1, 4):
                        turned = pltpu.roll(quads[x], 32 * (x - low) % 128, 1) if x != low else quads[x]
                        out = jnp.where(lane >= 32 * x, turned, out)
                    shift = low * 32 + high * 16
                    sides = [pltpu.roll(cells, (to - shift) % 128, 1) if to != shift else cells
                             for to, cells in ((112, left), (0, right), (48, left), (64, right))]
                    rows = pl.ds(top + 8, 8)
                    base[high * 4 + low, f, 0, rows, :] = out
                    base[high * 4 + low, f, 1, rows, :] = pltpu.roll(out, 64, 1)
                    base[high * 4 + low, f, 2, rows, :] = edges(*sides, lane)

    lax.fori_loop(0, 3, unpack, None)

    def prepare(step, tile):
        top = pl.multiple_of(tile * 8, 8)
        w = [wet[v, pl.ds(top, 8), :] for v in range(3)]

        def rows(f, shift):
            return [base[step, f, v, pl.ds(top + 8 + shift, 8), :] for v in range(3)]

        depth = [x + 1.0 for x in rows(0, 0)]
        b, c = rows(1, 0), rows(2, 0)
        hp, hm = from_right(depth, lane), from_left(depth, lane)
        bp, bm = from_right(b, lane), from_left(b, lane)
        cp, cm = from_right(c, lane), from_left(c, lane)
        hn, hs = rows(0, 1), rows(0, -1)
        bn, bs = rows(1, 1), rows(1, -1)
        cn, cs = rows(2, 1), rows(2, -1)
        for v in range(3):
            q = w[v]
            parts = (
                -q * hp[v], q * hm[v], -q * bp[v], q * bm[v],
                -q * (hn[v] + 1.0), q * (hs[v] + 1.0), -q * cn[v], q * cs[v],
                -q * b[v], -q * c[v],
                -q * (bp[v] - bm[v]), q * (1.0 - (bn[v] - bs[v])), -q * (1.0 + (cp[v] - cm[v])), -q * (cn[v] - cs[v]),
                q,
            )
            for k, part in enumerate(parts):
                coef[k, v, pl.ds(top, 8), :] = part

    def changes(ref, top, pairs):
        rows, north, south = (pl.ds(top + k, 8) for k in (0, 1, -1))
        moved = []
        for p in pairs:
            h, u, m = ([ref[f, p, v, rows, :] for v in range(3)] for f in range(3))
            moved.append(
                (h, u, m, from_right(h, lane), from_left(h, lane), from_right(u, lane), from_left(u, lane))
                + ([a - b for a, b in zip(from_right(m, lane), from_left(m, lane))],)
            )
        out = [([], [], []) for _ in pairs]
        for v in range(3):
            k = [coef[i, v, rows, :] for i in range(COEFS)]
            for p, (h, u, m, hp, hm, up, um, md), fields in zip(pairs, moved, out):
                hn, un, mn = (ref[f, p, v, north, :] for f in range(3))
                hs, us, ms = (ref[f, p, v, south, :] for f in range(3))
                fields[0].append(
                    ((k[0] * up[v] + k[1] * um[v]) + (k[2] * hp[v] + k[3] * hm[v]))
                    + ((k[4] * mn + k[5] * ms) + (k[6] * hn + k[7] * hs))
                )
                fields[1].append(
                    (k[8] * (up[v] - um[v]) + k[9] * (un - us)) + ((k[10] * u[v] + k[11] * m[v]) - k[14] * (hp[v] - hm[v]))
                )
                fields[2].append((k[8] * md[v] + k[9] * (mn - ms)) + ((k[12] * u[v] + k[13] * m[v]) - k[14] * (hn - hs)))
        return out

    def sweep(low, high, body):
        def window(i, _):
            lax.fori_loop(0, PAIRS // GROUP, lambda g, _: body(low + 8 * i, [g * GROUP + k for k in range(GROUP)]), None)

        lax.fori_loop(0, (high - low + 7) // 8, window, None)

    def first(top, pairs):
        for p, change in zip(pairs, changes(state, top, pairs)):
            for f in range(3):
                for v in range(3):
                    middle[f, p, v, pl.ds(top, 8), :] = state[f, p, v, pl.ds(top, 8), :] + change[f][v]

    def second(top, pairs):
        for p, change in zip(pairs, changes(middle, top, pairs)):
            for f in range(3):
                for v in range(3):
                    at = (f, p, v, pl.ds(top, 8), slice(None))
                    state[at] = 0.5 * ((state[at] + middle[at]) + change[f][v])

    def advance(step, _):
        low, high = 2 * step + 1, TALL - 2 * step - 1
        lax.fori_loop(low // 8, (high + 7) // 8, lambda tile, _: prepare(step, tile), None)
        sweep(low, high, first)
        sweep(low + 1, high - 1, second)

    lax.fori_loop(0, STEPS, advance, None)

    def deliver(f, _):
        for c in range(2):
            for v in range(2):
                for p in range(PAIRS):
                    turn[c, v, pl.ds(p, 8, stride=PAIRS), :] = state[f, p, v, HALO + c * 8 : HALO + c * 8 + 8, :]
        for c in range(2):
            for high in range(2):
                for v in range(2):
                    lines = [turn[c, v, (high * 4 + low) * 8 : (high * 4 + low) * 8 + 8, :] for low in range(4)]
                    for x in range(4):
                        at = (x + 2 * v) % 4
                        out = pltpu.roll(lines[0], (128 - 32 * at) % 128, 1) if at else lines[0]
                        for low in range(1, 4):
                            turned = pltpu.roll(lines[low], 32 * (low - at) % 128, 1) if low != at else lines[low]
                            out = jnp.where(lane >= 32 * low, turned, out)
                        out_ref[x * 2 + c, pl.ds(pl.multiple_of(f * 32 + (high * 2 + v) * 8, 8), 8), :] = out

    lax.fori_loop(0, 3, deliver, None)


def mix_kernel(coef_ref, cells_ref, out_ref, mixing):
    row = lax.broadcasted_iota(jnp.int32, (128, 128), 0)
    col = lax.broadcasted_iota(jnp.int32, (128, 128), 1)
    mixing[...] = jnp.where(row <= col, coef_ref[...], 0.0) + jnp.where(row == col, 1.0, 0.0)
    matrix = jnp.concatenate([mixing[pl.ds(t, 8, stride=16), :] for t in range(16)], axis=0)
    for k in range(6):
        cells = jnp.concatenate([cells_ref[p * 96 + k * 16 : p * 96 + k * 16 + 16, :] for p in range(8)], axis=0)
        out_ref[k * 128 : (k + 1) * 128, :] = lax.dot_general(
            cells, matrix, (((0,), (0,)), ((), ())), precision=lax.Precision.HIGHEST, preferred_element_type=f32
        )


VMEM = pl.BlockSpec(memory_space=pltpu.VMEM)
SMEM = pl.BlockSpec(memory_space=pltpu.SMEM)


def on_device(tangents, checkpoints, owner_order, land_mask, coefficients):
    block = lax.axis_index("y") * 2 + lax.axis_index("zh")
    core = lax.axis_index("c")
    s = block.reshape(1).astype(jnp.int32)
    flow = pl.pallas_call(
        flow_kernel,
        out_shape=jax.ShapeDtypeStruct((4, 48, LANES), f32),
        in_specs=[SMEM, VMEM],
        out_specs=VMEM,
        compiler_params=pltpu.CompilerParams(vmem_limit_bytes=16 * 2**20),
    )(owner_order, checkpoints)
    flows = lax.all_to_all(flow, "x", 0, 0, tiled=True)
    send, strip = pl.pallas_call(
        pack_kernel,
        out_shape=(jax.ShapeDtypeStruct((PEERS, 96, LANES), f32), jax.ShapeDtypeStruct((216, LANES), f32)),
        in_specs=[SMEM, VMEM, VMEM, VMEM],
        out_specs=(VMEM, VMEM),
        compiler_params=pltpu.CompilerParams(vmem_limit_bytes=16 * 2**20),
    )(s, tangents, land_mask, flows)
    own = lax.all_to_all(send, ("y", "zh", "c"), 0, 0, tiled=True)
    other = lax.ppermute(strip, "c", [(0, 1), (1, 0)])
    near = pl.pallas_call(
        near_kernel,
        out_shape=jax.ShapeDtypeStruct((NEAR, LANES), f32),
        in_specs=[SMEM, VMEM, VMEM, VMEM],
        out_specs=VMEM,
        compiler_params=pltpu.CompilerParams(vmem_limit_bytes=16 * 2**20),
    )(s, own.reshape(PEERS * 96, LANES), strip, other)
    parts = [
        lax.ppermute(near, "zl", [(i, i + 1) for i in range(7)]),
        near,
        lax.ppermute(near, "zl", [(i + 1, i) for i in range(7)]),
    ]
    out = pl.pallas_call(
        march_kernel,
        out_shape=jax.ShapeDtypeStruct((8, 96, LANES), f32),
        in_specs=[SMEM] + [VMEM] * 3,
        out_specs=VMEM,
        scratch_shapes=[
            pltpu.VMEM((3, PAIRS, 3, TALL + 8, LANES), f32),
            pltpu.VMEM((3, PAIRS, 3, TALL + 8, LANES), f32),
            pltpu.VMEM((STEPS, 3, 3, TALL + 16, LANES), f32),
            pltpu.VMEM((3, TALL, LANES), f32),
            pltpu.VMEM((COEFS, 3, TALL + 8, LANES), f32),
            pltpu.VMEM((2, 2, 64, LANES), f32),
        ],
        compiler_params=pltpu.CompilerParams(vmem_limit_bytes=32 * 2**20),
    )(core.reshape(1).astype(jnp.int32), *parts)
    cells = lax.all_to_all(out, ("x", "c"), 0, 0, tiled=True)
    mixed = pl.pallas_call(
        mix_kernel,
        out_shape=jax.ShapeDtypeStruct((768, 128), f32),
        in_specs=[VMEM, VMEM],
        out_specs=VMEM,
        scratch_shapes=[pltpu.VMEM((128, 128), f32)],
        compiler_params=pltpu.CompilerParams(vmem_limit_bytes=16 * 2**20),
    )(coefficients, cells.reshape(768, LANES))
    return mixed.reshape(3, 8, 32, 128).transpose(3, 0, 1, 2)


def solution(mesh):
    fine = jax.sharding.Mesh(mesh.devices.reshape(SIZES), AXES)
    mode, rows = ("y", "zh", "x"), ("zl", "c")
    placed = (
        P(mode, None, rows, None),
        P(None, None, rows, mode),
        P(),
        P(rows, None),
        P(),
    )
    return jax.shard_map(
        on_device, mesh=fine, in_specs=placed, out_specs=P(None, None, rows, mode), check_vma=False
    )
```

```python
import jax
import jax.numpy as jnp
from jax import lax
from jax.experimental import pallas as pl
from jax.experimental.pallas import tpu as pltpu
from jax.sharding import PartitionSpec as P

SIZES = (4, 2, 4, 8, 2)
AXES = ("y", "zh", "x", "zl", "c")
STEPS = 8
LANES = 128
HALO = 16
STRIP = 16
TALL = STRIP + 2 * HALO
PEERS = 16
COEFS = 15
PAIRS = 8
GROUP = 8
f32 = jnp.float32


def edges(left, right, left_turned, right_turned, lane):
    zero = jnp.zeros_like(left)
    out = jnp.where((lane >= 64) & (lane < 80), right_turned, zero)
    out = jnp.where((lane >= 48) & (lane < 64), left_turned, out)
    out = jnp.where(lane < 16, right, out)
    return jnp.where(lane >= 112, left, out)


def from_right(cells, lane):
    a, b, c = (pltpu.roll(x, LANES - 1, 1) for x in cells)
    last, mid = lane == LANES - 1, lane == 63
    return jnp.where(last, c, a), jnp.where(mid, c, b), jnp.where(last, a, jnp.where(mid, b, c))


def from_left(cells, lane):
    a, b, c = (pltpu.roll(x, 1, 1) for x in cells)
    first, mid = lane == 0, lane == 64
    return jnp.where(first, c, a), jnp.where(mid, c, b), jnp.where(first, a, jnp.where(mid, b, c))


def flow_kernel(block_ref, order_ref, base_ref, mask_ref, raw_ref):
    lane = lax.broadcasted_iota(jnp.int32, (8, LANES), 1)
    s = block_ref[0]
    for high in range(2):
        for f in range(3):
            flow = jnp.concatenate([base_ref[order_ref[high * 4 + low], f] for low in range(4)], axis=1)
            raw_ref[(high * 3 + f) * 8 : (high * 3 + f) * 8 + 8, :] = flow

    def column(k):
        return mask_ref[:, pl.ds(pl.multiple_of(k * LANES, LANES), LANES)].astype(f32)

    here, left, right = column(s), column(lax.rem(s + 7, 8)), column(lax.rem(s + 1, 8))
    raw_ref[48:56, :] = here
    raw_ref[56:64, :] = pltpu.roll(here, 64, 1)
    raw_ref[64:72, :] = edges(left, right, pltpu.roll(left, 64, 1), pltpu.roll(right, 64, 1), lane)


def pack_kernel(tan_ref, mask_ref, send_ref):
    lane = lax.broadcasted_iota(jnp.int32, (8, LANES), 1)
    wet = [mask_ref[:, k * LANES : (k + 1) * LANES].astype(f32) for k in range(8)]

    def fields(f, _):
        for core in range(2):
            one = [tan_ref[2 * core, f, :, k * LANES : (k + 1) * LANES] * wet[k] for k in range(8)]
            two = [
                pltpu.roll(tan_ref[2 * core + 1, f, :, k * LANES : (k + 1) * LANES] * wet[k], 64, 1) for k in range(8)
            ]
            for k in range(8):
                left, right = (k + 7) % 8, (k + 1) % 8
                halo = edges(one[left], one[right], two[left], two[right], lane)
                for v, part in enumerate((one[k], two[k], halo)):
                    send_ref[2 * k + core, pl.ds(pl.multiple_of(v * 24 + f * 8, 8), 8), :] = part

    lax.fori_loop(0, 3, fields, None)


def march_kernel(
    core_ref, prev_ref, own_ref, next_ref, strip_ref, other_ref,
    out_ref, state, middle, base, wet, coef, turn,
):
    lane = lax.broadcasted_iota(jnp.int32, (8, LANES), 1)
    def place(p, _):
        for z, ref in enumerate((prev_ref, own_ref, next_ref)):
            for c in range(2):
                for f in range(3):
                    for v in range(3):
                        at = pl.multiple_of((2 * p + c) * 72 + v * 24 + f * 8, 8)
                        state[f, p, v, z * 16 + c * 8 : z * 16 + c * 8 + 8, :] = ref[pl.ds(at, 8), :]

    lax.fori_loop(0, PAIRS, place, None)
    core, me = core_ref[0], core_ref[1]
    blocks = [lax.rem(me - x + 4, 4) * 288 for x in range(4)]
    places = blocks + [blocks[3] + 144, blocks[0] + 144]
    strips = []
    for other, ref in enumerate((strip_ref, other_ref)):
        for z in range(3):
            top = pl.multiple_of((1 - core if other else core) * 8 + z * 16, 8)
            strips.append((ref, z * 48, top))
            for v in range(3):
                at = 1152 + z * 24 + v * 8
                wet[v, pl.ds(top, 8), :] = ref[at : at + 8, :] * 0.25

    def unpack(part, _):
        high, f = part // 3, part % 3
        for ref, first, top in strips:
            quads = [ref[pl.ds(pl.multiple_of(first + at + part * 8, 8), 8), :] for at in places]
            for low in range(4):
                out = pltpu.roll(quads[0], (128 - 32 * low) % 128, 1) if low else quads[0]
                for x in range(1, 4):
                    turned = pltpu.roll(quads[x], 32 * (x - low) % 128, 1) if x != low else quads[x]
                    out = jnp.where(lane >= 32 * x, turned, out)
                left = pltpu.roll(quads[4], (96 - 32 * low) % 128, 1)
                right = pltpu.roll(quads[5], (128 - 32 * low) % 128, 1)
                halo = edges(left, right, pltpu.roll(left, 64, 1), pltpu.roll(right, 64, 1), lane)
                rows = pl.ds(top + 8, 8)
                base[high * 4 + low, f, 0, rows, :] = out
                base[high * 4 + low, f, 1, rows, :] = pltpu.roll(out, 64, 1)
                base[high * 4 + low, f, 2, rows, :] = halo

    lax.fori_loop(0, 6, unpack, None)

    def prepare(step, tile):
        top = pl.multiple_of(tile * 8, 8)
        w = [wet[v, pl.ds(top, 8), :] for v in range(3)]

        def rows(f, shift):
            return [base[step, f, v, pl.ds(top + 8 + shift, 8), :] for v in range(3)]

        depth = [x + 1.0 for x in rows(0, 0)]
        b, c = rows(1, 0), rows(2, 0)
        hp, hm = from_right(depth, lane), from_left(depth, lane)
        bp, bm = from_right(b, lane), from_left(b, lane)
        cp, cm = from_right(c, lane), from_left(c, lane)
        hn, hs = rows(0, 1), rows(0, -1)
        bn, bs = rows(1, 1), rows(1, -1)
        cn, cs = rows(2, 1), rows(2, -1)
        for v in range(3):
            q = w[v]
            parts = (
                -q * hp[v], q * hm[v], -q * bp[v], q * bm[v],
                -q * (hn[v] + 1.0), q * (hs[v] + 1.0), -q * cn[v], q * cs[v],
                -q * b[v], -q * c[v],
                -q * (bp[v] - bm[v]), q * (1.0 - (bn[v] - bs[v])), -q * (1.0 + (cp[v] - cm[v])), -q * (cn[v] - cs[v]),
                q,
            )
            for k, part in enumerate(parts):
                coef[k, v, pl.ds(top, 8), :] = part

    def changes(ref, top, pairs):
        rows, north, south = (pl.ds(top + k, 8) for k in (0, 1, -1))
        moved = []
        for p in pairs:
            h, u, m = ([ref[f, p, v, rows, :] for v in range(3)] for f in range(3))
            moved.append(
                (h, u, m, from_right(h, lane), from_left(h, lane), from_right(u, lane), from_left(u, lane))
                + ([a - b for a, b in zip(from_right(m, lane), from_left(m, lane))],)
            )
        out = [([], [], []) for _ in pairs]
        for v in range(3):
            k = [coef[i, v, rows, :] for i in range(COEFS)]
            for p, (h, u, m, hp, hm, up, um, md), fields in zip(pairs, moved, out):
                hn, un, mn = (ref[f, p, v, north, :] for f in range(3))
                hs, us, ms = (ref[f, p, v, south, :] for f in range(3))
                fields[0].append(
                    ((k[0] * up[v] + k[1] * um[v]) + (k[2] * hp[v] + k[3] * hm[v]))
                    + ((k[4] * mn + k[5] * ms) + (k[6] * hn + k[7] * hs))
                )
                fields[1].append(
                    (k[8] * (up[v] - um[v]) + k[9] * (un - us)) + ((k[10] * u[v] + k[11] * m[v]) - k[14] * (hp[v] - hm[v]))
                )
                fields[2].append((k[8] * md[v] + k[9] * (mn - ms)) + ((k[12] * u[v] + k[13] * m[v]) - k[14] * (hn - hs)))
        return out

    def sweep(low, high, body):
        def window(i, _):
            lax.fori_loop(0, PAIRS // GROUP, lambda g, _: body(low + 8 * i, [g * GROUP + k for k in range(GROUP)]), None)

        lax.fori_loop(0, (high - low + 7) // 8, window, None)

    def first(top, pairs):
        for p, change in zip(pairs, changes(state, top, pairs)):
            for f in range(3):
                for v in range(3):
                    middle[f, p, v, pl.ds(top, 8), :] = state[f, p, v, pl.ds(top, 8), :] + change[f][v]

    def second(top, pairs):
        for p, change in zip(pairs, changes(middle, top, pairs)):
            for f in range(3):
                for v in range(3):
                    at = (f, p, v, pl.ds(top, 8), slice(None))
                    state[at] = 0.5 * ((state[at] + middle[at]) + change[f][v])

    def advance(step, _):
        low, high = 2 * step + 1, TALL - 2 * step - 1
        lax.fori_loop(low // 8, (high + 7) // 8, lambda tile, _: prepare(step, tile), None)
        sweep(low, high, first)
        sweep(low + 1, high - 1, second)

    lax.fori_loop(0, STEPS, advance, None)

    def deliver(f, _):
        for c in range(2):
            for v in range(2):
                for p in range(PAIRS):
                    turn[c, v, pl.ds(p, 8, stride=PAIRS), :] = state[f, p, v, HALO + c * 8 : HALO + c * 8 + 8, :]
        for c in range(2):
            for high in range(2):
                for v in range(2):
                    lines = [turn[c, v, (high * 4 + low) * 8 : (high * 4 + low) * 8 + 8, :] for low in range(4)]
                    for x in range(4):
                        at = (x + 2 * v) % 4
                        out = pltpu.roll(lines[0], (128 - 32 * at) % 128, 1) if at else lines[0]
                        for low in range(1, 4):
                            turned = pltpu.roll(lines[low], 32 * (low - at) % 128, 1) if low != at else lines[low]
                            out = jnp.where(lane >= 32 * low, turned, out)
                        out_ref[x * 2 + c, pl.ds(pl.multiple_of(f * 32 + (high * 2 + v) * 8, 8), 8), :] = out

    lax.fori_loop(0, 3, deliver, None)


def mix_kernel(coef_ref, cells_ref, out_ref, mixing):
    row = lax.broadcasted_iota(jnp.int32, (128, 128), 0)
    col = lax.broadcasted_iota(jnp.int32, (128, 128), 1)
    mixing[...] = jnp.where(row <= col, coef_ref[...], 0.0) + jnp.where(row == col, 1.0, 0.0)
    matrix = jnp.concatenate([mixing[pl.ds(t, 8, stride=16), :] for t in range(16)], axis=0)
    for k in range(6):
        cells = jnp.concatenate([cells_ref[p * 96 + k * 16 : p * 96 + k * 16 + 16, :] for p in range(8)], axis=0)
        out_ref[k * 128 : (k + 1) * 128, :] = lax.dot_general(
            cells, matrix, (((0,), (0,)), ((), ())), precision=lax.Precision.HIGHEST, preferred_element_type=f32
        )


VMEM = pl.BlockSpec(memory_space=pltpu.VMEM)
SMEM = pl.BlockSpec(memory_space=pltpu.SMEM)


def on_device(tangents, checkpoints, owner_order, land_mask, coefficients):
    block = lax.axis_index("y") * 2 + lax.axis_index("zh")
    core = lax.axis_index("c")
    raw = pl.pallas_call(
        flow_kernel,
        out_shape=jax.ShapeDtypeStruct((72, LANES), f32),
        in_specs=[SMEM, SMEM, VMEM, VMEM],
        out_specs=VMEM,
        compiler_params=pltpu.CompilerParams(vmem_limit_bytes=16 * 2**20),
    )(block.reshape(1).astype(jnp.int32), owner_order, checkpoints, land_mask)
    send = pl.pallas_call(
        pack_kernel,
        out_shape=jax.ShapeDtypeStruct((PEERS, 72, LANES), f32),
        in_specs=[VMEM, VMEM],
        out_specs=VMEM,
        compiler_params=pltpu.CompilerParams(vmem_limit_bytes=16 * 2**20),
    )(tangents, land_mask)
    up = [(i, i + 1) for i in range(7)]
    down = [(i + 1, i) for i in range(7)]
    chips = [lax.ppermute(raw, "zl", up), raw, lax.ppermute(raw, "zl", down)]
    flow = jnp.concatenate([x[:48] for x in chips], axis=0)
    wet = [x[48:] for x in chips]
    ring = [(s * 4 + x, (s + step) % 8 * 4 + x) for s in range(8) for x, step in ((3, 1), (0, -1))]
    halo = lax.ppermute(flow, ("y", "zh", "x"), ring)
    send, halo = lax.optimization_barrier((send, halo))
    own = lax.all_to_all(send, ("y", "zh", "c"), 0, 0, tiled=True)
    flow = jnp.concatenate([flow, halo], axis=0)
    flows = [lax.ppermute(flow, "x", [(i, (i + k) % 4) for i in range(4)]) for k in (1, 2, 3)]
    strip = jnp.concatenate([flow, *flows, *wet], axis=0)
    other = lax.ppermute(strip, "c", [(0, 1), (1, 0)])
    own, other = lax.optimization_barrier((own, other))
    parts = [lax.ppermute(own, "zl", up), own, lax.ppermute(own, "zl", down)]
    parts = [x.reshape(PEERS * 72, LANES) for x in parts]
    out = pl.pallas_call(
        march_kernel,
        out_shape=jax.ShapeDtypeStruct((8, 96, LANES), f32),
        in_specs=[SMEM] + [VMEM] * 5,
        out_specs=VMEM,
        scratch_shapes=[
            pltpu.VMEM((3, PAIRS, 3, TALL + 8, LANES), f32),
            pltpu.VMEM((3, PAIRS, 3, TALL + 8, LANES), f32),
            pltpu.VMEM((STEPS, 3, 3, TALL + 16, LANES), f32),
            pltpu.VMEM((3, TALL, LANES), f32),
            pltpu.VMEM((COEFS, 3, TALL + 8, LANES), f32),
            pltpu.VMEM((2, 2, 64, LANES), f32),
        ],
        compiler_params=pltpu.CompilerParams(vmem_limit_bytes=32 * 2**20),
    )(jnp.stack([core, lax.axis_index("x")]).astype(jnp.int32), *parts, strip, other)
    cells = lax.all_to_all(out, ("x", "c"), 0, 0, tiled=True)
    mixed = pl.pallas_call(
        mix_kernel,
        out_shape=jax.ShapeDtypeStruct((768, 128), f32),
        in_specs=[VMEM, VMEM],
        out_specs=VMEM,
        scratch_shapes=[pltpu.VMEM((128, 128), f32)],
        compiler_params=pltpu.CompilerParams(vmem_limit_bytes=16 * 2**20),
    )(coefficients, cells.reshape(768, LANES))
    return mixed.reshape(3, 8, 32, 128).transpose(3, 0, 1, 2)


def solution(mesh):
    fine = jax.sharding.Mesh(mesh.devices.reshape(SIZES), AXES)
    mode, rows = ("y", "zh", "x"), ("zl", "c")
    placed = (
        P(mode, None, rows, None),
        P(None, None, rows, mode),
        P(),
        P(rows, None),
        P(),
    )
    return jax.shard_map(
        on_device, mesh=fine, in_specs=placed, out_specs=P(None, None, rows, mode), check_vma=False
    )
```

```python
import jax
import jax.numpy as jnp
from jax import lax
from jax.experimental import pallas as pl
from jax.experimental.pallas import tpu as pltpu
from jax.sharding import PartitionSpec as P

SIZES = (4, 2, 4, 8, 2)
AXES = ("y", "zh", "x", "zl", "c")
STEPS = 8
LANES = 128
HALO = 16
STRIP = 16
TALL = STRIP + 2 * HALO
PEERS = 16
COEFS = 15
PAIRS = 8
GROUP = 8
f32 = jnp.float32


def edges(left, right, left_turned, right_turned, lane):
    zero = jnp.zeros_like(left)
    out = jnp.where((lane >= 64) & (lane < 80), right_turned, zero)
    out = jnp.where((lane >= 48) & (lane < 64), left_turned, out)
    out = jnp.where(lane < 16, right, out)
    return jnp.where(lane >= 112, left, out)


def from_right(cells, lane):
    a, b, c = (pltpu.roll(x, LANES - 1, 1) for x in cells)
    last, mid = lane == LANES - 1, lane == 63
    return jnp.where(last, c, a), jnp.where(mid, c, b), jnp.where(last, a, jnp.where(mid, b, c))


def from_left(cells, lane):
    a, b, c = (pltpu.roll(x, 1, 1) for x in cells)
    first, mid = lane == 0, lane == 64
    return jnp.where(first, c, a), jnp.where(mid, c, b), jnp.where(first, a, jnp.where(mid, b, c))


def flow_kernel(block_ref, order_ref, base_ref, mask_ref, raw_ref):
    lane = lax.broadcasted_iota(jnp.int32, (8, LANES), 1)
    s = block_ref[0]
    for high in range(2):
        for f in range(3):
            flow = jnp.concatenate([base_ref[order_ref[high * 4 + low], f] for low in range(4)], axis=1)
            raw_ref[(high * 3 + f) * 8 : (high * 3 + f) * 8 + 8, :] = flow

    def column(k):
        return mask_ref[:, pl.ds(pl.multiple_of(k * LANES, LANES), LANES)].astype(f32)

    here, left, right = column(s), column(lax.rem(s + 7, 8)), column(lax.rem(s + 1, 8))
    raw_ref[48:56, :] = here
    raw_ref[56:64, :] = pltpu.roll(here, 64, 1)
    raw_ref[64:72, :] = edges(left, right, pltpu.roll(left, 64, 1), pltpu.roll(right, 64, 1), lane)


def pack_kernel(tan_ref, mask_ref, send_ref):
    lane = lax.broadcasted_iota(jnp.int32, (8, LANES), 1)
    wet = [mask_ref[:, k * LANES : (k + 1) * LANES].astype(f32) for k in range(8)]

    def fields(f, _):
        for core in range(2):
            one = [tan_ref[2 * core, f, :, k * LANES : (k + 1) * LANES] * wet[k] for k in range(8)]
            two = [
                pltpu.roll(tan_ref[2 * core + 1, f, :, k * LANES : (k + 1) * LANES] * wet[k], 64, 1) for k in range(8)
            ]
            for k in range(8):
                left, right = (k + 7) % 8, (k + 1) % 8
                halo = edges(one[left], one[right], two[left], two[right], lane)
                for v, part in enumerate((one[k], two[k], halo)):
                    send_ref[2 * k + core, pl.ds(pl.multiple_of(v * 24 + f * 8, 8), 8), :] = part

    lax.fori_loop(0, 3, fields, None)


def from_block(me, x):
    return lax.rem(me - x + 4, 4) * 216


def border_kernel(core_ref, strip_ref, other_ref, to_right_ref, to_left_ref):
    early = lax.broadcasted_iota(jnp.int32, (8, LANES), 1) % 32 < 16
    core, me = core_ref[0], core_ref[1]
    head, last = from_block(me, 0), from_block(me, 3)
    for other, ref in enumerate((strip_ref, other_ref)):
        which = 1 - core if other else core
        for z in range(3):
            for f in range(3):
                to = pl.ds(pl.multiple_of((which * 3 + z) * 24 + f * 8, 8), 8)
                rows = [z * 72 + high * 24 + f * 8 for high in range(2)]
                a, b = (ref[pl.ds(pl.multiple_of(last + k, 8), 8), :] for k in rows)
                to_right_ref[to, :] = jnp.where(early, pltpu.roll(a, LANES - 16, 1), b)
                a, b = (ref[pl.ds(pl.multiple_of(head + k, 8), 8), :] for k in rows)
                to_left_ref[to, :] = jnp.where(early, a, pltpu.roll(b, 16, 1))


def march_kernel(
    core_ref, prev_ref, own_ref, next_ref, strip_ref, other_ref, left_ref, right_ref,
    out_ref, state, middle, base, wet, coef, turn,
):
    lane = lax.broadcasted_iota(jnp.int32, (8, LANES), 1)
    def place(p, _):
        for z, ref in enumerate((prev_ref, own_ref, next_ref)):
            for c in range(2):
                for f in range(3):
                    for v in range(3):
                        at = pl.multiple_of((2 * p + c) * 72 + v * 24 + f * 8, 8)
                        state[f, p, v, z * 16 + c * 8 : z * 16 + c * 8 + 8, :] = ref[pl.ds(at, 8), :]

    lax.fori_loop(0, PAIRS, place, None)
    core, me = core_ref[0], core_ref[1]
    blocks = [from_block(me, x) for x in range(4)]
    strips = []
    for other, ref in enumerate((strip_ref, other_ref)):
        for z in range(3):
            which = 1 - core if other else core
            top = pl.multiple_of(which * 8 + z * 16, 8)
            strips.append((ref, z * 72, (which * 3 + z) * 24, top))
            for v in range(3):
                at = z * 72 + 48 + v * 8
                wet[v, pl.ds(top, 8), :] = ref[at : at + 8, :] * 0.25

    def unpack(f, _):
        for ref, first, border, top in strips:
            at = pl.multiple_of(border + f * 8, 8)
            left, right = left_ref[pl.ds(at, 8), :], right_ref[pl.ds(at, 8), :]
            for high in range(2):
                quads = [ref[pl.ds(pl.multiple_of(first + at + high * 24 + f * 8, 8), 8), :] for at in blocks]
                for low in range(4):
                    out = pltpu.roll(quads[0], (128 - 32 * low) % 128, 1) if low else quads[0]
                    for x in range(1, 4):
                        turned = pltpu.roll(quads[x], 32 * (x - low) % 128, 1) if x != low else quads[x]
                        out = jnp.where(lane >= 32 * x, turned, out)
                    shift = low * 32 + high * 16
                    sides = [pltpu.roll(cells, (to - shift) % 128, 1) if to != shift else cells
                             for to, cells in ((112, left), (0, right), (48, left), (64, right))]
                    rows = pl.ds(top + 8, 8)
                    base[high * 4 + low, f, 0, rows, :] = out
                    base[high * 4 + low, f, 1, rows, :] = pltpu.roll(out, 64, 1)
                    base[high * 4 + low, f, 2, rows, :] = edges(*sides, lane)

    lax.fori_loop(0, 3, unpack, None)

    def prepare(step, tile):
        top = pl.multiple_of(tile * 8, 8)
        w = [wet[v, pl.ds(top, 8), :] for v in range(3)]

        def rows(f, shift):
            return [base[step, f, v, pl.ds(top + 8 + shift, 8), :] for v in range(3)]

        depth = [x + 1.0 for x in rows(0, 0)]
        b, c = rows(1, 0), rows(2, 0)
        hp, hm = from_right(depth, lane), from_left(depth, lane)
        bp, bm = from_right(b, lane), from_left(b, lane)
        cp, cm = from_right(c, lane), from_left(c, lane)
        hn, hs = rows(0, 1), rows(0, -1)
        bn, bs = rows(1, 1), rows(1, -1)
        cn, cs = rows(2, 1), rows(2, -1)
        for v in range(3):
            q = w[v]
            parts = (
                -q * hp[v], q * hm[v], -q * bp[v], q * bm[v],
                -q * (hn[v] + 1.0), q * (hs[v] + 1.0), -q * cn[v], q * cs[v],
                -q * b[v], -q * c[v],
                -q * (bp[v] - bm[v]), q * (1.0 - (bn[v] - bs[v])), -q * (1.0 + (cp[v] - cm[v])), -q * (cn[v] - cs[v]),
                q,
            )
            for k, part in enumerate(parts):
                coef[k, v, pl.ds(top, 8), :] = part

    def changes(ref, top, pairs):
        rows, north, south = (pl.ds(top + k, 8) for k in (0, 1, -1))
        moved = []
        for p in pairs:
            h, u, m = ([ref[f, p, v, rows, :] for v in range(3)] for f in range(3))
            moved.append(
                (h, u, m, from_right(h, lane), from_left(h, lane), from_right(u, lane), from_left(u, lane))
                + ([a - b for a, b in zip(from_right(m, lane), from_left(m, lane))],)
            )
        out = [([], [], []) for _ in pairs]
        for v in range(3):
            k = [coef[i, v, rows, :] for i in range(COEFS)]
            for p, (h, u, m, hp, hm, up, um, md), fields in zip(pairs, moved, out):
                hn, un, mn = (ref[f, p, v, north, :] for f in range(3))
                hs, us, ms = (ref[f, p, v, south, :] for f in range(3))
                fields[0].append(
                    ((k[0] * up[v] + k[1] * um[v]) + (k[2] * hp[v] + k[3] * hm[v]))
                    + ((k[4] * mn + k[5] * ms) + (k[6] * hn + k[7] * hs))
                )
                fields[1].append(
                    (k[8] * (up[v] - um[v]) + k[9] * (un - us)) + ((k[10] * u[v] + k[11] * m[v]) - k[14] * (hp[v] - hm[v]))
                )
                fields[2].append((k[8] * md[v] + k[9] * (mn - ms)) + ((k[12] * u[v] + k[13] * m[v]) - k[14] * (hn - hs)))
        return out

    def sweep(low, high, body):
        def window(i, _):
            lax.fori_loop(0, PAIRS // GROUP, lambda g, _: body(low + 8 * i, [g * GROUP + k for k in range(GROUP)]), None)

        lax.fori_loop(0, (high - low + 7) // 8, window, None)

    def first(top, pairs):
        for p, change in zip(pairs, changes(state, top, pairs)):
            for f in range(3):
                for v in range(3):
                    middle[f, p, v, pl.ds(top, 8), :] = state[f, p, v, pl.ds(top, 8), :] + change[f][v]

    def second(top, pairs):
        for p, change in zip(pairs, changes(middle, top, pairs)):
            for f in range(3):
                for v in range(3):
                    at = (f, p, v, pl.ds(top, 8), slice(None))
                    state[at] = 0.5 * ((state[at] + middle[at]) + change[f][v])

    def advance(step, _):
        low, high = 2 * step + 1, TALL - 2 * step - 1
        lax.fori_loop(low // 8, (high + 7) // 8, lambda tile, _: prepare(step, tile), None)
        sweep(low, high, first)
        sweep(low + 1, high - 1, second)

    lax.fori_loop(0, STEPS, advance, None)

    def deliver(f, _):
        for c in range(2):
            for v in range(2):
                for p in range(PAIRS):
                    turn[c, v, pl.ds(p, 8, stride=PAIRS), :] = state[f, p, v, HALO + c * 8 : HALO + c * 8 + 8, :]
        for c in range(2):
            for high in range(2):
                for v in range(2):
                    lines = [turn[c, v, (high * 4 + low) * 8 : (high * 4 + low) * 8 + 8, :] for low in range(4)]
                    for x in range(4):
                        at = (x + 2 * v) % 4
                        out = pltpu.roll(lines[0], (128 - 32 * at) % 128, 1) if at else lines[0]
                        for low in range(1, 4):
                            turned = pltpu.roll(lines[low], 32 * (low - at) % 128, 1) if low != at else lines[low]
                            out = jnp.where(lane >= 32 * low, turned, out)
                        out_ref[x * 2 + c, pl.ds(pl.multiple_of(f * 32 + (high * 2 + v) * 8, 8), 8), :] = out

    lax.fori_loop(0, 3, deliver, None)


def mix_kernel(coef_ref, cells_ref, out_ref, mixing):
    row = lax.broadcasted_iota(jnp.int32, (128, 128), 0)
    col = lax.broadcasted_iota(jnp.int32, (128, 128), 1)
    mixing[...] = jnp.where(row <= col, coef_ref[...], 0.0) + jnp.where(row == col, 1.0, 0.0)
    matrix = jnp.concatenate([mixing[pl.ds(t, 8, stride=16), :] for t in range(16)], axis=0)
    for k in range(6):
        cells = jnp.concatenate([cells_ref[p * 96 + k * 16 : p * 96 + k * 16 + 16, :] for p in range(8)], axis=0)
        out_ref[k * 128 : (k + 1) * 128, :] = lax.dot_general(
            cells, matrix, (((0,), (0,)), ((), ())), precision=lax.Precision.HIGHEST, preferred_element_type=f32
        )


VMEM = pl.BlockSpec(memory_space=pltpu.VMEM)
SMEM = pl.BlockSpec(memory_space=pltpu.SMEM)


def on_device(tangents, checkpoints, owner_order, land_mask, coefficients):
    block = lax.axis_index("y") * 2 + lax.axis_index("zh")
    core = lax.axis_index("c")
    raw = pl.pallas_call(
        flow_kernel,
        out_shape=jax.ShapeDtypeStruct((72, LANES), f32),
        in_specs=[SMEM, SMEM, VMEM, VMEM],
        out_specs=VMEM,
        compiler_params=pltpu.CompilerParams(vmem_limit_bytes=16 * 2**20),
    )(block.reshape(1).astype(jnp.int32), owner_order, checkpoints, land_mask)
    send = pl.pallas_call(
        pack_kernel,
        out_shape=jax.ShapeDtypeStruct((PEERS, 72, LANES), f32),
        in_specs=[VMEM, VMEM],
        out_specs=VMEM,
        compiler_params=pltpu.CompilerParams(vmem_limit_bytes=16 * 2**20),
    )(tangents, land_mask)
    up = [(i, i + 1) for i in range(7)]
    down = [(i + 1, i) for i in range(7)]
    own = lax.all_to_all(send, ("y", "zh", "c"), 0, 0, tiled=True)
    chips = jnp.concatenate([lax.ppermute(raw, "zl", up), raw, lax.ppermute(raw, "zl", down)], axis=0)
    strip = jnp.concatenate(
        [chips] + [lax.ppermute(chips, "x", [(i, (i + k) % 4) for i in range(4)]) for k in (1, 2, 3)], axis=0
    )
    other = lax.ppermute(strip, "c", [(0, 1), (1, 0)])
    here = jnp.stack([core, lax.axis_index("x")]).astype(jnp.int32)
    borders = pl.pallas_call(
        border_kernel,
        out_shape=(jax.ShapeDtypeStruct((144, LANES), f32), jax.ShapeDtypeStruct((144, LANES), f32)),
        in_specs=[SMEM, VMEM, VMEM],
        out_specs=(VMEM, VMEM),
        compiler_params=pltpu.CompilerParams(vmem_limit_bytes=16 * 2**20),
    )(here, strip, other)
    own, borders = lax.optimization_barrier((own, borders))
    parts = [lax.ppermute(own, "zl", up), own, lax.ppermute(own, "zl", down)]
    left = lax.ppermute(borders[0], ("y", "zh"), [(i, (i + 1) % 8) for i in range(8)])
    right = lax.ppermute(borders[1], ("y", "zh"), [((i + 1) % 8, i) for i in range(8)])
    parts = [x.reshape(PEERS * 72, LANES) for x in parts]
    out = pl.pallas_call(
        march_kernel,
        out_shape=jax.ShapeDtypeStruct((8, 96, LANES), f32),
        in_specs=[SMEM] + [VMEM] * 7,
        out_specs=VMEM,
        scratch_shapes=[
            pltpu.VMEM((3, PAIRS, 3, TALL + 8, LANES), f32),
            pltpu.VMEM((3, PAIRS, 3, TALL + 8, LANES), f32),
            pltpu.VMEM((STEPS, 3, 3, TALL + 16, LANES), f32),
            pltpu.VMEM((3, TALL, LANES), f32),
            pltpu.VMEM((COEFS, 3, TALL + 8, LANES), f32),
            pltpu.VMEM((2, 2, 64, LANES), f32),
        ],
        compiler_params=pltpu.CompilerParams(vmem_limit_bytes=32 * 2**20),
    )(here, *parts, strip, other, left, right)
    cells = lax.all_to_all(out, ("x", "c"), 0, 0, tiled=True)
    mixed = pl.pallas_call(
        mix_kernel,
        out_shape=jax.ShapeDtypeStruct((768, 128), f32),
        in_specs=[VMEM, VMEM],
        out_specs=VMEM,
        scratch_shapes=[pltpu.VMEM((128, 128), f32)],
        compiler_params=pltpu.CompilerParams(vmem_limit_bytes=16 * 2**20),
    )(coefficients, cells.reshape(768, LANES))
    return mixed.reshape(3, 8, 32, 128).transpose(3, 0, 1, 2)


def solution(mesh):
    fine = jax.sharding.Mesh(mesh.devices.reshape(SIZES), AXES)
    mode, rows = ("y", "zh", "x"), ("zl", "c")
    placed = (
        P(mode, None, rows, None),
        P(None, None, rows, mode),
        P(),
        P(rows, None),
        P(),
    )
    return jax.shard_map(
        on_device, mesh=fine, in_specs=placed, out_specs=P(None, None, rows, mode), check_vma=False
    )
```

```python
import jax
import jax.numpy as jnp
from jax import lax
from jax.experimental import pallas as pl
from jax.experimental.pallas import tpu as pltpu
from jax.sharding import PartitionSpec as P

SIZES = (4, 2, 4, 8, 2)
AXES = ("y", "zh", "x", "zl", "c")
STEPS = 8
LANES = 128
HALO = 16
STRIP = 16
TALL = STRIP + 2 * HALO
PEERS = 16
COEFS = 15
QUADS = 4
GROUP = 4
f32 = jnp.float32


PARTS = 5


def halo_columns(left, right, lane):
    return jnp.where(lane >= 112, left, right)


def spread(inner, halo, part, lane):
    column = (lane % 32) * PARTS + (part - HALO)
    index = (column + LANES) % LANES
    a, b = (jnp.take_along_axis(x, index, axis=1) for x in (inner, halo))
    return jnp.where((column >= 0) & (column < LANES), a, b)


def gathered(parts, quarter, lane):
    column = lane + HALO
    index, rest = column // PARTS + quarter * 32, column % PARTS
    out = jnp.take_along_axis(parts[0], index, axis=1)
    for j in range(1, PARTS):
        out = jnp.where(rest == j, jnp.take_along_axis(parts[j], index, axis=1), out)
    return out


def from_right(cells):
    return [*cells[1:], pltpu.roll(cells[0], LANES - 1, 1)]


def from_left(cells):
    return [pltpu.roll(cells[-1], 1, 1), *cells[:-1]]


def flow_kernel(block_ref, order_ref, base_ref, mask_ref, raw_ref):
    lane = lax.broadcasted_iota(jnp.int32, (8, LANES), 1)
    s = block_ref[0]
    for high in range(2):
        for f in range(3):
            flow = jnp.concatenate([base_ref[order_ref[high * 4 + low], f] for low in range(4)], axis=1)
            raw_ref[(high * 3 + f) * 8 : (high * 3 + f) * 8 + 8, :] = flow

    def column(k):
        return mask_ref[:, pl.ds(pl.multiple_of(k * LANES, LANES), LANES)].astype(f32)

    raw_ref[48:56, :] = column(s)
    raw_ref[56:64, :] = halo_columns(column(lax.rem(s + 7, 8)), column(lax.rem(s + 1, 8)), lane)


def pack_kernel(tan_ref, mask_ref, send_ref):
    lane = lax.broadcasted_iota(jnp.int32, (8, LANES), 1)
    wet = [mask_ref[:, k * LANES : (k + 1) * LANES].astype(f32) for k in range(8)]

    def send(core, _):
        cells = [
            [[tan_ref[2 * core + q, f, :, k * LANES : (k + 1) * LANES] * wet[k] for k in range(8)] for f in range(3)]
            for q in range(2)
        ]
        for k in range(8):
            lines = []
            for f in range(3):
                for j in range(PARTS):
                    for q in range(2):
                        row = cells[q][f]
                        halo = halo_columns(row[(k + 7) % 8], row[(k + 1) % 8], lane)
                        lines.append(spread(row[k], halo, j, lane))
            lines += lines[:2]
            for i in range(8):
                a, b, c, d = lines[4 * i : 4 * i + 4]
                out = jnp.where(lane < 32, a, jnp.where(lane < 64, b, jnp.where(lane < 96, c, d)))
                send_ref[2 * k + core, i * 8 : i * 8 + 8, :] = out

    lax.fori_loop(0, 2, send, None)


def march_kernel(
    core_ref, prev_ref, own_ref, next_ref, strip_ref, other_ref,
    out_ref, state, middle, base, wet, coef, turn,
):
    lane = lax.broadcasted_iota(jnp.int32, (8, LANES), 1)
    def place(quad, _):
        for z, ref in enumerate((prev_ref, own_ref, next_ref)):
            for c in range(2):
                for f in range(3):
                    for j in range(PARTS):
                        i, odd = divmod(f * PARTS + j, 2)
                        one, two = (
                            ref[pl.ds(pl.multiple_of((4 * quad + 2 * p + c) * 64 + i * 8, 8), 8), :] for p in range(2)
                        )
                        one, two = (pltpu.roll(one, 64, 1), two) if odd else (one, pltpu.roll(two, 64, 1))
                        rows = slice(z * 16 + c * 8, z * 16 + c * 8 + 8)
                        state[f, quad, j, rows, :] = jnp.where(lane < 64, one, two)

    lax.fori_loop(0, QUADS, place, None)
    core, me = core_ref[0], core_ref[1]
    blocks = [lax.rem(me - x + 4, 4) * 288 for x in range(4)]
    places = blocks + [blocks[3] + 144, blocks[0] + 144]
    strips = []
    for other, ref in enumerate((strip_ref, other_ref)):
        for z in range(3):
            top = pl.multiple_of((1 - core if other else core) * 8 + z * 16, 8)
            strips.append((ref, z * 48, top))
            at = 1152 + z * 16
            for j in range(PARTS):
                wet[j, pl.ds(top, 8), :] = spread(ref[at : at + 8, :], ref[at + 8 : at + 16, :], j, lane) * 0.25

    def unpack(part, _):
        high, f = part // 3, part % 3
        for ref, first, top in strips:
            quads = [ref[pl.ds(pl.multiple_of(first + at + part * 8, 8), 8), :] for at in places]
            for low in range(4):
                out = pltpu.roll(quads[0], (128 - 32 * low) % 128, 1) if low else quads[0]
                for x in range(1, 4):
                    turned = pltpu.roll(quads[x], 32 * (x - low) % 128, 1) if x != low else quads[x]
                    out = jnp.where(lane >= 32 * x, turned, out)
                left = pltpu.roll(quads[4], (96 - 32 * low) % 128, 1)
                right = pltpu.roll(quads[5], (128 - 32 * low) % 128, 1)
                halo = halo_columns(left, right, lane)
                for j in range(PARTS):
                    base[high * 4 + low, f, j, pl.ds(top + 8, 8), :] = spread(out, halo, j, lane)

    lax.fori_loop(0, 6, unpack, None)

    def prepare(step, tile):
        top = pl.multiple_of(tile * 8, 8)
        w = [wet[v, pl.ds(top, 8), :] for v in range(PARTS)]

        def rows(f, shift):
            return [base[step, f, v, pl.ds(top + 8 + shift, 8), :] for v in range(PARTS)]

        depth = [x + 1.0 for x in rows(0, 0)]
        b, c = rows(1, 0), rows(2, 0)
        hp, hm = from_right(depth), from_left(depth)
        bp, bm = from_right(b), from_left(b)
        cp, cm = from_right(c), from_left(c)
        hn, hs = rows(0, 1), rows(0, -1)
        bn, bs = rows(1, 1), rows(1, -1)
        cn, cs = rows(2, 1), rows(2, -1)
        for v in range(PARTS):
            q = w[v]
            parts = (
                -q * hp[v], q * hm[v], -q * bp[v], q * bm[v],
                -q * (hn[v] + 1.0), q * (hs[v] + 1.0), -q * cn[v], q * cs[v],
                -q * b[v], -q * c[v],
                -q * (bp[v] - bm[v]), q * (1.0 - (bn[v] - bs[v])), -q * (1.0 + (cp[v] - cm[v])), -q * (cn[v] - cs[v]),
                q,
            )
            for k, part in enumerate(parts):
                coef[k, v, pl.ds(top, 8), :] = part

    def changes(ref, top, pairs):
        rows, north, south = (pl.ds(top + k, 8) for k in (0, 1, -1))
        moved = []
        for p in pairs:
            h, u, m = ([ref[f, p, v, rows, :] for v in range(PARTS)] for f in range(3))
            moved.append(
                (h, u, m, from_right(h), from_left(h), from_right(u), from_left(u))
                + ([a - b for a, b in zip(from_right(m), from_left(m))],)
            )
        out = [([], [], []) for _ in pairs]
        for v in range(PARTS):
            k = [coef[i, v, rows, :] for i in range(COEFS)]
            for p, (h, u, m, hp, hm, up, um, md), fields in zip(pairs, moved, out):
                hn, un, mn = (ref[f, p, v, north, :] for f in range(3))
                hs, us, ms = (ref[f, p, v, south, :] for f in range(3))
                fields[0].append(
                    ((k[0] * up[v] + k[1] * um[v]) + (k[2] * hp[v] + k[3] * hm[v]))
                    + ((k[4] * mn + k[5] * ms) + (k[6] * hn + k[7] * hs))
                )
                fields[1].append(
                    (k[8] * (up[v] - um[v]) + k[9] * (un - us)) + ((k[10] * u[v] + k[11] * m[v]) - k[14] * (hp[v] - hm[v]))
                )
                fields[2].append((k[8] * md[v] + k[9] * (mn - ms)) + ((k[12] * u[v] + k[13] * m[v]) - k[14] * (hn - hs)))
        return out

    def sweep(low, high, body):
        def window(i, _):
            lax.fori_loop(0, QUADS // GROUP, lambda g, _: body(low + 8 * i, [g * GROUP + k for k in range(GROUP)]), None)

        lax.fori_loop(0, (high - low + 7) // 8, window, None)

    def first(top, pairs):
        for p, change in zip(pairs, changes(state, top, pairs)):
            for f in range(3):
                for v in range(PARTS):
                    middle[f, p, v, pl.ds(top, 8), :] = state[f, p, v, pl.ds(top, 8), :] + change[f][v]

    def second(top, pairs):
        for p, change in zip(pairs, changes(middle, top, pairs)):
            for f in range(3):
                for v in range(PARTS):
                    at = (f, p, v, pl.ds(top, 8), slice(None))
                    state[at] = 0.5 * ((state[at] + middle[at]) + change[f][v])

    def advance(step, _):
        low, high = 2 * step + 1, TALL - 2 * step - 1
        lax.fori_loop(low // 8, (high + 7) // 8, lambda tile, _: prepare(step, tile), None)
        sweep(low, high, first)
        sweep(low + 1, high - 1, second)

    lax.fori_loop(0, STEPS, advance, None)

    def deliver(f, _):
        for c in range(2):
            for quad in range(QUADS):
                rows = slice(HALO + c * 8, HALO + c * 8 + 8)
                parts = [state[f, quad, j, rows, :] for j in range(PARTS)]
                for quarter in range(4):
                    at = pl.ds(2 * quad + quarter // 2, 8, stride=8)
                    turn[c, quarter % 2, at, :] = gathered(parts, quarter, lane)
        for c in range(2):
            for high in range(2):
                for v in range(2):
                    lines = [turn[c, v, (high * 4 + low) * 8 : (high * 4 + low) * 8 + 8, :] for low in range(4)]
                    for x in range(4):
                        out = pltpu.roll(lines[0], 128 - 32 * x, 1) if x else lines[0]
                        for low in range(1, 4):
                            turned = pltpu.roll(lines[low], 32 * (low - x) % 128, 1) if low != x else lines[low]
                            out = jnp.where(lane >= 32 * low, turned, out)
                        out_ref[x * 2 + c, pl.ds(pl.multiple_of(f * 32 + (high * 2 + v) * 8, 8), 8), :] = out

    lax.fori_loop(0, 3, deliver, None)


def mix_kernel(coef_ref, cells_ref, out_ref, mixing):
    row = lax.broadcasted_iota(jnp.int32, (128, 128), 0)
    col = lax.broadcasted_iota(jnp.int32, (128, 128), 1)
    mixing[...] = jnp.where(row <= col, coef_ref[...], 0.0) + jnp.where(row == col, 1.0, 0.0)
    matrix = jnp.concatenate([mixing[pl.ds(t, 8, stride=16), :] for t in range(16)], axis=0)
    for k in range(6):
        cells = jnp.concatenate([cells_ref[p * 96 + k * 16 : p * 96 + k * 16 + 16, :] for p in range(8)], axis=0)
        out_ref[k * 128 : (k + 1) * 128, :] = lax.dot_general(
            cells, matrix, (((0,), (0,)), ((), ())), precision=lax.Precision.HIGHEST, preferred_element_type=f32
        )


VMEM = pl.BlockSpec(memory_space=pltpu.VMEM)
SMEM = pl.BlockSpec(memory_space=pltpu.SMEM)


def on_device(tangents, checkpoints, owner_order, land_mask, coefficients):
    block = lax.axis_index("y") * 2 + lax.axis_index("zh")
    core = lax.axis_index("c")
    raw = pl.pallas_call(
        flow_kernel,
        out_shape=jax.ShapeDtypeStruct((64, LANES), f32),
        in_specs=[SMEM, SMEM, VMEM, VMEM],
        out_specs=VMEM,
        compiler_params=pltpu.CompilerParams(vmem_limit_bytes=16 * 2**20),
    )(block.reshape(1).astype(jnp.int32), owner_order, checkpoints, land_mask)
    send = pl.pallas_call(
        pack_kernel,
        out_shape=jax.ShapeDtypeStruct((PEERS, 64, LANES), f32),
        in_specs=[VMEM, VMEM],
        out_specs=VMEM,
        compiler_params=pltpu.CompilerParams(vmem_limit_bytes=16 * 2**20),
    )(tangents, land_mask)
    up = [(i, i + 1) for i in range(7)]
    down = [(i + 1, i) for i in range(7)]
    chips = [lax.ppermute(raw, "zl", up), raw, lax.ppermute(raw, "zl", down)]
    flow = [x[:48] for x in chips]
    wet = [x[48:] for x in chips]

    def ring(chip):
        ends = [(s, (s + step) % 8, x) for s in range(8) for x, step in ((3, 1), (0, -1))]
        return [
            ((s * 4 + x) * 8 + z, (t * 4 + x) * 8 + z + chip) for s, t, x in ends for z in range(8) if 0 <= z + chip < 8
        ]

    halo = [lax.ppermute(raw[:48], ("y", "zh", "x", "zl"), ring(chip)) for chip in (1, 0, -1)]
    send, flow, halo = lax.optimization_barrier((send, flow, halo))
    own = lax.all_to_all(send, ("y", "zh", "c"), 0, 0, tiled=True)
    flow = jnp.concatenate([*flow, *halo], axis=0)
    flows = [lax.ppermute(flow, "x", [(i, (i + k) % 4) for i in range(4)]) for k in (1, 2, 3)]
    strip = jnp.concatenate([flow, *flows, *wet], axis=0)
    other = lax.ppermute(strip, "c", [(0, 1), (1, 0)])
    own, other = lax.optimization_barrier((own, other))
    parts = [lax.ppermute(own, "zl", up), own, lax.ppermute(own, "zl", down)]
    parts = [x.reshape(PEERS * 64, LANES) for x in parts]
    out = pl.pallas_call(
        march_kernel,
        out_shape=jax.ShapeDtypeStruct((8, 96, LANES), f32),
        in_specs=[SMEM] + [VMEM] * 5,
        out_specs=VMEM,
        scratch_shapes=[
            pltpu.VMEM((3, QUADS, PARTS, TALL + 8, LANES), f32),
            pltpu.VMEM((3, QUADS, PARTS, TALL + 8, LANES), f32),
            pltpu.VMEM((STEPS, 3, PARTS, TALL + 16, LANES), f32),
            pltpu.VMEM((PARTS, TALL, LANES), f32),
            pltpu.VMEM((COEFS, PARTS, TALL + 8, LANES), f32),
            pltpu.VMEM((2, 2, 64, LANES), f32),
        ],
        compiler_params=pltpu.CompilerParams(vmem_limit_bytes=32 * 2**20),
    )(jnp.stack([core, lax.axis_index("x")]).astype(jnp.int32), *parts, strip, other)
    cells = lax.all_to_all(out, ("x", "c"), 0, 0, tiled=True)
    mixed = pl.pallas_call(
        mix_kernel,
        out_shape=jax.ShapeDtypeStruct((768, 128), f32),
        in_specs=[VMEM, VMEM],
        out_specs=VMEM,
        scratch_shapes=[pltpu.VMEM((128, 128), f32)],
        compiler_params=pltpu.CompilerParams(vmem_limit_bytes=16 * 2**20),
    )(coefficients, cells.reshape(768, LANES))
    return mixed.reshape(3, 8, 32, 128).transpose(3, 0, 1, 2)


def solution(mesh):
    fine = jax.sharding.Mesh(mesh.devices.reshape(SIZES), AXES)
    mode, rows = ("y", "zh", "x"), ("zl", "c")
    placed = (
        P(mode, None, rows, None),
        P(None, None, rows, mode),
        P(),
        P(rows, None),
        P(),
    )
    return jax.shard_map(
        on_device, mesh=fine, in_specs=placed, out_specs=P(None, None, rows, mode), check_vma=False
    )
```

```python
import functools

import jax
import jax.numpy as jnp
from jax import lax
from jax.experimental import pallas as pl
from jax.experimental.pallas import tpu as pltpu
from jax.sharding import PartitionSpec as P

SIZES = (4, 2, 4, 8, 2)
AXES = ("y", "zh", "x", "zl", "c")
STEPS = 8
LANES = 128
HALO = 16
STRIP = 16
TALL = STRIP + 2 * HALO
PEERS = 16
COEFS = 15
QUADS = 4
GROUP = 4
f32 = jnp.float32


PARTS = 5


def halo_columns(left, right, lane):
    return jnp.where(lane >= 112, left, right)


def spread(inner, halo, part, lane):
    column = (lane % 32) * PARTS + (part - HALO)
    index = (column + LANES) % LANES
    a, b = (jnp.take_along_axis(x, index, axis=1) for x in (inner, halo))
    return jnp.where((column >= 0) & (column < LANES), a, b)


def gathered(parts, quarter, lane):
    column = lane + HALO
    index, rest = column // PARTS + quarter * 32, column % PARTS
    out = jnp.take_along_axis(parts[0], index, axis=1)
    for j in range(1, PARTS):
        out = jnp.where(rest == j, jnp.take_along_axis(parts[j], index, axis=1), out)
    return out


def from_right(cells):
    return [*cells[1:], pltpu.roll(cells[0], LANES - 1, 1)]


def from_left(cells):
    return [pltpu.roll(cells[-1], 1, 1), *cells[:-1]]


def flow_kernel(block_ref, order_ref, base_ref, mask_ref, raw_ref):
    lane = lax.broadcasted_iota(jnp.int32, (8, LANES), 1)
    s = block_ref[0]
    for high in range(2):
        for f in range(3):
            flow = jnp.concatenate([base_ref[order_ref[high * 4 + low], f] for low in range(4)], axis=1)
            raw_ref[(high * 3 + f) * 8 : (high * 3 + f) * 8 + 8, :] = flow

    def column(k):
        return mask_ref[:, pl.ds(pl.multiple_of(k * LANES, LANES), LANES)].astype(f32)

    raw_ref[48:56, :] = column(s)
    raw_ref[56:64, :] = halo_columns(column(lax.rem(s + 7, 8)), column(lax.rem(s + 1, 8)), lane)


def pack_kernel(tan_ref, mask_ref, send_ref):
    lane = lax.broadcasted_iota(jnp.int32, (8, LANES), 1)
    wet = [mask_ref[:, k * LANES : (k + 1) * LANES].astype(f32) for k in range(8)]

    def send(core, _):
        cells = [
            [[tan_ref[2 * core + q, f, :, k * LANES : (k + 1) * LANES] * wet[k] for k in range(8)] for f in range(3)]
            for q in range(2)
        ]
        for k in range(8):
            lines = []
            for f in range(3):
                for j in range(PARTS):
                    for q in range(2):
                        row = cells[q][f]
                        halo = halo_columns(row[(k + 7) % 8], row[(k + 1) % 8], lane)
                        lines.append(spread(row[k], halo, j, lane))
            lines += lines[:2]
            for i in range(8):
                a, b, c, d = lines[4 * i : 4 * i + 4]
                out = jnp.where(lane < 32, a, jnp.where(lane < 64, b, jnp.where(lane < 96, c, d)))
                send_ref[2 * k + core, i * 8 : i * 8 + 8, :] = out

    lax.fori_loop(0, 2, send, None)


def coef_kernel(core_ref, strip_ref, other_ref, coef, base, wet):
    lane = lax.broadcasted_iota(jnp.int32, (8, LANES), 1)
    core, me = core_ref[0], core_ref[1]
    blocks = [lax.rem(me - x + 4, 4) * 336 for x in range(4)]
    places = blocks + [blocks[3] + 64, blocks[0] + 64]
    strips = []
    for other, ref in enumerate((strip_ref, other_ref)):
        for z in range(3):
            top = pl.multiple_of((1 - core if other else core) * 8 + z * 16, 8)
            strips.append((ref, z * 112, top))
            at = z * 112 + 48
            for j in range(PARTS):
                wet[j, pl.ds(top, 8), :] = spread(ref[at : at + 8, :], ref[at + 8 : at + 16, :], j, lane) * 0.25

    def unpack(part, _):
        high, f = part // 3, part % 3
        for ref, first, top in strips:
            quads = [ref[pl.ds(pl.multiple_of(first + at + part * 8, 8), 8), :] for at in places]
            for low in range(4):
                out = pltpu.roll(quads[0], (128 - 32 * low) % 128, 1) if low else quads[0]
                for x in range(1, 4):
                    turned = pltpu.roll(quads[x], 32 * (x - low) % 128, 1) if x != low else quads[x]
                    out = jnp.where(lane >= 32 * x, turned, out)
                left = pltpu.roll(quads[4], (96 - 32 * low) % 128, 1)
                right = pltpu.roll(quads[5], (128 - 32 * low) % 128, 1)
                halo = halo_columns(left, right, lane)
                for j in range(PARTS):
                    base[high * 4 + low, f, j, pl.ds(top + 8, 8), :] = spread(out, halo, j, lane)

    lax.fori_loop(0, 6, unpack, None)

    def prepare(step, tile):
        top = pl.multiple_of(tile * 8, 8)
        w = [wet[v, pl.ds(top, 8), :] for v in range(PARTS)]

        def rows(f, shift):
            return [base[step, f, v, pl.ds(top + 8 + shift, 8), :] for v in range(PARTS)]

        depth = [x + 1.0 for x in rows(0, 0)]
        b, c = rows(1, 0), rows(2, 0)
        hp, hm = from_right(depth), from_left(depth)
        bp, bm = from_right(b), from_left(b)
        cp, cm = from_right(c), from_left(c)
        hn, hs = rows(0, 1), rows(0, -1)
        bn, bs = rows(1, 1), rows(1, -1)
        cn, cs = rows(2, 1), rows(2, -1)
        for v in range(PARTS):
            q = w[v]
            parts = (
                -q * hp[v], q * hm[v], -q * bp[v], q * bm[v],
                -q * (hn[v] + 1.0), q * (hs[v] + 1.0), -q * cn[v], q * cs[v],
                -q * b[v], -q * c[v],
                -q * (bp[v] - bm[v]), q * (1.0 - (bn[v] - bs[v])), -q * (1.0 + (cp[v] - cm[v])), -q * (cn[v] - cs[v]),
                q,
            )
            for k, part in enumerate(parts):
                coef[step, k, v, pl.ds(top, 8), :] = part

    def tiles(step, _):
        lax.fori_loop((2 * step + 1) // 8, (TALL - 2 * step + 6) // 8, lambda tile, _: prepare(step, tile), None)

    lax.fori_loop(0, STEPS, tiles, None)


def march_kernel(prev_ref, own_ref, next_ref, coef, out_ref, state, middle, turn):
    lane = lax.broadcasted_iota(jnp.int32, (8, LANES), 1)
    def place(quad, _):
        for z, ref in enumerate((prev_ref, own_ref, next_ref)):
            for c in range(2):
                for f in range(3):
                    for j in range(PARTS):
                        i, odd = divmod(f * PARTS + j, 2)
                        one, two = (
                            ref[pl.ds(pl.multiple_of((4 * quad + 2 * p + c) * 64 + i * 8, 8), 8), :] for p in range(2)
                        )
                        one, two = (pltpu.roll(one, 64, 1), two) if odd else (one, pltpu.roll(two, 64, 1))
                        rows = slice(z * 16 + c * 8, z * 16 + c * 8 + 8)
                        state[f, quad, j, rows, :] = jnp.where(lane < 64, one, two)

    lax.fori_loop(0, QUADS, place, None)
    def changes(ref, step, top, pairs):
        rows, north, south = (pl.ds(top + k, 8) for k in (0, 1, -1))
        moved = []
        for p in pairs:
            h, u, m = ([ref[f, p, v, rows, :] for v in range(PARTS)] for f in range(3))
            moved.append(
                (h, u, m, from_right(h), from_left(h), from_right(u), from_left(u))
                + ([a - b for a, b in zip(from_right(m), from_left(m))],)
            )
        out = [([], [], []) for _ in pairs]
        for v in range(PARTS):
            k = [coef[step, i, v, rows, :] for i in range(COEFS)]
            for p, (h, u, m, hp, hm, up, um, md), fields in zip(pairs, moved, out):
                hn, un, mn = (ref[f, p, v, north, :] for f in range(3))
                hs, us, ms = (ref[f, p, v, south, :] for f in range(3))
                fields[0].append(
                    ((k[0] * up[v] + k[1] * um[v]) + (k[2] * hp[v] + k[3] * hm[v]))
                    + ((k[4] * mn + k[5] * ms) + (k[6] * hn + k[7] * hs))
                )
                fields[1].append(
                    (k[8] * (up[v] - um[v]) + k[9] * (un - us)) + ((k[10] * u[v] + k[11] * m[v]) - k[14] * (hp[v] - hm[v]))
                )
                fields[2].append((k[8] * md[v] + k[9] * (mn - ms)) + ((k[12] * u[v] + k[13] * m[v]) - k[14] * (hn - hs)))
        return out

    def sweep(low, high, body):
        def window(i, _):
            lax.fori_loop(0, QUADS // GROUP, lambda g, _: body(low + 8 * i, [g * GROUP + k for k in range(GROUP)]), None)

        lax.fori_loop(0, (high - low + 7) // 8, window, None)

    def first(step, top, pairs):
        for p, change in zip(pairs, changes(state, step, top, pairs)):
            for f in range(3):
                for v in range(PARTS):
                    middle[f, p, v, pl.ds(top, 8), :] = state[f, p, v, pl.ds(top, 8), :] + change[f][v]

    def second(step, top, pairs):
        for p, change in zip(pairs, changes(middle, step, top, pairs)):
            for f in range(3):
                for v in range(PARTS):
                    at = (f, p, v, pl.ds(top, 8), slice(None))
                    state[at] = 0.5 * ((state[at] + middle[at]) + change[f][v])

    def advance(step, _):
        low, high = 2 * step + 1, TALL - 2 * step - 1
        sweep(low, high, functools.partial(first, step))
        sweep(low + 1, high - 1, functools.partial(second, step))

    lax.fori_loop(0, STEPS, advance, None)

    def deliver(f, _):
        for c in range(2):
            for quad in range(QUADS):
                rows = slice(HALO + c * 8, HALO + c * 8 + 8)
                parts = [state[f, quad, j, rows, :] for j in range(PARTS)]
                for quarter in range(4):
                    at = pl.ds(2 * quad + quarter // 2, 8, stride=8)
                    turn[c, quarter % 2, at, :] = gathered(parts, quarter, lane)
        for c in range(2):
            for high in range(2):
                for v in range(2):
                    lines = [turn[c, v, (high * 4 + low) * 8 : (high * 4 + low) * 8 + 8, :] for low in range(4)]
                    for x in range(4):
                        out = pltpu.roll(lines[0], 128 - 32 * x, 1) if x else lines[0]
                        for low in range(1, 4):
                            turned = pltpu.roll(lines[low], 32 * (low - x) % 128, 1) if low != x else lines[low]
                            out = jnp.where(lane >= 32 * low, turned, out)
                        out_ref[x * 2 + c, pl.ds(pl.multiple_of(f * 32 + (high * 2 + v) * 8, 8), 8), :] = out

    lax.fori_loop(0, 3, deliver, None)


def mix_kernel(coef_ref, cells_ref, out_ref, mixing):
    row = lax.broadcasted_iota(jnp.int32, (128, 128), 0)
    col = lax.broadcasted_iota(jnp.int32, (128, 128), 1)
    mixing[...] = jnp.where(row <= col, coef_ref[...], 0.0) + jnp.where(row == col, 1.0, 0.0)
    matrix = jnp.concatenate([mixing[pl.ds(t, 8, stride=16), :] for t in range(16)], axis=0)
    for k in range(6):
        cells = jnp.concatenate([cells_ref[p * 96 + k * 16 : p * 96 + k * 16 + 16, :] for p in range(8)], axis=0)
        out_ref[k * 128 : (k + 1) * 128, :] = lax.dot_general(
            cells, matrix, (((0,), (0,)), ((), ())), precision=lax.Precision.HIGHEST, preferred_element_type=f32
        )


VMEM = pl.BlockSpec(memory_space=pltpu.VMEM)
SMEM = pl.BlockSpec(memory_space=pltpu.SMEM)


def on_device(tangents, checkpoints, owner_order, land_mask, coefficients):
    block = lax.axis_index("y") * 2 + lax.axis_index("zh")
    core = lax.axis_index("c")
    raw = pl.pallas_call(
        flow_kernel,
        out_shape=jax.ShapeDtypeStruct((64, LANES), f32),
        in_specs=[SMEM, SMEM, VMEM, VMEM],
        out_specs=VMEM,
        compiler_params=pltpu.CompilerParams(vmem_limit_bytes=16 * 2**20),
    )(block.reshape(1).astype(jnp.int32), owner_order, checkpoints, land_mask)
    up = [(i, i + 1) for i in range(7)]
    down = [(i + 1, i) for i in range(7)]
    ring = [(s * 4 + x, (s + step) % 8 * 4 + x) for s in range(8) for x, step in ((3, 1), (0, -1))]
    halo = lax.ppermute(raw[:48], ("y", "zh", "x"), ring)
    wide = jnp.concatenate([raw, halo], axis=0)
    above, below = lax.ppermute(wide, "zl", up), lax.ppermute(wide, "zl", down)
    send = pl.pallas_call(
        pack_kernel,
        out_shape=jax.ShapeDtypeStruct((PEERS, 64, LANES), f32),
        in_specs=[VMEM, VMEM],
        out_specs=VMEM,
        compiler_params=pltpu.CompilerParams(vmem_limit_bytes=16 * 2**20),
    )(tangents, land_mask)
    send, above, below = lax.optimization_barrier((send, above, below))
    own = lax.all_to_all(send, ("y", "zh", "c"), 0, 0, tiled=True)
    chips = jnp.concatenate([above, wide, below], axis=0)
    strip = jnp.concatenate(
        [chips] + [lax.ppermute(chips, "x", [(i, (i + k) % 4) for i in range(4)]) for k in (1, 2, 3)], axis=0
    )
    other = lax.ppermute(strip, "c", [(0, 1), (1, 0)])
    own, strip, other = lax.optimization_barrier((own, strip, other))
    coef = pl.pallas_call(
        coef_kernel,
        out_shape=jax.ShapeDtypeStruct((STEPS, COEFS, PARTS, TALL + 8, LANES), f32),
        in_specs=[SMEM, VMEM, VMEM],
        out_specs=VMEM,
        scratch_shapes=[
            pltpu.VMEM((STEPS, 3, PARTS, TALL + 16, LANES), f32),
            pltpu.VMEM((PARTS, TALL, LANES), f32),
        ],
        compiler_params=pltpu.CompilerParams(vmem_limit_bytes=32 * 2**20),
        cost_estimate=pl.CostEstimate(flops=2 * 10**9, bytes_accessed=50 * 10**6, transcendentals=0),
    )(jnp.stack([core, lax.axis_index("x")]).astype(jnp.int32), strip, other)
    parts = [lax.ppermute(own, "zl", up), own, lax.ppermute(own, "zl", down)]
    parts = [x.reshape(PEERS * 64, LANES) for x in parts]
    out = pl.pallas_call(
        march_kernel,
        out_shape=jax.ShapeDtypeStruct((8, 96, LANES), f32),
        in_specs=[VMEM] * 4,
        out_specs=VMEM,
        scratch_shapes=[
            pltpu.VMEM((3, QUADS, PARTS, TALL + 8, LANES), f32),
            pltpu.VMEM((3, QUADS, PARTS, TALL + 8, LANES), f32),
            pltpu.VMEM((2, 2, 64, LANES), f32),
        ],
        compiler_params=pltpu.CompilerParams(vmem_limit_bytes=26 * 2**20),
    )(*parts, coef)
    cells = lax.all_to_all(out, ("x", "c"), 0, 0, tiled=True)
    mixed = pl.pallas_call(
        mix_kernel,
        out_shape=jax.ShapeDtypeStruct((768, 128), f32),
        in_specs=[VMEM, VMEM],
        out_specs=VMEM,
        scratch_shapes=[pltpu.VMEM((128, 128), f32)],
        compiler_params=pltpu.CompilerParams(vmem_limit_bytes=16 * 2**20),
    )(coefficients, cells.reshape(768, LANES))
    return mixed.reshape(3, 8, 32, 128).transpose(3, 0, 1, 2)


def solution(mesh):
    fine = jax.sharding.Mesh(mesh.devices.reshape(SIZES), AXES)
    mode, rows = ("y", "zh", "x"), ("zl", "c")
    placed = (
        P(mode, None, rows, None),
        P(None, None, rows, mode),
        P(),
        P(rows, None),
        P(),
    )
    return jax.shard_map(
        on_device, mesh=fine, in_specs=placed, out_specs=P(None, None, rows, mode), check_vma=False
    )
```

```python
import functools

import jax
import jax.numpy as jnp
from jax import lax
from jax.experimental import pallas as pl
from jax.experimental.pallas import tpu as pltpu
from jax.sharding import PartitionSpec as P

SIZES = (4, 2, 4, 8, 2)
AXES = ("y", "zh", "x", "zl", "c")
STEPS = 8
LANES = 128
HALO = 16
STRIP = 16
TALL = STRIP + 2 * HALO
PEERS = 16
COEFS = 15
QUADS = 4
GROUP = 4
f32 = jnp.float32


PARTS = 5


def halo_columns(left, right, lane):
    return jnp.where(lane >= 112, left, right)


def spread(inner, halo, part, lane):
    column = (lane % 32) * PARTS + (part - HALO)
    index = (column + LANES) % LANES
    a, b = (jnp.take_along_axis(x, index, axis=1) for x in (inner, halo))
    return jnp.where((column >= 0) & (column < LANES), a, b)


def gathered(parts, quarter, lane):
    column = lane + HALO
    index, rest = column // PARTS + quarter * 32, column % PARTS
    out = jnp.take_along_axis(parts[0], index, axis=1)
    for j in range(1, PARTS):
        out = jnp.where(rest == j, jnp.take_along_axis(parts[j], index, axis=1), out)
    return out


def from_right(cells):
    return [*cells[1:], pltpu.roll(cells[0], LANES - 1, 1)]


def from_left(cells):
    return [pltpu.roll(cells[-1], 1, 1), *cells[:-1]]


def flow_kernel(block_ref, order_ref, base_ref, mask_ref, raw_ref):
    lane = lax.broadcasted_iota(jnp.int32, (8, LANES), 1)
    s = block_ref[0]
    for high in range(2):
        for f in range(3):
            flow = jnp.concatenate([base_ref[order_ref[high * 4 + low], f] for low in range(4)], axis=1)
            raw_ref[(high * 3 + f) * 8 : (high * 3 + f) * 8 + 8, :] = flow

    def column(k):
        return mask_ref[:, pl.ds(pl.multiple_of(k * LANES, LANES), LANES)].astype(f32)

    raw_ref[48:56, :] = column(s)
    raw_ref[56:64, :] = halo_columns(column(lax.rem(s + 7, 8)), column(lax.rem(s + 1, 8)), lane)


def pack_kernel(tan_ref, mask_ref, send_ref):
    lane = lax.broadcasted_iota(jnp.int32, (8, LANES), 1)
    wet = [mask_ref[:, k * LANES : (k + 1) * LANES].astype(f32) for k in range(8)]

    def send(core, _):
        cells = [
            [[tan_ref[2 * core + q, f, :, k * LANES : (k + 1) * LANES] * wet[k] for k in range(8)] for f in range(3)]
            for q in range(2)
        ]
        for k in range(8):
            lines = []
            for f in range(3):
                for j in range(PARTS):
                    for q in range(2):
                        row = cells[q][f]
                        halo = halo_columns(row[(k + 7) % 8], row[(k + 1) % 8], lane)
                        lines.append(spread(row[k], halo, j, lane))
            lines += lines[:2]
            for i in range(8):
                a, b, c, d = lines[4 * i : 4 * i + 4]
                out = jnp.where(lane < 32, a, jnp.where(lane < 64, b, jnp.where(lane < 96, c, d)))
                send_ref[2 * k + core, i * 8 : i * 8 + 8, :] = out

    lax.fori_loop(0, 2, send, None)


def coef_kernel(core_ref, strip_ref, other_ref, coef, base, wet):
    lane = lax.broadcasted_iota(jnp.int32, (8, LANES), 1)
    core, me = core_ref[0], core_ref[1]
    blocks = [lax.rem(me - x + 4, 4) * 336 for x in range(4)]
    places = blocks + [blocks[3] + 64, blocks[0] + 64]
    strips = []
    for other, ref in enumerate((strip_ref, other_ref)):
        for z in range(3):
            top = pl.multiple_of((1 - core if other else core) * 8 + z * 16, 8)
            strips.append((ref, z * 112, top))
            at = z * 112 + 48
            for j in range(PARTS):
                wet[j, pl.ds(top, 8), :] = spread(ref[at : at + 8, :], ref[at + 8 : at + 16, :], j, lane) * 0.25

    def unpack(part, _):
        high, f = part // 3, part % 3
        for ref, first, top in strips:
            quads = [ref[pl.ds(pl.multiple_of(first + at + part * 8, 8), 8), :] for at in places]
            for low in range(4):
                out = pltpu.roll(quads[0], (128 - 32 * low) % 128, 1) if low else quads[0]
                for x in range(1, 4):
                    turned = pltpu.roll(quads[x], 32 * (x - low) % 128, 1) if x != low else quads[x]
                    out = jnp.where(lane >= 32 * x, turned, out)
                left = pltpu.roll(quads[4], (96 - 32 * low) % 128, 1)
                right = pltpu.roll(quads[5], (128 - 32 * low) % 128, 1)
                halo = halo_columns(left, right, lane)
                for j in range(PARTS):
                    base[high * 4 + low, f, j, pl.ds(top + 8, 8), :] = spread(out, halo, j, lane)

    lax.fori_loop(0, 6, unpack, None)

    def prepare(step, tile):
        top = pl.multiple_of(tile * 8, 8)
        w = [wet[v, pl.ds(top, 8), :] for v in range(PARTS)]

        def rows(f, shift):
            return [base[step, f, v, pl.ds(top + 8 + shift, 8), :] for v in range(PARTS)]

        depth = [x + 1.0 for x in rows(0, 0)]
        b, c = rows(1, 0), rows(2, 0)
        hp, hm = from_right(depth), from_left(depth)
        bp, bm = from_right(b), from_left(b)
        cp, cm = from_right(c), from_left(c)
        hn, hs = rows(0, 1), rows(0, -1)
        bn, bs = rows(1, 1), rows(1, -1)
        cn, cs = rows(2, 1), rows(2, -1)
        for v in range(PARTS):
            q = w[v]
            parts = (
                -q * hp[v], q * hm[v], -q * bp[v], q * bm[v],
                -q * (hn[v] + 1.0), q * (hs[v] + 1.0), -q * cn[v], q * cs[v],
                -q * b[v], -q * c[v],
                -q * (bp[v] - bm[v]), q * (1.0 - (bn[v] - bs[v])), -q * (1.0 + (cp[v] - cm[v])), -q * (cn[v] - cs[v]),
                q,
            )
            for k, part in enumerate(parts):
                coef[step, k, v, pl.ds(top, 8), :] = part

    def tiles(step, _):
        lax.fori_loop((2 * step + 1) // 8, (TALL - 2 * step + 6) // 8, lambda tile, _: prepare(step, tile), None)

    lax.fori_loop(0, STEPS, tiles, None)


def march_kernel(prev_ref, own_ref, next_ref, coef, out_ref, state, middle, turn):
    lane = lax.broadcasted_iota(jnp.int32, (8, LANES), 1)
    def place(quad, _):
        for z, ref in enumerate((prev_ref, own_ref, next_ref)):
            for c in range(2):
                for f in range(3):
                    for j in range(PARTS):
                        i, odd = divmod(f * PARTS + j, 2)
                        one, two = (
                            ref[pl.ds(pl.multiple_of((4 * quad + 2 * p + c) * 64 + i * 8, 8), 8), :] for p in range(2)
                        )
                        one, two = (pltpu.roll(one, 64, 1), two) if odd else (one, pltpu.roll(two, 64, 1))
                        rows = slice(z * 16 + c * 8, z * 16 + c * 8 + 8)
                        state[f, quad, j, rows, :] = jnp.where(lane < 64, one, two)

    lax.fori_loop(0, QUADS, place, None)
    def changes(ref, step, top, pairs):
        rows, north, south = (pl.ds(top + k, 8) for k in (0, 1, -1))
        moved = []
        for p in pairs:
            h, u, m = ([ref[f, p, v, rows, :] for v in range(PARTS)] for f in range(3))
            moved.append(
                (h, u, m, from_right(h), from_left(h), from_right(u), from_left(u))
                + ([a - b for a, b in zip(from_right(m), from_left(m))],)
            )
        out = [([], [], []) for _ in pairs]
        for v in range(PARTS):
            k = [coef[step, i, v, rows, :] for i in range(COEFS)]
            for p, (h, u, m, hp, hm, up, um, md), fields in zip(pairs, moved, out):
                hn, un, mn = (ref[f, p, v, north, :] for f in range(3))
                hs, us, ms = (ref[f, p, v, south, :] for f in range(3))
                fields[0].append(
                    ((k[0] * up[v] + k[1] * um[v]) + (k[2] * hp[v] + k[3] * hm[v]))
                    + ((k[4] * mn + k[5] * ms) + (k[6] * hn + k[7] * hs))
                )
                fields[1].append(
                    (k[8] * (up[v] - um[v]) + k[9] * (un - us)) + ((k[10] * u[v] + k[11] * m[v]) - k[14] * (hp[v] - hm[v]))
                )
                fields[2].append((k[8] * md[v] + k[9] * (mn - ms)) + ((k[12] * u[v] + k[13] * m[v]) - k[14] * (hn - hs)))
        return out

    def sweep(low, high, body):
        def window(i, _):
            lax.fori_loop(0, QUADS // GROUP, lambda g, _: body(low + 8 * i, [g * GROUP + k for k in range(GROUP)]), None)

        lax.fori_loop(0, (high - low + 7) // 8, window, None)

    def first(step, top, pairs):
        for p, change in zip(pairs, changes(state, step, top, pairs)):
            for f in range(3):
                for v in range(PARTS):
                    middle[f, p, v, pl.ds(top, 8), :] = state[f, p, v, pl.ds(top, 8), :] + change[f][v]

    def second(step, top, pairs):
        for p, change in zip(pairs, changes(middle, step, top, pairs)):
            for f in range(3):
                for v in range(PARTS):
                    at = (f, p, v, pl.ds(top, 8), slice(None))
                    state[at] = 0.5 * ((state[at] + middle[at]) + change[f][v])

    def advance(step, _):
        low, high = 2 * step + 1, TALL - 2 * step - 1
        sweep(low, high, functools.partial(first, step))
        sweep(low + 1, high - 1, functools.partial(second, step))

    lax.fori_loop(0, STEPS, advance, None)

    def deliver(f, _):
        for c in range(2):
            for quad in range(QUADS):
                rows = slice(HALO + c * 8, HALO + c * 8 + 8)
                parts = [state[f, quad, j, rows, :] for j in range(PARTS)]
                for quarter in range(4):
                    at = pl.ds(2 * quad + quarter // 2, 8, stride=8)
                    turn[c, quarter % 2, at, :] = gathered(parts, quarter, lane)
        for c in range(2):
            for high in range(2):
                for v in range(2):
                    lines = [turn[c, v, (high * 4 + low) * 8 : (high * 4 + low) * 8 + 8, :] for low in range(4)]
                    for x in range(4):
                        out = pltpu.roll(lines[0], 128 - 32 * x, 1) if x else lines[0]
                        for low in range(1, 4):
                            turned = pltpu.roll(lines[low], 32 * (low - x) % 128, 1) if low != x else lines[low]
                            out = jnp.where(lane >= 32 * low, turned, out)
                        out_ref[x * 2 + c, pl.ds(pl.multiple_of(f * 32 + (high * 2 + v) * 8, 8), 8), :] = out

    lax.fori_loop(0, 3, deliver, None)


def mix_kernel(coef_ref, cells_ref, out_ref, mixing):
    row = lax.broadcasted_iota(jnp.int32, (128, 128), 0)
    col = lax.broadcasted_iota(jnp.int32, (128, 128), 1)
    mixing[...] = jnp.where(row <= col, coef_ref[...], 0.0) + jnp.where(row == col, 1.0, 0.0)
    matrix = jnp.concatenate([mixing[pl.ds(t, 8, stride=16), :] for t in range(16)], axis=0)
    for k in range(6):
        cells = jnp.concatenate([cells_ref[p * 96 + k * 16 : p * 96 + k * 16 + 16, :] for p in range(8)], axis=0)
        out_ref[k * 128 : (k + 1) * 128, :] = lax.dot_general(
            cells, matrix, (((0,), (0,)), ((), ())), precision=lax.Precision.HIGHEST, preferred_element_type=f32
        )


VMEM = pl.BlockSpec(memory_space=pltpu.VMEM)
SMEM = pl.BlockSpec(memory_space=pltpu.SMEM)


def on_device(tangents, checkpoints, owner_order, land_mask, coefficients):
    block = lax.axis_index("y") * 2 + lax.axis_index("zh")
    core = lax.axis_index("c")
    raw = pl.pallas_call(
        flow_kernel,
        out_shape=jax.ShapeDtypeStruct((64, LANES), f32),
        in_specs=[SMEM, SMEM, VMEM, VMEM],
        out_specs=VMEM,
        compiler_params=pltpu.CompilerParams(vmem_limit_bytes=16 * 2**20),
    )(block.reshape(1).astype(jnp.int32), owner_order, checkpoints, land_mask)
    up = [(i, i + 1) for i in range(7)]
    down = [(i + 1, i) for i in range(7)]
    ring = [(s * 4 + x, (s + step) % 8 * 4 + x) for s in range(8) for x, step in ((3, 1), (0, -1))]
    halo = lax.ppermute(raw[:48], ("y", "zh", "x"), ring)
    wide = jnp.concatenate([raw, halo], axis=0)
    above, below = lax.ppermute(wide, "zl", up), lax.ppermute(wide, "zl", down)
    send = pl.pallas_call(
        pack_kernel,
        out_shape=jax.ShapeDtypeStruct((PEERS, 64, LANES), f32),
        in_specs=[VMEM, VMEM],
        out_specs=VMEM,
        compiler_params=pltpu.CompilerParams(vmem_limit_bytes=16 * 2**20),
    )(tangents, land_mask)
    send, above, below = lax.optimization_barrier((send, above, below))
    own = lax.all_to_all(send, ("y", "zh", "c"), 0, 0, tiled=True)
    chips = jnp.concatenate([above, wide, below], axis=0)
    strip = jnp.concatenate(
        [chips] + [lax.ppermute(chips, "x", [(i, (i + k) % 4) for i in range(4)]) for k in (1, 2, 3)], axis=0
    )
    other = lax.ppermute(strip, "c", [(0, 1), (1, 0)])
    coef = pl.pallas_call(
        coef_kernel,
        out_shape=jax.ShapeDtypeStruct((STEPS, COEFS, PARTS, TALL + 8, LANES), f32),
        in_specs=[SMEM, VMEM, VMEM],
        out_specs=VMEM,
        scratch_shapes=[
            pltpu.VMEM((STEPS, 3, PARTS, TALL + 16, LANES), f32),
            pltpu.VMEM((PARTS, TALL, LANES), f32),
        ],
        compiler_params=pltpu.CompilerParams(vmem_limit_bytes=32 * 2**20),
        cost_estimate=pl.CostEstimate(flops=2 * 10**9, bytes_accessed=50 * 10**6, transcendentals=0),
    )(jnp.stack([core, lax.axis_index("x")]).astype(jnp.int32), strip, other)
    own, coef = lax.optimization_barrier((own, coef))
    parts = [lax.ppermute(own, "zl", up), own, lax.ppermute(own, "zl", down)]
    parts = [x.reshape(PEERS * 64, LANES) for x in parts]
    out = pl.pallas_call(
        march_kernel,
        out_shape=jax.ShapeDtypeStruct((8, 96, LANES), f32),
        in_specs=[VMEM] * 4,
        out_specs=VMEM,
        scratch_shapes=[
            pltpu.VMEM((3, QUADS, PARTS, TALL + 8, LANES), f32),
            pltpu.VMEM((3, QUADS, PARTS, TALL + 8, LANES), f32),
            pltpu.VMEM((2, 2, 64, LANES), f32),
        ],
        compiler_params=pltpu.CompilerParams(vmem_limit_bytes=26 * 2**20),
    )(*parts, coef)
    cells = lax.all_to_all(out, ("x", "c"), 0, 0, tiled=True)
    mixed = pl.pallas_call(
        mix_kernel,
        out_shape=jax.ShapeDtypeStruct((768, 128), f32),
        in_specs=[VMEM, VMEM],
        out_specs=VMEM,
        scratch_shapes=[pltpu.VMEM((128, 128), f32)],
        compiler_params=pltpu.CompilerParams(vmem_limit_bytes=16 * 2**20),
    )(coefficients, cells.reshape(768, LANES))
    return mixed.reshape(3, 8, 32, 128).transpose(3, 0, 1, 2)


def solution(mesh):
    fine = jax.sharding.Mesh(mesh.devices.reshape(SIZES), AXES)
    mode, rows = ("y", "zh", "x"), ("zl", "c")
    placed = (
        P(mode, None, rows, None),
        P(None, None, rows, mode),
        P(),
        P(rows, None),
        P(),
    )
    return jax.shard_map(
        on_device, mesh=fine, in_specs=placed, out_specs=P(None, None, rows, mode), check_vma=False
    )
```

```python
import functools

import jax
import jax.numpy as jnp
from jax import lax
from jax.experimental import pallas as pl
from jax.experimental.pallas import tpu as pltpu
from jax.sharding import PartitionSpec as P

SIZES = (4, 2, 4, 8, 2)
AXES = ("y", "zh", "x", "zl", "c")
STEPS = 8
LANES = 128
HALO = 16
STRIP = 16
TALL = STRIP + 2 * HALO
PEERS = 16
COEFS = 15
QUADS = 4
GROUP = 4
f32 = jnp.float32


PARTS = 5


def halo_columns(left, right, lane):
    return jnp.where(lane >= 112, left, right)


def spread(inner, halo, part, lane):
    column = (lane % 32) * PARTS + (part - HALO)
    index = (column + LANES) % LANES
    a, b = (jnp.take_along_axis(x, index, axis=1) for x in (inner, halo))
    return jnp.where((column >= 0) & (column < LANES), a, b)


def gathered(parts, quarter, lane):
    column = lane + HALO
    index, rest = column // PARTS + quarter * 32, column % PARTS
    out = jnp.take_along_axis(parts[0], index, axis=1)
    for j in range(1, PARTS):
        out = jnp.where(rest == j, jnp.take_along_axis(parts[j], index, axis=1), out)
    return out


def from_right(cells):
    return [*cells[1:], pltpu.roll(cells[0], LANES - 1, 1)]


def from_left(cells):
    return [pltpu.roll(cells[-1], 1, 1), *cells[:-1]]


def flow_kernel(block_ref, order_ref, base_ref, mask_ref, raw_ref):
    lane = lax.broadcasted_iota(jnp.int32, (8, LANES), 1)
    s = block_ref[0]
    for high in range(2):
        for f in range(3):
            flow = jnp.concatenate([base_ref[order_ref[high * 4 + low], f] for low in range(4)], axis=1)
            raw_ref[(high * 3 + f) * 8 : (high * 3 + f) * 8 + 8, :] = flow

    def column(k):
        return mask_ref[:, pl.ds(pl.multiple_of(k * LANES, LANES), LANES)].astype(f32)

    raw_ref[48:56, :] = column(s)
    raw_ref[56:64, :] = halo_columns(column(lax.rem(s + 7, 8)), column(lax.rem(s + 1, 8)), lane)


def pack_kernel(tan_ref, mask_ref, send_ref):
    lane = lax.broadcasted_iota(jnp.int32, (8, LANES), 1)
    wet = [mask_ref[:, k * LANES : (k + 1) * LANES].astype(f32) for k in range(8)]

    def send(core, _):
        cells = [
            [[tan_ref[2 * core + q, f, :, k * LANES : (k + 1) * LANES] * wet[k] for k in range(8)] for f in range(3)]
            for q in range(2)
        ]
        for k in range(8):
            lines = []
            for f in range(3):
                for j in range(PARTS):
                    for q in range(2):
                        row = cells[q][f]
                        halo = halo_columns(row[(k + 7) % 8], row[(k + 1) % 8], lane)
                        lines.append(spread(row[k], halo, j, lane))
            lines += lines[:2]
            for i in range(8):
                a, b, c, d = lines[4 * i : 4 * i + 4]
                out = jnp.where(lane < 32, a, jnp.where(lane < 64, b, jnp.where(lane < 96, c, d)))
                send_ref[2 * k + core, i * 8 : i * 8 + 8, :] = out

    lax.fori_loop(0, 2, send, None)


def coef_kernel(core_ref, strip_ref, other_ref, coef, base, lines, spread_matrix):
    lane = lax.broadcasted_iota(jnp.int32, (8, LANES), 1)
    core, me = core_ref[0], core_ref[1]
    blocks = [lax.rem(me - x + 4, 4) * 336 for x in range(4)]
    places = blocks + [blocks[3] + 64, blocks[0] + 64]
    strips = []
    for other, ref in enumerate((strip_ref, other_ref)):
        for z in range(3):
            top = pl.multiple_of((1 - core if other else core) * 8 + z * 16, 8)
            strips.append((ref, z * 112, top))
            at = z * 112 + 48
            lines[STEPS, pl.ds(top, 8), :LANES] = ref[at : at + 8, :]
            lines[STEPS, pl.ds(top, 8), LANES:] = ref[at + 8 : at + 16, :]

    def unpack(part, _):
        high, f = part // 3, part % 3
        for ref, first, top in strips:
            quads = [ref[pl.ds(pl.multiple_of(first + at + part * 8, 8), 8), :] for at in places]
            for low in range(4):
                out = pltpu.roll(quads[0], (128 - 32 * low) % 128, 1) if low else quads[0]
                for x in range(1, 4):
                    turned = pltpu.roll(quads[x], 32 * (x - low) % 128, 1) if x != low else quads[x]
                    out = jnp.where(lane >= 32 * x, turned, out)
                left = pltpu.roll(quads[4], (96 - 32 * low) % 128, 1)
                right = pltpu.roll(quads[5], (128 - 32 * low) % 128, 1)
                halo = halo_columns(left, right, lane)
                rows = pl.ds(pl.multiple_of(f * TALL + top, 8), 8)
                lines[high * 4 + low, rows, :LANES] = out
                lines[high * 4 + low, rows, LANES:] = halo

    lax.fori_loop(0, 6, unpack, None)

    place = lax.broadcasted_iota(jnp.int32, (2 * LANES, LANES), 0)
    column = jnp.where(place < LANES, place, jnp.where(place < LANES + 16, place, place - 2 * LANES))
    target = lax.broadcasted_iota(jnp.int32, (2 * LANES, LANES), 1) % 32 * PARTS - HALO
    for j in range(PARTS):
        spread_matrix[:, j * LANES : (j + 1) * LANES] = (column == target + j).astype(jnp.bfloat16)

    def spread_lines(step, _):
        cells = lines[step]
        high = cells.astype(jnp.bfloat16)
        rest = cells - high.astype(f32)
        mid = rest.astype(jnp.bfloat16)
        low = (rest - mid.astype(f32)).astype(jnp.bfloat16)
        out = [jnp.dot(x, spread_matrix[...], preferred_element_type=f32) for x in (high, mid, low)]
        out = (out[0] + out[1]) + out[2]
        for j in range(PARTS):
            for f in range(3):
                part = out[f * TALL : (f + 1) * TALL, j * LANES : (j + 1) * LANES]
                base[step, f, j, 8 : TALL + 8, :] = part
        return _

    lax.fori_loop(0, STEPS + 1, spread_lines, None)

    def prepare(step, tile):
        top = pl.multiple_of(tile * 8, 8)
        w = [base[STEPS, 0, v, pl.ds(top + 8, 8), :] * 0.25 for v in range(PARTS)]

        def rows(f, shift):
            return [base[step, f, v, pl.ds(top + 8 + shift, 8), :] for v in range(PARTS)]

        depth = [x + 1.0 for x in rows(0, 0)]
        b, c = rows(1, 0), rows(2, 0)
        hp, hm = from_right(depth), from_left(depth)
        bp, bm = from_right(b), from_left(b)
        cp, cm = from_right(c), from_left(c)
        hn, hs = rows(0, 1), rows(0, -1)
        bn, bs = rows(1, 1), rows(1, -1)
        cn, cs = rows(2, 1), rows(2, -1)
        for v in range(PARTS):
            q = w[v]
            parts = (
                -q * hp[v], q * hm[v], -q * bp[v], q * bm[v],
                -q * (hn[v] + 1.0), q * (hs[v] + 1.0), -q * cn[v], q * cs[v],
                -q * b[v], -q * c[v],
                -q * (bp[v] - bm[v]), q * (1.0 - (bn[v] - bs[v])), -q * (1.0 + (cp[v] - cm[v])), -q * (cn[v] - cs[v]),
                q,
            )
            for k, part in enumerate(parts):
                coef[step, k, v, pl.ds(top, 8), :] = part

    def tiles(step, _):
        lax.fori_loop((2 * step + 1) // 8, (TALL - 2 * step + 6) // 8, lambda tile, _: prepare(step, tile), None)

    lax.fori_loop(0, STEPS, tiles, None)


def march_kernel(prev_ref, own_ref, next_ref, coef, out_ref, state, middle, turn):
    lane = lax.broadcasted_iota(jnp.int32, (8, LANES), 1)
    def place(quad, _):
        for z, ref in enumerate((prev_ref, own_ref, next_ref)):
            for c in range(2):
                for f in range(3):
                    for j in range(PARTS):
                        i, odd = divmod(f * PARTS + j, 2)
                        one, two = (
                            ref[pl.ds(pl.multiple_of((4 * quad + 2 * p + c) * 64 + i * 8, 8), 8), :] for p in range(2)
                        )
                        one, two = (pltpu.roll(one, 64, 1), two) if odd else (one, pltpu.roll(two, 64, 1))
                        rows = slice(z * 16 + c * 8, z * 16 + c * 8 + 8)
                        state[f, quad, j, rows, :] = jnp.where(lane < 64, one, two)

    lax.fori_loop(0, QUADS, place, None)
    def changes(ref, step, top, pairs):
        rows, north, south = (pl.ds(top + k, 8) for k in (0, 1, -1))
        moved = []
        for p in pairs:
            h, u, m = ([ref[f, p, v, rows, :] for v in range(PARTS)] for f in range(3))
            moved.append(
                (h, u, m, from_right(h), from_left(h), from_right(u), from_left(u))
                + ([a - b for a, b in zip(from_right(m), from_left(m))],)
            )
        out = [([], [], []) for _ in pairs]
        for v in range(PARTS):
            k = [coef[step, i, v, rows, :] for i in range(COEFS)]
            for p, (h, u, m, hp, hm, up, um, md), fields in zip(pairs, moved, out):
                hn, un, mn = (ref[f, p, v, north, :] for f in range(3))
                hs, us, ms = (ref[f, p, v, south, :] for f in range(3))
                fields[0].append(
                    ((k[0] * up[v] + k[1] * um[v]) + (k[2] * hp[v] + k[3] * hm[v]))
                    + ((k[4] * mn + k[5] * ms) + (k[6] * hn + k[7] * hs))
                )
                fields[1].append(
                    (k[8] * (up[v] - um[v]) + k[9] * (un - us)) + ((k[10] * u[v] + k[11] * m[v]) - k[14] * (hp[v] - hm[v]))
                )
                fields[2].append((k[8] * md[v] + k[9] * (mn - ms)) + ((k[12] * u[v] + k[13] * m[v]) - k[14] * (hn - hs)))
        return out

    def sweep(low, high, body):
        def window(i, _):
            lax.fori_loop(0, QUADS // GROUP, lambda g, _: body(low + 8 * i, [g * GROUP + k for k in range(GROUP)]), None)

        lax.fori_loop(0, (high - low + 7) // 8, window, None)

    def first(step, top, pairs):
        for p, change in zip(pairs, changes(state, step, top, pairs)):
            for f in range(3):
                for v in range(PARTS):
                    middle[f, p, v, pl.ds(top, 8), :] = state[f, p, v, pl.ds(top, 8), :] + change[f][v]

    def second(step, top, pairs):
        for p, change in zip(pairs, changes(middle, step, top, pairs)):
            for f in range(3):
                for v in range(PARTS):
                    at = (f, p, v, pl.ds(top, 8), slice(None))
                    state[at] = 0.5 * ((state[at] + middle[at]) + change[f][v])

    def advance(step, _):
        low, high = 2 * step + 1, TALL - 2 * step - 1
        sweep(low, high, functools.partial(first, step))
        sweep(low + 1, high - 1, functools.partial(second, step))

    lax.fori_loop(0, STEPS, advance, None)

    def deliver(f, _):
        for c in range(2):
            for quad in range(QUADS):
                rows = slice(HALO + c * 8, HALO + c * 8 + 8)
                parts = [state[f, quad, j, rows, :] for j in range(PARTS)]
                for quarter in range(4):
                    at = pl.ds(2 * quad + quarter // 2, 8, stride=8)
                    turn[c, quarter % 2, at, :] = gathered(parts, quarter, lane)
        for c in range(2):
            for high in range(2):
                for v in range(2):
                    lines = [turn[c, v, (high * 4 + low) * 8 : (high * 4 + low) * 8 + 8, :] for low in range(4)]
                    for x in range(4):
                        out = pltpu.roll(lines[0], 128 - 32 * x, 1) if x else lines[0]
                        for low in range(1, 4):
                            turned = pltpu.roll(lines[low], 32 * (low - x) % 128, 1) if low != x else lines[low]
                            out = jnp.where(lane >= 32 * low, turned, out)
                        out_ref[x * 2 + c, pl.ds(pl.multiple_of(f * 32 + (high * 2 + v) * 8, 8), 8), :] = out

    lax.fori_loop(0, 3, deliver, None)


def mix_kernel(coef_ref, cells_ref, out_ref, mixing):
    row = lax.broadcasted_iota(jnp.int32, (128, 128), 0)
    col = lax.broadcasted_iota(jnp.int32, (128, 128), 1)
    mixing[...] = jnp.where(row <= col, coef_ref[...], 0.0) + jnp.where(row == col, 1.0, 0.0)
    matrix = jnp.concatenate([mixing[pl.ds(t, 8, stride=16), :] for t in range(16)], axis=0)
    for k in range(6):
        cells = jnp.concatenate([cells_ref[p * 96 + k * 16 : p * 96 + k * 16 + 16, :] for p in range(8)], axis=0)
        out_ref[k * 128 : (k + 1) * 128, :] = lax.dot_general(
            cells, matrix, (((0,), (0,)), ((), ())), precision=lax.Precision.HIGHEST, preferred_element_type=f32
        )


VMEM = pl.BlockSpec(memory_space=pltpu.VMEM)
SMEM = pl.BlockSpec(memory_space=pltpu.SMEM)


def on_device(tangents, checkpoints, owner_order, land_mask, coefficients):
    block = lax.axis_index("y") * 2 + lax.axis_index("zh")
    core = lax.axis_index("c")
    raw = pl.pallas_call(
        flow_kernel,
        out_shape=jax.ShapeDtypeStruct((64, LANES), f32),
        in_specs=[SMEM, SMEM, VMEM, VMEM],
        out_specs=VMEM,
        compiler_params=pltpu.CompilerParams(vmem_limit_bytes=16 * 2**20),
    )(block.reshape(1).astype(jnp.int32), owner_order, checkpoints, land_mask)
    up = [(i, i + 1) for i in range(7)]
    down = [(i + 1, i) for i in range(7)]
    ring = [(s * 4 + x, (s + step) % 8 * 4 + x) for s in range(8) for x, step in ((3, 1), (0, -1))]
    halo = lax.ppermute(raw[:48], ("y", "zh", "x"), ring)
    wide = jnp.concatenate([raw, halo], axis=0)
    above, below = lax.ppermute(wide, "zl", up), lax.ppermute(wide, "zl", down)
    send = pl.pallas_call(
        pack_kernel,
        out_shape=jax.ShapeDtypeStruct((PEERS, 64, LANES), f32),
        in_specs=[VMEM, VMEM],
        out_specs=VMEM,
        compiler_params=pltpu.CompilerParams(vmem_limit_bytes=16 * 2**20),
    )(tangents, land_mask)
    send, above, below = lax.optimization_barrier((send, above, below))
    own = lax.all_to_all(send, ("y", "zh", "c"), 0, 0, tiled=True)
    chips = jnp.concatenate([above, wide, below], axis=0)
    strip = jnp.concatenate(
        [chips] + [lax.ppermute(chips, "x", [(i, (i + k) % 4) for i in range(4)]) for k in (1, 2, 3)], axis=0
    )
    other = lax.ppermute(strip, "c", [(0, 1), (1, 0)])
    own, strip, other = lax.optimization_barrier((own, strip, other))
    coef = pl.pallas_call(
        coef_kernel,
        out_shape=jax.ShapeDtypeStruct((STEPS, COEFS, PARTS, TALL + 8, LANES), f32),
        in_specs=[SMEM, VMEM, VMEM],
        out_specs=VMEM,
        scratch_shapes=[
            pltpu.VMEM((STEPS + 1, 3, PARTS, TALL + 16, LANES), f32),
            pltpu.VMEM((STEPS + 1, 3 * TALL, 2 * LANES), f32),
            pltpu.VMEM((2 * LANES, PARTS * LANES), jnp.bfloat16),
        ],
        compiler_params=pltpu.CompilerParams(vmem_limit_bytes=32 * 2**20),
        cost_estimate=pl.CostEstimate(flops=2 * 10**9, bytes_accessed=50 * 10**6, transcendentals=0),
    )(jnp.stack([core, lax.axis_index("x")]).astype(jnp.int32), strip, other)
    parts = [lax.ppermute(own, "zl", up), own, lax.ppermute(own, "zl", down)]
    parts = [x.reshape(PEERS * 64, LANES) for x in parts]
    out = pl.pallas_call(
        march_kernel,
        out_shape=jax.ShapeDtypeStruct((8, 96, LANES), f32),
        in_specs=[VMEM] * 4,
        out_specs=VMEM,
        scratch_shapes=[
            pltpu.VMEM((3, QUADS, PARTS, TALL + 8, LANES), f32),
            pltpu.VMEM((3, QUADS, PARTS, TALL + 8, LANES), f32),
            pltpu.VMEM((2, 2, 64, LANES), f32),
        ],
        compiler_params=pltpu.CompilerParams(vmem_limit_bytes=26 * 2**20),
    )(*parts, coef)
    cells = lax.all_to_all(out, ("x", "c"), 0, 0, tiled=True)
    mixed = pl.pallas_call(
        mix_kernel,
        out_shape=jax.ShapeDtypeStruct((768, 128), f32),
        in_specs=[VMEM, VMEM],
        out_specs=VMEM,
        scratch_shapes=[pltpu.VMEM((128, 128), f32)],
        compiler_params=pltpu.CompilerParams(vmem_limit_bytes=16 * 2**20),
    )(coefficients, cells.reshape(768, LANES))
    return mixed.reshape(3, 8, 32, 128).transpose(3, 0, 1, 2)


def solution(mesh):
    fine = jax.sharding.Mesh(mesh.devices.reshape(SIZES), AXES)
    mode, rows = ("y", "zh", "x"), ("zl", "c")
    placed = (
        P(mode, None, rows, None),
        P(None, None, rows, mode),
        P(),
        P(rows, None),
        P(),
    )
    return jax.shard_map(
        on_device, mesh=fine, in_specs=placed, out_specs=P(None, None, rows, mode), check_vma=False
    )
```

```python
import functools

import jax
import jax.numpy as jnp
from jax import lax
from jax.experimental import pallas as pl
from jax.experimental.pallas import tpu as pltpu
from jax.sharding import PartitionSpec as P

SIZES = (4, 2, 4, 8, 2)
AXES = ("y", "zh", "x", "zl", "c")
STEPS = 8
LANES = 128
HALO = 16
STRIP = 16
TALL = STRIP + 2 * HALO
PEERS = 16
COEFS = 15
QUADS = 4
GROUP = 4
f32 = jnp.float32


PARTS = 5


def halo_columns(left, right, lane):
    return jnp.where(lane >= 112, left, right)


def spread(inner, halo, part, lane):
    column = (lane % 32) * PARTS + (part - HALO)
    index = (column + LANES) % LANES
    a, b = (jnp.take_along_axis(x, index, axis=1) for x in (inner, halo))
    return jnp.where((column >= 0) & (column < LANES), a, b)


def gathered(parts, quarter, lane):
    column = lane + HALO
    index, rest = column // PARTS + quarter * 32, column % PARTS
    out = jnp.take_along_axis(parts[0], index, axis=1)
    for j in range(1, PARTS):
        out = jnp.where(rest == j, jnp.take_along_axis(parts[j], index, axis=1), out)
    return out


def from_right(cells):
    return [*cells[1:], pltpu.roll(cells[0], LANES - 1, 1)]


def from_left(cells):
    return [pltpu.roll(cells[-1], 1, 1), *cells[:-1]]


def flow_kernel(block_ref, order_ref, base_ref, mask_ref, raw_ref):
    lane = lax.broadcasted_iota(jnp.int32, (8, LANES), 1)
    s = block_ref[0]
    for high in range(2):
        for f in range(3):
            flow = jnp.concatenate([base_ref[order_ref[high * 4 + low], f] for low in range(4)], axis=1)
            raw_ref[(high * 3 + f) * 8 : (high * 3 + f) * 8 + 8, :] = flow

    def column(k):
        return mask_ref[:, pl.ds(pl.multiple_of(k * LANES, LANES), LANES)].astype(f32)

    raw_ref[48:56, :] = column(s)
    raw_ref[56:64, :] = halo_columns(column(lax.rem(s + 7, 8)), column(lax.rem(s + 1, 8)), lane)


def pack_kernel(tan_ref, mask_ref, send_ref):
    lane = lax.broadcasted_iota(jnp.int32, (8, LANES), 1)
    wet = [mask_ref[:, k * LANES : (k + 1) * LANES].astype(f32) for k in range(8)]

    def send(core, _):
        cells = [
            [[tan_ref[2 * core + q, f, :, k * LANES : (k + 1) * LANES] * wet[k] for k in range(8)] for f in range(3)]
            for q in range(2)
        ]
        for k in range(8):
            lines = []
            for f in range(3):
                for j in range(PARTS):
                    for q in range(2):
                        row = cells[q][f]
                        halo = halo_columns(row[(k + 7) % 8], row[(k + 1) % 8], lane)
                        lines.append(spread(row[k], halo, j, lane))
            lines += lines[:2]
            for i in range(8):
                a, b, c, d = lines[4 * i : 4 * i + 4]
                out = jnp.where(lane < 32, a, jnp.where(lane < 64, b, jnp.where(lane < 96, c, d)))
                send_ref[(k % 2 * 4 + k // 2) * 2 + core, i * 8 : i * 8 + 8, :] = out

    lax.fori_loop(0, 2, send, None)


def coef_kernel(core_ref, strip_ref, other_ref, coef, base, lines, spread_matrix):
    lane = lax.broadcasted_iota(jnp.int32, (8, LANES), 1)
    core, me = core_ref[0], core_ref[1]
    blocks = [lax.rem(me - x + 4, 4) * 336 for x in range(4)]
    places = blocks + [blocks[3] + 64, blocks[0] + 64]
    strips = []
    for other, ref in enumerate((strip_ref, other_ref)):
        for z in range(3):
            top = pl.multiple_of((1 - core if other else core) * 8 + z * 16, 8)
            strips.append((ref, z * 112, top))
            at = z * 112 + 48
            lines[STEPS, pl.ds(top, 8), :LANES] = ref[at : at + 8, :]
            lines[STEPS, pl.ds(top, 8), LANES:] = ref[at + 8 : at + 16, :]

    def unpack(part, _):
        high, f = part // 3, part % 3
        for ref, first, top in strips:
            quads = [ref[pl.ds(pl.multiple_of(first + at + part * 8, 8), 8), :] for at in places]
            for low in range(4):
                out = pltpu.roll(quads[0], (128 - 32 * low) % 128, 1) if low else quads[0]
                for x in range(1, 4):
                    turned = pltpu.roll(quads[x], 32 * (x - low) % 128, 1) if x != low else quads[x]
                    out = jnp.where(lane >= 32 * x, turned, out)
                left = pltpu.roll(quads[4], (96 - 32 * low) % 128, 1)
                right = pltpu.roll(quads[5], (128 - 32 * low) % 128, 1)
                halo = halo_columns(left, right, lane)
                rows = pl.ds(pl.multiple_of(f * TALL + top, 8), 8)
                lines[high * 4 + low, rows, :LANES] = out
                lines[high * 4 + low, rows, LANES:] = halo

    lax.fori_loop(0, 6, unpack, None)

    place = lax.broadcasted_iota(jnp.int32, (2 * LANES, LANES), 0)
    column = jnp.where(place < LANES, place, jnp.where(place < LANES + 16, place, place - 2 * LANES))
    target = lax.broadcasted_iota(jnp.int32, (2 * LANES, LANES), 1) % 32 * PARTS - HALO
    for j in range(PARTS):
        spread_matrix[:, j * LANES : (j + 1) * LANES] = (column == target + j).astype(jnp.bfloat16)

    def spread_lines(step, _):
        cells = lines[step]
        high = cells.astype(jnp.bfloat16)
        rest = cells - high.astype(f32)
        mid = rest.astype(jnp.bfloat16)
        low = (rest - mid.astype(f32)).astype(jnp.bfloat16)
        out = [jnp.dot(x, spread_matrix[...], preferred_element_type=f32) for x in (high, mid, low)]
        out = (out[0] + out[1]) + out[2]
        for j in range(PARTS):
            for f in range(3):
                part = out[f * TALL : (f + 1) * TALL, j * LANES : (j + 1) * LANES]
                base[step, f, j, 8 : TALL + 8, :] = part
        return _

    lax.fori_loop(0, STEPS + 1, spread_lines, None)

    def prepare(step, tile):
        top = pl.multiple_of(tile * 8, 8)
        w = [base[STEPS, 0, v, pl.ds(top + 8, 8), :] * 0.25 for v in range(PARTS)]

        def rows(f, shift):
            return [base[step, f, v, pl.ds(top + 8 + shift, 8), :] for v in range(PARTS)]

        depth = [x + 1.0 for x in rows(0, 0)]
        b, c = rows(1, 0), rows(2, 0)
        hp, hm = from_right(depth), from_left(depth)
        bp, bm = from_right(b), from_left(b)
        cp, cm = from_right(c), from_left(c)
        hn, hs = rows(0, 1), rows(0, -1)
        bn, bs = rows(1, 1), rows(1, -1)
        cn, cs = rows(2, 1), rows(2, -1)
        for v in range(PARTS):
            q = w[v]
            parts = (
                -q * hp[v], q * hm[v], -q * bp[v], q * bm[v],
                -q * (hn[v] + 1.0), q * (hs[v] + 1.0), -q * cn[v], q * cs[v],
                -q * b[v], -q * c[v],
                -q * (bp[v] - bm[v]), q * (1.0 - (bn[v] - bs[v])), -q * (1.0 + (cp[v] - cm[v])), -q * (cn[v] - cs[v]),
                q,
            )
            for k, part in enumerate(parts):
                coef[step, k, v, pl.ds(top, 8), :] = part

    def tiles(step, _):
        lax.fori_loop((2 * step + 1) // 8, (TALL - 2 * step + 6) // 8, lambda tile, _: prepare(step, tile), None)

    lax.fori_loop(0, STEPS, tiles, None)


def march_kernel(prev_ref, own_ref, next_ref, coef, out_ref, state, middle, turn):
    lane = lax.broadcasted_iota(jnp.int32, (8, LANES), 1)
    def place(quad, _):
        for z, ref in enumerate((prev_ref, own_ref, next_ref)):
            for c in range(2):
                for f in range(3):
                    for j in range(PARTS):
                        i, odd = divmod(f * PARTS + j, 2)
                        one, two = (
                            ref[pl.ds(pl.multiple_of(((p * 4 + quad) * 2 + c) * 64 + i * 8, 8), 8), :] for p in range(2)
                        )
                        one, two = (pltpu.roll(one, 64, 1), two) if odd else (one, pltpu.roll(two, 64, 1))
                        rows = slice(z * 16 + c * 8, z * 16 + c * 8 + 8)
                        state[f, quad, j, rows, :] = jnp.where(lane < 64, one, two)

    lax.fori_loop(0, QUADS, place, None)
    def changes(ref, step, top, pairs):
        rows, north, south = (pl.ds(top + k, 8) for k in (0, 1, -1))
        moved = []
        for p in pairs:
            h, u, m = ([ref[f, p, v, rows, :] for v in range(PARTS)] for f in range(3))
            moved.append(
                (h, u, m, from_right(h), from_left(h), from_right(u), from_left(u))
                + ([a - b for a, b in zip(from_right(m), from_left(m))],)
            )
        out = [([], [], []) for _ in pairs]
        for v in range(PARTS):
            k = [coef[step, i, v, rows, :] for i in range(COEFS)]
            for p, (h, u, m, hp, hm, up, um, md), fields in zip(pairs, moved, out):
                hn, un, mn = (ref[f, p, v, north, :] for f in range(3))
                hs, us, ms = (ref[f, p, v, south, :] for f in range(3))
                fields[0].append(
                    ((k[0] * up[v] + k[1] * um[v]) + (k[2] * hp[v] + k[3] * hm[v]))
                    + ((k[4] * mn + k[5] * ms) + (k[6] * hn + k[7] * hs))
                )
                fields[1].append(
                    (k[8] * (up[v] - um[v]) + k[9] * (un - us)) + ((k[10] * u[v] + k[11] * m[v]) - k[14] * (hp[v] - hm[v]))
                )
                fields[2].append((k[8] * md[v] + k[9] * (mn - ms)) + ((k[12] * u[v] + k[13] * m[v]) - k[14] * (hn - hs)))
        return out

    def sweep(low, high, body):
        def window(i, _):
            lax.fori_loop(0, QUADS // GROUP, lambda g, _: body(low + 8 * i, [g * GROUP + k for k in range(GROUP)]), None)

        lax.fori_loop(0, (high - low + 7) // 8, window, None)

    def first(step, top, pairs):
        for p, change in zip(pairs, changes(state, step, top, pairs)):
            for f in range(3):
                for v in range(PARTS):
                    middle[f, p, v, pl.ds(top, 8), :] = state[f, p, v, pl.ds(top, 8), :] + change[f][v]

    def second(step, top, pairs):
        for p, change in zip(pairs, changes(middle, step, top, pairs)):
            for f in range(3):
                for v in range(PARTS):
                    at = (f, p, v, pl.ds(top, 8), slice(None))
                    state[at] = 0.5 * ((state[at] + middle[at]) + change[f][v])

    def advance(step, _):
        low, high = 2 * step + 1, TALL - 2 * step - 1
        sweep(low, high, functools.partial(first, step))
        sweep(low + 1, high - 1, functools.partial(second, step))

    lax.fori_loop(0, STEPS, advance, None)

    def deliver(f, _):
        for c in range(2):
            for quad in range(QUADS):
                rows = slice(HALO + c * 8, HALO + c * 8 + 8)
                parts = [state[f, quad, j, rows, :] for j in range(PARTS)]
                for quarter in range(4):
                    at = pl.ds(2 * quad + quarter // 2, 8, stride=8)
                    turn[c, quarter % 2, at, :] = gathered(parts, quarter, lane)
        for c in range(2):
            for high in range(2):
                for v in range(2):
                    lines = [turn[c, v, (high * 4 + low) * 8 : (high * 4 + low) * 8 + 8, :] for low in range(4)]
                    for x in range(4):
                        out = pltpu.roll(lines[0], 128 - 32 * x, 1) if x else lines[0]
                        for low in range(1, 4):
                            turned = pltpu.roll(lines[low], 32 * (low - x) % 128, 1) if low != x else lines[low]
                            out = jnp.where(lane >= 32 * low, turned, out)
                        out_ref[x * 2 + c, pl.ds(pl.multiple_of(f * 32 + (high * 2 + v) * 8, 8), 8), :] = out

    lax.fori_loop(0, 3, deliver, None)


def mix_kernel(coef_ref, cells_ref, out_ref, mixing):
    row = lax.broadcasted_iota(jnp.int32, (128, 128), 0)
    col = lax.broadcasted_iota(jnp.int32, (128, 128), 1)
    mixing[...] = jnp.where(row <= col, coef_ref[...], 0.0) + jnp.where(row == col, 1.0, 0.0)
    matrix = jnp.concatenate([mixing[pl.ds(t, 8, stride=16), :] for t in range(16)], axis=0)
    for k in range(6):
        cells = jnp.concatenate([cells_ref[p * 96 + k * 16 : p * 96 + k * 16 + 16, :] for p in range(8)], axis=0)
        out_ref[k * 128 : (k + 1) * 128, :] = lax.dot_general(
            cells, matrix, (((0,), (0,)), ((), ())), precision=lax.Precision.HIGHEST, preferred_element_type=f32
        )


VMEM = pl.BlockSpec(memory_space=pltpu.VMEM)
SMEM = pl.BlockSpec(memory_space=pltpu.SMEM)


def on_device(tangents, checkpoints, owner_order, land_mask, coefficients):
    block = lax.axis_index("y") * 2 + lax.axis_index("zh")
    core = lax.axis_index("c")
    raw = pl.pallas_call(
        flow_kernel,
        out_shape=jax.ShapeDtypeStruct((64, LANES), f32),
        in_specs=[SMEM, SMEM, VMEM, VMEM],
        out_specs=VMEM,
        compiler_params=pltpu.CompilerParams(vmem_limit_bytes=16 * 2**20),
    )(block.reshape(1).astype(jnp.int32), owner_order, checkpoints, land_mask)
    up = [(i, i + 1) for i in range(7)]
    down = [(i + 1, i) for i in range(7)]
    ring = [(s * 4 + x, (s + step) % 8 * 4 + x) for s in range(8) for x, step in ((3, 1), (0, -1))]
    halo = lax.ppermute(raw[:48], ("y", "zh", "x"), ring)
    wide = jnp.concatenate([raw, halo], axis=0)
    above, below = lax.ppermute(wide, "zl", up), lax.ppermute(wide, "zl", down)
    send = pl.pallas_call(
        pack_kernel,
        out_shape=jax.ShapeDtypeStruct((PEERS, 64, LANES), f32),
        in_specs=[VMEM, VMEM],
        out_specs=VMEM,
        compiler_params=pltpu.CompilerParams(vmem_limit_bytes=16 * 2**20),
    )(tangents, land_mask)
    send, above, below = lax.optimization_barrier((send, above, below))
    own = lax.all_to_all(send, ("zh", "y", "c"), 0, 0, tiled=True)
    chips = jnp.concatenate([above, wide, below], axis=0)
    strip = jnp.concatenate(
        [chips] + [lax.ppermute(chips, "x", [(i, (i + k) % 4) for i in range(4)]) for k in (1, 2, 3)], axis=0
    )
    other = lax.ppermute(strip, "c", [(0, 1), (1, 0)])
    own, strip, other = lax.optimization_barrier((own, strip, other))
    coef = pl.pallas_call(
        coef_kernel,
        out_shape=jax.ShapeDtypeStruct((STEPS, COEFS, PARTS, TALL + 8, LANES), f32),
        in_specs=[SMEM, VMEM, VMEM],
        out_specs=VMEM,
        scratch_shapes=[
            pltpu.VMEM((STEPS + 1, 3, PARTS, TALL + 16, LANES), f32),
            pltpu.VMEM((STEPS + 1, 3 * TALL, 2 * LANES), f32),
            pltpu.VMEM((2 * LANES, PARTS * LANES), jnp.bfloat16),
        ],
        compiler_params=pltpu.CompilerParams(vmem_limit_bytes=32 * 2**20),
        cost_estimate=pl.CostEstimate(flops=2 * 10**9, bytes_accessed=50 * 10**6, transcendentals=0),
    )(jnp.stack([core, lax.axis_index("x")]).astype(jnp.int32), strip, other)
    parts = [lax.ppermute(own, "zl", up), own, lax.ppermute(own, "zl", down)]
    parts = [x.reshape(PEERS * 64, LANES) for x in parts]
    out = pl.pallas_call(
        march_kernel,
        out_shape=jax.ShapeDtypeStruct((8, 96, LANES), f32),
        in_specs=[VMEM] * 4,
        out_specs=VMEM,
        scratch_shapes=[
            pltpu.VMEM((3, QUADS, PARTS, TALL + 8, LANES), f32),
            pltpu.VMEM((3, QUADS, PARTS, TALL + 8, LANES), f32),
            pltpu.VMEM((2, 2, 64, LANES), f32),
        ],
        compiler_params=pltpu.CompilerParams(vmem_limit_bytes=26 * 2**20),
    )(*parts, coef)
    cells = lax.all_to_all(out, ("x", "c"), 0, 0, tiled=True)
    mixed = pl.pallas_call(
        mix_kernel,
        out_shape=jax.ShapeDtypeStruct((768, 128), f32),
        in_specs=[VMEM, VMEM],
        out_specs=VMEM,
        scratch_shapes=[pltpu.VMEM((128, 128), f32)],
        compiler_params=pltpu.CompilerParams(vmem_limit_bytes=16 * 2**20),
    )(coefficients, cells.reshape(768, LANES))
    return mixed.reshape(3, 8, 32, 128).transpose(3, 0, 1, 2)


def solution(mesh):
    fine = jax.sharding.Mesh(mesh.devices.reshape(SIZES), AXES)
    mode, rows = ("y", "zh", "x"), ("zl", "c")
    placed = (
        P(mode, None, rows, None),
        P(None, None, rows, mode),
        P(),
        P(rows, None),
        P(),
    )
    return jax.shard_map(
        on_device, mesh=fine, in_specs=placed, out_specs=P(None, None, rows, mode), check_vma=False
    )
```

```python
import functools

import jax
import jax.numpy as jnp
from jax import lax
from jax.experimental import pallas as pl
from jax.experimental.pallas import tpu as pltpu
from jax.sharding import PartitionSpec as P

SIZES = (4, 2, 4, 8, 2)
AXES = ("y", "zh", "x", "zl", "c")
STEPS = 8
LANES = 128
HALO = 16
STRIP = 16
TALL = STRIP + 2 * HALO
PEERS = 16
COEFS = 15
QUADS = 4
GROUP = 4
f32 = jnp.float32


PARTS = 5


def halo_columns(left, right, lane):
    return jnp.where(lane >= 112, left, right)


def spread(inner, halo, part, lane):
    column = (lane % 32) * PARTS + (part - HALO)
    index = (column + LANES) % LANES
    a, b = (jnp.take_along_axis(x, index, axis=1) for x in (inner, halo))
    return jnp.where((column >= 0) & (column < LANES), a, b)


def gathered(parts, quarter, lane):
    column = lane + HALO
    index, rest = column // PARTS + quarter * 32, column % PARTS
    out = jnp.take_along_axis(parts[0], index, axis=1)
    for j in range(1, PARTS):
        out = jnp.where(rest == j, jnp.take_along_axis(parts[j], index, axis=1), out)
    return out


def from_right(cells):
    return [*cells[1:], pltpu.roll(cells[0], LANES - 1, 1)]


def from_left(cells):
    return [pltpu.roll(cells[-1], 1, 1), *cells[:-1]]


def flow_kernel(block_ref, base_ref, mask_ref, raw_ref):
    lane = lax.broadcasted_iota(jnp.int32, (8, LANES), 1)
    s = block_ref[0]
    for high in range(2):
        for f in range(3):
            flow = jnp.concatenate([base_ref[high * 4 + low, f] for low in range(4)], axis=1)
            raw_ref[(high * 3 + f) * 8 : (high * 3 + f) * 8 + 8, :] = flow

    def column(k):
        return mask_ref[:, pl.ds(pl.multiple_of(k * LANES, LANES), LANES)].astype(f32)

    raw_ref[48:56, :] = column(s)
    raw_ref[56:64, :] = halo_columns(column(lax.rem(s + 7, 8)), column(lax.rem(s + 1, 8)), lane)


def pack_kernel(tan_ref, mask_ref, send_ref):
    lane = lax.broadcasted_iota(jnp.int32, (8, LANES), 1)
    wet = [mask_ref[:, k * LANES : (k + 1) * LANES].astype(f32) for k in range(8)]

    def send(core, _):
        cells = [
            [[tan_ref[2 * core + q, f, :, k * LANES : (k + 1) * LANES] * wet[k] for k in range(8)] for f in range(3)]
            for q in range(2)
        ]
        for k in range(8):
            lines = []
            for f in range(3):
                for j in range(PARTS):
                    for q in range(2):
                        row = cells[q][f]
                        halo = halo_columns(row[(k + 7) % 8], row[(k + 1) % 8], lane)
                        lines.append(spread(row[k], halo, j, lane))
            lines += lines[:2]
            for i in range(8):
                a, b, c, d = lines[4 * i : 4 * i + 4]
                out = jnp.where(lane < 32, a, jnp.where(lane < 64, b, jnp.where(lane < 96, c, d)))
                send_ref[(k % 2 * 4 + k // 2) * 2 + core, i * 8 : i * 8 + 8, :] = out

    lax.fori_loop(0, 2, send, None)


def coef_kernel(core_ref, order_ref, strip_ref, other_ref, coef, base, lines, spread_matrix):
    lane = lax.broadcasted_iota(jnp.int32, (8, LANES), 1)
    core, me = core_ref[0], core_ref[1]
    blocks = [lax.rem(me - x + 4, 4) * 336 for x in range(4)]
    places = blocks + [blocks[3] + 64, blocks[0] + 64]
    strips = []
    for other, ref in enumerate((strip_ref, other_ref)):
        for z in range(3):
            top = pl.multiple_of((1 - core if other else core) * 8 + z * 16, 8)
            strips.append((ref, z * 112, top))
            at = z * 112 + 48
            lines[STEPS, pl.ds(top, 8), :LANES] = ref[at : at + 8, :]
            lines[STEPS, pl.ds(top, 8), LANES:] = ref[at + 8 : at + 16, :]

    def unpack(part, _):
        high, f = part // 3, part % 3
        for ref, first, top in strips:
            quads = [ref[pl.ds(pl.multiple_of(first + at + part * 8, 8), 8), :] for at in places]
            for low in range(4):
                out = pltpu.roll(quads[0], (128 - 32 * low) % 128, 1) if low else quads[0]
                for x in range(1, 4):
                    turned = pltpu.roll(quads[x], 32 * (x - low) % 128, 1) if x != low else quads[x]
                    out = jnp.where(lane >= 32 * x, turned, out)
                left = pltpu.roll(quads[4], (96 - 32 * low) % 128, 1)
                right = pltpu.roll(quads[5], (128 - 32 * low) % 128, 1)
                halo = halo_columns(left, right, lane)
                rows = pl.ds(pl.multiple_of(f * TALL + top, 8), 8)
                lines[high * 4 + low, rows, :LANES] = out
                lines[high * 4 + low, rows, LANES:] = halo

    lax.fori_loop(0, 6, unpack, None)

    place = lax.broadcasted_iota(jnp.int32, (2 * LANES, LANES), 0)
    column = jnp.where(place < LANES, place, jnp.where(place < LANES + 16, place, place - 2 * LANES))
    target = lax.broadcasted_iota(jnp.int32, (2 * LANES, LANES), 1) % 32 * PARTS - HALO
    for j in range(PARTS):
        spread_matrix[:, j * LANES : (j + 1) * LANES] = (column == target + j).astype(jnp.bfloat16)

    def spread_lines(step, _):
        cells = lines[step]
        high = cells.astype(jnp.bfloat16)
        rest = cells - high.astype(f32)
        mid = rest.astype(jnp.bfloat16)
        low = (rest - mid.astype(f32)).astype(jnp.bfloat16)
        out = [jnp.dot(x, spread_matrix[...], preferred_element_type=f32) for x in (high, mid, low)]
        out = (out[0] + out[1]) + out[2]
        for j in range(PARTS):
            for f in range(3):
                part = out[f * TALL : (f + 1) * TALL, j * LANES : (j + 1) * LANES]
                base[step, f, j, 8 : TALL + 8, :] = part
        return _

    lax.fori_loop(0, STEPS + 1, spread_lines, None)

    def prepare(step, tile):
        top = pl.multiple_of(tile * 8, 8)
        slot = order_ref[step]
        w = [base[STEPS, 0, v, pl.ds(top + 8, 8), :] * 0.25 for v in range(PARTS)]

        def rows(f, shift):
            return [base[slot, f, v, pl.ds(top + 8 + shift, 8), :] for v in range(PARTS)]

        depth = [x + 1.0 for x in rows(0, 0)]
        b, c = rows(1, 0), rows(2, 0)
        hp, hm = from_right(depth), from_left(depth)
        bp, bm = from_right(b), from_left(b)
        cp, cm = from_right(c), from_left(c)
        hn, hs = rows(0, 1), rows(0, -1)
        bn, bs = rows(1, 1), rows(1, -1)
        cn, cs = rows(2, 1), rows(2, -1)
        for v in range(PARTS):
            q = w[v]
            parts = (
                -q * hp[v], q * hm[v], -q * bp[v], q * bm[v],
                -q * (hn[v] + 1.0), q * (hs[v] + 1.0), -q * cn[v], q * cs[v],
                -q * b[v], -q * c[v],
                -q * (bp[v] - bm[v]), q * (1.0 - (bn[v] - bs[v])), -q * (1.0 + (cp[v] - cm[v])), -q * (cn[v] - cs[v]),
                q,
            )
            for k, part in enumerate(parts):
                coef[step, k, v, pl.ds(top, 8), :] = part

    def tiles(step, _):
        lax.fori_loop((2 * step + 1) // 8, (TALL - 2 * step + 6) // 8, lambda tile, _: prepare(step, tile), None)

    lax.fori_loop(0, STEPS, tiles, None)


def march_kernel(prev_ref, own_ref, next_ref, coef, out_ref, state, middle, turn):
    lane = lax.broadcasted_iota(jnp.int32, (8, LANES), 1)
    def place(quad, _):
        for z, ref in enumerate((prev_ref, own_ref, next_ref)):
            for c in range(2):
                for f in range(3):
                    for j in range(PARTS):
                        i, odd = divmod(f * PARTS + j, 2)
                        one, two = (
                            ref[pl.ds(pl.multiple_of(((p * 4 + quad) * 2 + c) * 64 + i * 8, 8), 8), :] for p in range(2)
                        )
                        one, two = (pltpu.roll(one, 64, 1), two) if odd else (one, pltpu.roll(two, 64, 1))
                        rows = slice(z * 16 + c * 8, z * 16 + c * 8 + 8)
                        state[f, quad, j, rows, :] = jnp.where(lane < 64, one, two)

    lax.fori_loop(0, QUADS, place, None)
    def changes(ref, step, top, pairs):
        rows, north, south = (pl.ds(top + k, 8) for k in (0, 1, -1))
        moved = []
        for p in pairs:
            h, u, m = ([ref[f, p, v, rows, :] for v in range(PARTS)] for f in range(3))
            moved.append(
                (h, u, m, from_right(h), from_left(h), from_right(u), from_left(u))
                + ([a - b for a, b in zip(from_right(m), from_left(m))],)
            )
        out = [([], [], []) for _ in pairs]
        for v in range(PARTS):
            k = [coef[step, i, v, rows, :] for i in range(COEFS)]
            for p, (h, u, m, hp, hm, up, um, md), fields in zip(pairs, moved, out):
                hn, un, mn = (ref[f, p, v, north, :] for f in range(3))
                hs, us, ms = (ref[f, p, v, south, :] for f in range(3))
                fields[0].append(
                    ((k[0] * up[v] + k[1] * um[v]) + (k[2] * hp[v] + k[3] * hm[v]))
                    + ((k[4] * mn + k[5] * ms) + (k[6] * hn + k[7] * hs))
                )
                fields[1].append(
                    (k[8] * (up[v] - um[v]) + k[9] * (un - us)) + ((k[10] * u[v] + k[11] * m[v]) - k[14] * (hp[v] - hm[v]))
                )
                fields[2].append((k[8] * md[v] + k[9] * (mn - ms)) + ((k[12] * u[v] + k[13] * m[v]) - k[14] * (hn - hs)))
        return out

    def sweep(low, high, body):
        count = (high - low + 7) // 8
        quads = list(range(QUADS))

        def two(i, _):
            body(low + 16 * i, quads)
            body(low + 16 * i + 8, quads)

        lax.fori_loop(0, count // 2, two, None)
        lax.fori_loop(count // 2 * 2, count, lambda i, _: body(low + 8 * i, quads), None)

    def first(step, top, pairs):
        for p, change in zip(pairs, changes(state, step, top, pairs)):
            for f in range(3):
                for v in range(PARTS):
                    middle[f, p, v, pl.ds(top, 8), :] = state[f, p, v, pl.ds(top, 8), :] + change[f][v]

    def second(step, top, pairs):
        for p, change in zip(pairs, changes(middle, step, top, pairs)):
            for f in range(3):
                for v in range(PARTS):
                    at = (f, p, v, pl.ds(top, 8), slice(None))
                    state[at] = 0.5 * ((state[at] + middle[at]) + change[f][v])

    def advance(step, _):
        low, high = 2 * step + 1, TALL - 2 * step - 1
        sweep(low, high, functools.partial(first, step))
        sweep(low + 1, high - 1, functools.partial(second, step))

    lax.fori_loop(0, STEPS, advance, None)

    def deliver(f, _):
        for c in range(2):
            for quad in range(QUADS):
                rows = slice(HALO + c * 8, HALO + c * 8 + 8)
                parts = [state[f, quad, j, rows, :] for j in range(PARTS)]
                for quarter in range(4):
                    at = pl.ds(2 * quad + quarter // 2, 8, stride=8)
                    turn[c, quarter % 2, at, :] = gathered(parts, quarter, lane)
        for c in range(2):
            for high in range(2):
                for v in range(2):
                    lines = [turn[c, v, (high * 4 + low) * 8 : (high * 4 + low) * 8 + 8, :] for low in range(4)]
                    for x in range(4):
                        out = pltpu.roll(lines[0], 128 - 32 * x, 1) if x else lines[0]
                        for low in range(1, 4):
                            turned = pltpu.roll(lines[low], 32 * (low - x) % 128, 1) if low != x else lines[low]
                            out = jnp.where(lane >= 32 * low, turned, out)
                        out_ref[x * 2 + c, pl.ds(pl.multiple_of(f * 32 + (high * 2 + v) * 8, 8), 8), :] = out

    lax.fori_loop(0, 3, deliver, None)


def mix_kernel(coef_ref, cells_ref, out_ref, mixing):
    row = lax.broadcasted_iota(jnp.int32, (128, 128), 0)
    col = lax.broadcasted_iota(jnp.int32, (128, 128), 1)
    mixing[...] = jnp.where(row <= col, coef_ref[...], 0.0) + jnp.where(row == col, 1.0, 0.0)
    matrix = jnp.concatenate([mixing[pl.ds(t, 8, stride=16), :] for t in range(16)], axis=0)
    for k in range(6):
        cells = jnp.concatenate([cells_ref[p * 96 + k * 16 : p * 96 + k * 16 + 16, :] for p in range(8)], axis=0)
        out_ref[k * 128 : (k + 1) * 128, :] = lax.dot_general(
            cells, matrix, (((0,), (0,)), ((), ())), precision=lax.Precision.HIGHEST, preferred_element_type=f32
        )


VMEM = pl.BlockSpec(memory_space=pltpu.VMEM)
SMEM = pl.BlockSpec(memory_space=pltpu.SMEM)


def on_device(tangents, checkpoints, owner_order, land_mask, coefficients):
    block = lax.axis_index("y") * 2 + lax.axis_index("zh")
    core = lax.axis_index("c")
    raw = pl.pallas_call(
        flow_kernel,
        out_shape=jax.ShapeDtypeStruct((64, LANES), f32),
        in_specs=[SMEM, VMEM, VMEM],
        out_specs=VMEM,
        compiler_params=pltpu.CompilerParams(vmem_limit_bytes=16 * 2**20),
    )(block.reshape(1).astype(jnp.int32), checkpoints, land_mask)
    up = [(i, i + 1) for i in range(7)]
    down = [(i + 1, i) for i in range(7)]
    ring = [(s * 4 + x, (s + step) % 8 * 4 + x) for s in range(8) for x, step in ((3, 1), (0, -1))]
    halo = lax.ppermute(raw[:48], ("y", "zh", "x"), ring)
    wide = jnp.concatenate([raw, halo], axis=0)
    above, below = lax.ppermute(wide, "zl", up), lax.ppermute(wide, "zl", down)
    send = pl.pallas_call(
        pack_kernel,
        out_shape=jax.ShapeDtypeStruct((PEERS, 64, LANES), f32),
        in_specs=[VMEM, VMEM],
        out_specs=VMEM,
        compiler_params=pltpu.CompilerParams(vmem_limit_bytes=16 * 2**20),
    )(tangents, land_mask)
    send, above, below = lax.optimization_barrier((send, above, below))
    own = lax.all_to_all(send, ("zh", "y", "c"), 0, 0, tiled=True)
    chips = jnp.concatenate([above, wide, below], axis=0)
    strip = jnp.concatenate(
        [chips] + [lax.ppermute(chips, "x", [(i, (i + k) % 4) for i in range(4)]) for k in (1, 2, 3)], axis=0
    )
    other = lax.ppermute(strip, "c", [(0, 1), (1, 0)])
    own, strip, other = lax.optimization_barrier((own, strip, other))
    coef = pl.pallas_call(
        coef_kernel,
        out_shape=jax.ShapeDtypeStruct((STEPS, COEFS, PARTS, TALL + 8, LANES), f32),
        in_specs=[SMEM, SMEM, VMEM, VMEM],
        out_specs=VMEM,
        scratch_shapes=[
            pltpu.VMEM((STEPS + 1, 3, PARTS, TALL + 16, LANES), f32),
            pltpu.VMEM((STEPS + 1, 3 * TALL, 2 * LANES), f32),
            pltpu.VMEM((2 * LANES, PARTS * LANES), jnp.bfloat16),
        ],
        compiler_params=pltpu.CompilerParams(vmem_limit_bytes=32 * 2**20),
        cost_estimate=pl.CostEstimate(flops=2 * 10**9, bytes_accessed=50 * 10**6, transcendentals=0),
    )(jnp.stack([core, lax.axis_index("x")]).astype(jnp.int32), owner_order, strip, other)
    parts = [lax.ppermute(own, "zl", up), own, lax.ppermute(own, "zl", down)]
    parts = [x.reshape(PEERS * 64, LANES) for x in parts]
    out = pl.pallas_call(
        march_kernel,
        out_shape=jax.ShapeDtypeStruct((8, 96, LANES), f32),
        in_specs=[VMEM] * 4,
        out_specs=VMEM,
        scratch_shapes=[
            pltpu.VMEM((3, QUADS, PARTS, TALL + 8, LANES), f32),
            pltpu.VMEM((3, QUADS, PARTS, TALL + 8, LANES), f32),
            pltpu.VMEM((2, 2, 64, LANES), f32),
        ],
        compiler_params=pltpu.CompilerParams(vmem_limit_bytes=26 * 2**20),
    )(*parts, coef)
    cells = lax.all_to_all(out, ("x", "c"), 0, 0, tiled=True)
    mixed = pl.pallas_call(
        mix_kernel,
        out_shape=jax.ShapeDtypeStruct((768, 128), f32),
        in_specs=[VMEM, VMEM],
        out_specs=VMEM,
        scratch_shapes=[pltpu.VMEM((128, 128), f32)],
        compiler_params=pltpu.CompilerParams(vmem_limit_bytes=16 * 2**20),
    )(coefficients, cells.reshape(768, LANES))
    return mixed.reshape(3, 8, 32, 128).transpose(3, 0, 1, 2)


def solution(mesh):
    fine = jax.sharding.Mesh(mesh.devices.reshape(SIZES), AXES)
    mode, rows = ("y", "zh", "x"), ("zl", "c")
    placed = (
        P(mode, None, rows, None),
        P(None, None, rows, mode),
        P(),
        P(rows, None),
        P(),
    )
    return jax.shard_map(
        on_device, mesh=fine, in_specs=placed, out_specs=P(None, None, rows, mode), check_vma=False
    )
```

```python
import functools

import jax
import jax.numpy as jnp
from jax import lax
from jax.experimental import pallas as pl
from jax.experimental.pallas import tpu as pltpu
from jax.sharding import PartitionSpec as P

SIZES = (4, 2, 4, 8, 2)
AXES = ("y", "zh", "x", "zl", "c")
STEPS = 8
LANES = 128
HALO = 16
STRIP = 16
TALL = STRIP + 2 * HALO
PEERS = 16
COEFS = 15
QUADS = 4
GROUP = 4
f32 = jnp.float32


PARTS = 5


def halo_columns(left, right, lane):
    return jnp.where(lane >= 112, left, right)


def spread(inner, halo, part, lane):
    column = (lane % 32) * PARTS + (part - HALO)
    index = (column + LANES) % LANES
    a, b = (jnp.take_along_axis(x, index, axis=1) for x in (inner, halo))
    return jnp.where((column >= 0) & (column < LANES), a, b)


def gathered(parts, quarter, lane):
    column = lane + HALO
    index, rest = column // PARTS + quarter * 32, column % PARTS
    out = jnp.take_along_axis(parts[0], index, axis=1)
    for j in range(1, PARTS):
        out = jnp.where(rest == j, jnp.take_along_axis(parts[j], index, axis=1), out)
    return out


def from_right(cells):
    return [*cells[1:], pltpu.roll(cells[0], LANES - 1, 1)]


def from_left(cells):
    return [pltpu.roll(cells[-1], 1, 1), *cells[:-1]]


def flow_kernel(block_ref, base_ref, mask_ref, raw_ref, wet_ref):
    lane = lax.broadcasted_iota(jnp.int32, (8, LANES), 1)
    wet_ref[...] = mask_ref[...].astype(f32)
    s = block_ref[0]
    for high in range(2):
        for f in range(3):
            flow = jnp.concatenate([base_ref[high * 4 + low, f] for low in range(4)], axis=1)
            raw_ref[(high * 3 + f) * 8 : (high * 3 + f) * 8 + 8, :] = flow

    def column(k):
        return mask_ref[:, pl.ds(pl.multiple_of(k * LANES, LANES), LANES)].astype(f32)

    raw_ref[48:56, :] = column(s)
    raw_ref[56:64, :] = halo_columns(column(lax.rem(s + 7, 8)), column(lax.rem(s + 1, 8)), lane)


def pack_kernel(tan_ref, wet_ref, send_ref):
    lane = lax.broadcasted_iota(jnp.int32, (8, LANES), 1)
    wet = [wet_ref[:, k * LANES : (k + 1) * LANES] for k in range(8)]

    def send(core, _):
        cells = [
            [[tan_ref[2 * core + q, f, :, k * LANES : (k + 1) * LANES] * wet[k] for k in range(8)] for f in range(3)]
            for q in range(2)
        ]
        for k in range(8):
            lines = []
            for f in range(3):
                for j in range(PARTS):
                    for q in range(2):
                        row = cells[q][f]
                        halo = halo_columns(row[(k + 7) % 8], row[(k + 1) % 8], lane)
                        lines.append(spread(row[k], halo, j, lane))
            lines += lines[:2]
            for i in range(8):
                a, b, c, d = lines[4 * i : 4 * i + 4]
                out = jnp.where(lane < 32, a, jnp.where(lane < 64, b, jnp.where(lane < 96, c, d)))
                send_ref[(k % 2 * 4 + k // 2) * 2 + core, i * 8 : i * 8 + 8, :] = out

    lax.fori_loop(0, 2, send, None)


def coef_kernel(core_ref, order_ref, strip_ref, other_ref, coef, base, lines, spread_matrix):
    lane = lax.broadcasted_iota(jnp.int32, (8, LANES), 1)
    core, me = core_ref[0], core_ref[1]
    blocks = [lax.rem(me - x + 4, 4) * 336 for x in range(4)]
    places = blocks + [blocks[3] + 64, blocks[0] + 64]
    strips = []
    for other, ref in enumerate((strip_ref, other_ref)):
        for z in range(3):
            top = pl.multiple_of((1 - core if other else core) * 8 + z * 16, 8)
            strips.append((ref, z * 112, top))
            at = z * 112 + 48
            lines[STEPS, pl.ds(top, 8), :LANES] = ref[at : at + 8, :]
            lines[STEPS, pl.ds(top, 8), LANES:] = ref[at + 8 : at + 16, :]

    def unpack(part, _):
        high, f = part // 3, part % 3
        for ref, first, top in strips:
            quads = [ref[pl.ds(pl.multiple_of(first + at + part * 8, 8), 8), :] for at in places]
            for low in range(4):
                out = pltpu.roll(quads[0], (128 - 32 * low) % 128, 1) if low else quads[0]
                for x in range(1, 4):
                    turned = pltpu.roll(quads[x], 32 * (x - low) % 128, 1) if x != low else quads[x]
                    out = jnp.where(lane >= 32 * x, turned, out)
                left = pltpu.roll(quads[4], (96 - 32 * low) % 128, 1)
                right = pltpu.roll(quads[5], (128 - 32 * low) % 128, 1)
                halo = halo_columns(left, right, lane)
                rows = pl.ds(pl.multiple_of(f * TALL + top, 8), 8)
                lines[high * 4 + low, rows, :LANES] = out
                lines[high * 4 + low, rows, LANES:] = halo

    lax.fori_loop(0, 6, unpack, None)

    place = lax.broadcasted_iota(jnp.int32, (2 * LANES, LANES), 0)
    column = jnp.where(place < LANES, place, jnp.where(place < LANES + 16, place, place - 2 * LANES))
    target = lax.broadcasted_iota(jnp.int32, (2 * LANES, LANES), 1) % 32 * PARTS - HALO
    for j in range(PARTS):
        spread_matrix[:, j * LANES : (j + 1) * LANES] = (column == target + j).astype(jnp.bfloat16)

    def spread_lines(step, _):
        cells = lines[step]
        high = cells.astype(jnp.bfloat16)
        rest = cells - high.astype(f32)
        mid = rest.astype(jnp.bfloat16)
        low = (rest - mid.astype(f32)).astype(jnp.bfloat16)
        out = [jnp.dot(x, spread_matrix[...], preferred_element_type=f32) for x in (high, mid, low)]
        out = (out[0] + out[1]) + out[2]
        for j in range(PARTS):
            for f in range(3):
                part = out[f * TALL : (f + 1) * TALL, j * LANES : (j + 1) * LANES]
                base[step, f, j, 8 : TALL + 8, :] = part
        return _

    lax.fori_loop(0, STEPS + 1, spread_lines, None)

    def prepare(step, tile):
        top = pl.multiple_of(tile * 8, 8)
        slot = order_ref[step]
        w = [base[STEPS, 0, v, pl.ds(top + 8, 8), :] * 0.25 for v in range(PARTS)]

        def rows(f, shift):
            return [base[slot, f, v, pl.ds(top + 8 + shift, 8), :] for v in range(PARTS)]

        depth = [x + 1.0 for x in rows(0, 0)]
        b, c = rows(1, 0), rows(2, 0)
        hp, hm = from_right(depth), from_left(depth)
        bp, bm = from_right(b), from_left(b)
        cp, cm = from_right(c), from_left(c)
        hn, hs = rows(0, 1), rows(0, -1)
        bn, bs = rows(1, 1), rows(1, -1)
        cn, cs = rows(2, 1), rows(2, -1)
        for v in range(PARTS):
            q = w[v]
            parts = (
                -q * hp[v], q * hm[v], -q * bp[v], q * bm[v],
                -q * (hn[v] + 1.0), q * (hs[v] + 1.0), -q * cn[v], q * cs[v],
                -q * b[v], -q * c[v],
                -q * (bp[v] - bm[v]), q * (1.0 - (bn[v] - bs[v])), -q * (1.0 + (cp[v] - cm[v])), -q * (cn[v] - cs[v]),
                q,
            )
            for k, part in enumerate(parts):
                coef[step, k, v, pl.ds(top, 8), :] = part

    def tiles(step, _):
        lax.fori_loop((2 * step + 1) // 8, (TALL - 2 * step + 6) // 8, lambda tile, _: prepare(step, tile), None)

    lax.fori_loop(0, STEPS, tiles, None)


def march_kernel(prev_ref, own_ref, next_ref, coef, out_ref, state, middle, turn):
    lane = lax.broadcasted_iota(jnp.int32, (8, LANES), 1)
    def place(quad, _):
        for z, ref in enumerate((prev_ref, own_ref, next_ref)):
            for c in range(2):
                for f in range(3):
                    for j in range(PARTS):
                        i, odd = divmod(f * PARTS + j, 2)
                        one, two = (
                            ref[pl.ds(pl.multiple_of(((p * 4 + quad) * 2 + c) * 64 + i * 8, 8), 8), :] for p in range(2)
                        )
                        one, two = (pltpu.roll(one, 64, 1), two) if odd else (one, pltpu.roll(two, 64, 1))
                        rows = slice(z * 16 + c * 8, z * 16 + c * 8 + 8)
                        state[f, quad, j, rows, :] = jnp.where(lane < 64, one, two)

    lax.fori_loop(0, QUADS, place, None)
    def changes(ref, step, top, pairs):
        rows, north, south = (pl.ds(top + k, 8) for k in (0, 1, -1))
        moved = []
        for p in pairs:
            h, u, m = ([ref[f, p, v, rows, :] for v in range(PARTS)] for f in range(3))
            moved.append(
                (h, u, m, from_right(h), from_left(h), from_right(u), from_left(u))
                + ([a - b for a, b in zip(from_right(m), from_left(m))],)
            )
        out = [([], [], []) for _ in pairs]
        for v in range(PARTS):
            k = [coef[step, i, v, rows, :] for i in range(COEFS)]
            for p, (h, u, m, hp, hm, up, um, md), fields in zip(pairs, moved, out):
                hn, un, mn = (ref[f, p, v, north, :] for f in range(3))
                hs, us, ms = (ref[f, p, v, south, :] for f in range(3))
                fields[0].append(
                    ((k[0] * up[v] + k[1] * um[v]) + (k[2] * hp[v] + k[3] * hm[v]))
                    + ((k[4] * mn + k[5] * ms) + (k[6] * hn + k[7] * hs))
                )
                fields[1].append(
                    (k[8] * (up[v] - um[v]) + k[9] * (un - us)) + ((k[10] * u[v] + k[11] * m[v]) - k[14] * (hp[v] - hm[v]))
                )
                fields[2].append((k[8] * md[v] + k[9] * (mn - ms)) + ((k[12] * u[v] + k[13] * m[v]) - k[14] * (hn - hs)))
        return out

    def sweep(low, high, body):
        count = (high - low + 7) // 8
        quads = list(range(QUADS))

        def two(i, _):
            body(low + 16 * i, quads)
            body(low + 16 * i + 8, quads)

        lax.fori_loop(0, count // 2, two, None)
        lax.fori_loop(count // 2 * 2, count, lambda i, _: body(low + 8 * i, quads), None)

    def first(step, top, pairs):
        for p, change in zip(pairs, changes(state, step, top, pairs)):
            for f in range(3):
                for v in range(PARTS):
                    middle[f, p, v, pl.ds(top, 8), :] = state[f, p, v, pl.ds(top, 8), :] + change[f][v]

    def second(step, top, pairs):
        for p, change in zip(pairs, changes(middle, step, top, pairs)):
            for f in range(3):
                for v in range(PARTS):
                    at = (f, p, v, pl.ds(top, 8), slice(None))
                    state[at] = 0.5 * ((state[at] + middle[at]) + change[f][v])

    def advance(step, _):
        low, high = 2 * step + 1, TALL - 2 * step - 1
        sweep(low, high, functools.partial(first, step))
        sweep(low + 1, high - 1, functools.partial(second, step))

    lax.fori_loop(0, STEPS, advance, None)

    def deliver(f, _):
        for c in range(2):
            for quad in range(QUADS):
                rows = slice(HALO + c * 8, HALO + c * 8 + 8)
                parts = [state[f, quad, j, rows, :] for j in range(PARTS)]
                for quarter in range(4):
                    at = pl.ds(2 * quad + quarter // 2, 8, stride=8)
                    turn[c, quarter % 2, at, :] = gathered(parts, quarter, lane)
        for c in range(2):
            for high in range(2):
                for v in range(2):
                    lines = [turn[c, v, (high * 4 + low) * 8 : (high * 4 + low) * 8 + 8, :] for low in range(4)]
                    for x in range(4):
                        out = pltpu.roll(lines[0], 128 - 32 * x, 1) if x else lines[0]
                        for low in range(1, 4):
                            turned = pltpu.roll(lines[low], 32 * (low - x) % 128, 1) if low != x else lines[low]
                            out = jnp.where(lane >= 32 * low, turned, out)
                        out_ref[x * 2 + c, pl.ds(pl.multiple_of(f * 32 + (high * 2 + v) * 8, 8), 8), :] = out

    lax.fori_loop(0, 3, deliver, None)


def mix_kernel(coef_ref, cells_ref, out_ref, mixing):
    row = lax.broadcasted_iota(jnp.int32, (128, 128), 0)
    col = lax.broadcasted_iota(jnp.int32, (128, 128), 1)
    mixing[...] = jnp.where(row <= col, coef_ref[...], 0.0) + jnp.where(row == col, 1.0, 0.0)
    matrix = jnp.concatenate([mixing[pl.ds(t, 8, stride=16), :] for t in range(16)], axis=0)
    for k in range(6):
        cells = jnp.concatenate([cells_ref[p * 96 + k * 16 : p * 96 + k * 16 + 16, :] for p in range(8)], axis=0)
        out_ref[k * 128 : (k + 1) * 128, :] = lax.dot_general(
            cells, matrix, (((0,), (0,)), ((), ())), precision=lax.Precision.HIGHEST, preferred_element_type=f32
        )


VMEM = pl.BlockSpec(memory_space=pltpu.VMEM)
SMEM = pl.BlockSpec(memory_space=pltpu.SMEM)


def on_device(tangents, checkpoints, owner_order, land_mask, coefficients):
    block = lax.axis_index("y") * 2 + lax.axis_index("zh")
    core = lax.axis_index("c")
    raw, mask = pl.pallas_call(
        flow_kernel,
        out_shape=(jax.ShapeDtypeStruct((64, LANES), f32), jax.ShapeDtypeStruct(land_mask.shape, f32)),
        in_specs=[SMEM, VMEM, VMEM],
        out_specs=(VMEM, VMEM),
        compiler_params=pltpu.CompilerParams(vmem_limit_bytes=16 * 2**20),
    )(block.reshape(1).astype(jnp.int32), checkpoints, land_mask)
    up = [(i, i + 1) for i in range(7)]
    down = [(i + 1, i) for i in range(7)]
    ring = [(s * 4 + x, (s + step) % 8 * 4 + x) for s in range(8) for x, step in ((3, 1), (0, -1))]
    halo = lax.ppermute(raw[:48], ("y", "zh", "x"), ring)
    wide = jnp.concatenate([raw, halo], axis=0)
    above, below = lax.ppermute(wide, "zl", up), lax.ppermute(wide, "zl", down)
    send = pl.pallas_call(
        pack_kernel,
        out_shape=jax.ShapeDtypeStruct((PEERS, 64, LANES), f32),
        in_specs=[VMEM, VMEM],
        out_specs=VMEM,
        compiler_params=pltpu.CompilerParams(vmem_limit_bytes=16 * 2**20),
    )(tangents, mask)
    send, above, below = lax.optimization_barrier((send, above, below))
    own = lax.all_to_all(send, ("zh", "y", "c"), 0, 0, tiled=True)
    chips = jnp.concatenate([above, wide, below], axis=0)
    strip = jnp.concatenate(
        [chips] + [lax.ppermute(chips, "x", [(i, (i + k) % 4) for i in range(4)]) for k in (1, 2, 3)], axis=0
    )
    other = lax.ppermute(strip, "c", [(0, 1), (1, 0)])
    own, strip, other = lax.optimization_barrier((own, strip, other))
    coef = pl.pallas_call(
        coef_kernel,
        out_shape=jax.ShapeDtypeStruct((STEPS, COEFS, PARTS, TALL + 8, LANES), f32),
        in_specs=[SMEM, SMEM, VMEM, VMEM],
        out_specs=VMEM,
        scratch_shapes=[
            pltpu.VMEM((STEPS + 1, 3, PARTS, TALL + 16, LANES), f32),
            pltpu.VMEM((STEPS + 1, 3 * TALL, 2 * LANES), f32),
            pltpu.VMEM((2 * LANES, PARTS * LANES), jnp.bfloat16),
        ],
        compiler_params=pltpu.CompilerParams(vmem_limit_bytes=32 * 2**20),
        cost_estimate=pl.CostEstimate(flops=2 * 10**9, bytes_accessed=50 * 10**6, transcendentals=0),
    )(jnp.stack([core, lax.axis_index("x")]).astype(jnp.int32), owner_order, strip, other)
    parts = [lax.ppermute(own, "zl", up), own, lax.ppermute(own, "zl", down)]
    parts = [x.reshape(PEERS * 64, LANES) for x in parts]
    out = pl.pallas_call(
        march_kernel,
        out_shape=jax.ShapeDtypeStruct((8, 96, LANES), f32),
        in_specs=[VMEM] * 4,
        out_specs=VMEM,
        scratch_shapes=[
            pltpu.VMEM((3, QUADS, PARTS, TALL + 8, LANES), f32),
            pltpu.VMEM((3, QUADS, PARTS, TALL + 8, LANES), f32),
            pltpu.VMEM((2, 2, 64, LANES), f32),
        ],
        compiler_params=pltpu.CompilerParams(vmem_limit_bytes=26 * 2**20),
    )(*parts, coef)
    cells = lax.all_to_all(out, ("x", "c"), 0, 0, tiled=True)
    mixed = pl.pallas_call(
        mix_kernel,
        out_shape=jax.ShapeDtypeStruct((768, 128), f32),
        in_specs=[VMEM, VMEM],
        out_specs=VMEM,
        scratch_shapes=[pltpu.VMEM((128, 128), f32)],
        compiler_params=pltpu.CompilerParams(vmem_limit_bytes=16 * 2**20),
    )(coefficients, cells.reshape(768, LANES))
    return mixed.reshape(3, 8, 32, 128).transpose(3, 0, 1, 2)


def solution(mesh):
    fine = jax.sharding.Mesh(mesh.devices.reshape(SIZES), AXES)
    mode, rows = ("y", "zh", "x"), ("zl", "c")
    placed = (
        P(mode, None, rows, None),
        P(None, None, rows, mode),
        P(),
        P(rows, None),
        P(),
    )
    return jax.shard_map(
        on_device, mesh=fine, in_specs=placed, out_specs=P(None, None, rows, mode), check_vma=False
    )
```
